32 devices in a mesh: groups: 2 (over y), replica: 16 (over z, x, core).
Axes of the slice: x: 2, y: 2, z: 4, core: 2. Of those that a mesh axis runs over, the one named last changes fastest.
Arguments:
- hidden_state_input: bfloat16 [32, 8192], P(('groups', 'replica')), parts along dimension 0, may hold values from -6 to 6
- attention_norm_scale: bfloat16 [8192], replicated, may hold values from 0.099609375 to 1.8984375
- query_weight: bfloat16 [8192, 8192], P(None, 'replica'), may hold values from -0.0625 to 0.0625
- key_value_weight: bfloat16 [8192, 2048], P(None, 'replica'), may hold values from -0.0625 to 0.0625
- output_weight: bfloat16 [8192, 8192], P('replica'), may hold values from -0.0625 to 0.0625
- adapter_down_weight: bfloat16 [32, 8192, 64], P('replica'), may hold values from -0.0625 to 0.0625
- adapter_up_weight: bfloat16 [32, 64, 8192], P(None, None, 'replica'), may hold values from -0.75 to 0.75
- row_adapter_index: int32 [32], P(('groups', 'replica')), parts along dimension 0, may hold values from 0 to 31
- adapter_storage_index: int32 [32], replicated, may hold values from 0 to 31, each once
- cache_length_per_row: int32 [32], P(('groups', 'replica')), parts along dimension 0, may hold values from 32 to 512, as said below
- key_value_cache: bfloat16 [32, 2, 512, 1024], P(('groups', 'replica')), parts along dimension 0
Outputs:
- layer_out: bfloat16 [2, 32, 8192], P(None, ('groups', 'replica')), parts along dimension 1
The draws below stay inside these ranges and needn't reach their ends.
There are 2 independent parts, one for each index of `groups`. The reference program is written for one: setup_inputs(seed, part) draws one part's arguments, and reference() takes and returns one part's arrays. A program takes and returns all parts, laid end to end along the dimension named above; an argument that names none is the same for every part. Nothing has to cross between parts.
Inputs may be any that keep to these rules, and one draw needn't show every extreme that they name: `cache_length_per_row`: some row uses exactly 512 positions. `adapter_storage_index`: each storage index appears once.
All inputs are finite; a program needn't handle non-finite values.
Results may differ from the reference program's by a relative error of at most 0.033.
Values may be sent and summed in bfloat16 or wider, within the bound.
No kernel may reach another device: no remote copies, remote signals or barrier semaphores. Data moves between devices by JAX's collectives and lax.ppermute only.
A program may use at most 128 MiB of HBM per device.

```python
import math
import jax
import jax.numpy as jnp
import numpy as np
from jax import lax

MODEL_WIDTH = 8192
H = 64
KVH = 8
HD = 128
ADAPTER_RANK = 64
CACHE = 512
STEPS = 2
ROWS = 16
ADAPTER_COUNT = 32
QUERY_FEATURES = 8192
KV = 1024


def draw_cache_length_per_row(key, part):
    key = jax.random.fold_in(key, 11)
    first_key, second_key = jax.random.split(key)
    drawn = jax.random.randint(first_key, (ROWS,), CACHE // 16, CACHE + 1)
    chosen = jax.random.permutation(second_key, ROWS)
    drawn = drawn.at[chosen[0]].set(CACHE).at[chosen[1]].set(CACHE // 16)
    return drawn.astype(jnp.int32)


def draw_key_value_cache(key, part):
    key = jax.random.fold_in(key, 23)
    keys_list = jax.random.split(key, 1)
    whole = jax.random.normal(keys_list[0], (ROWS, 2, CACHE, KV), jnp.float32)
    return whole.astype(jnp.bfloat16)


def touch_ends(values, own_key, least, top_value):
    place = [jax.random.randint(jax.random.fold_in(own_key, axis), (), 0, length) for axis, length in enumerate(values.shape)]
    main_axis = values.shape.index(max(values.shape))
    beside = place[:main_axis] + [(place[main_axis] + 1) % values.shape[main_axis]] + place[main_axis + 1:]
    return values.at[tuple(place)].set(least).at[tuple(beside)].set(top_value)


def shard_levels(own_key, dims, pieces, low, top_value):
    factor_of = 1.0
    for dim, shards_of in pieces:
        heights = jax.random.uniform(jax.random.fold_in(jax.random.fold_in(own_key, 6), dim), (shards_of,), jnp.float32, low / len(pieces), top_value / len(pieces))
        factor_of = factor_of * jnp.repeat(jnp.exp(heights), dims[dim] // shards_of).reshape((-1,) + (1,) * (len(dims) - 1 - dim))
    return factor_of


def rank_table(amount, lean):
    loads = [(1 << 20) // math.isqrt(grade ** lean) + 1 for grade in range(1, amount + 1)]
    width = 1 + sum(loads) // (1 << 30)
    return np.cumsum(np.array([max(1, weight // width) for weight in loads]))


def ranked(key, dims, count, skew):
    listing = rank_table(count, skew)
    lot = jax.random.randint(jax.random.fold_in(key, 1), dims, 0, int(listing[count - 1]))
    grade = jnp.searchsorted(jnp.asarray(listing, jnp.int32), lot, side="right")
    return jax.random.permutation(jax.random.fold_in(key, 2), count)[grade].astype(jnp.int32)


def noise(key, dims, scale, reach, cuts=(), kind=jnp.bfloat16):
    values = scale * jax.random.normal(key, dims, jnp.float32)
    if cuts:
        values = values * shard_levels(key, dims, cuts, -0.22, 0.18)
    return jnp.clip(values, -reach, reach).astype(kind)


def setup_inputs(seed: int = 0, part: int = 0) -> dict:
    key_of = jax.random.split(jax.random.key(seed), 12)
    part_splits = jax.random.split(jax.random.fold_in(key_of[11], part), 12)
    hidden_state_input = noise(part_splits[0], (ROWS, MODEL_WIDTH), 1.0, 6.0, ((0, 16),))
    attention_norm_scale = jnp.clip(1.0 + 0.18 * jax.random.normal(key_of[1], (MODEL_WIDTH,), jnp.float32), 0.099609375, 1.8984375).astype(jnp.bfloat16)
    query_weight = noise(key_of[2], (MODEL_WIDTH, QUERY_FEATURES), MODEL_WIDTH ** -0.5, 0.0625, ((1, 16),))
    key_value_weight = noise(key_of[3], (MODEL_WIDTH, 2 * KV), MODEL_WIDTH ** -0.5, 0.0625, ((1, 16),))
    output_weight = noise(key_of[4], (QUERY_FEATURES, MODEL_WIDTH), QUERY_FEATURES ** -0.5, 0.0625, ((0, 16),))
    adapter_down_weight = noise(key_of[5], (ADAPTER_COUNT, MODEL_WIDTH, ADAPTER_RANK), MODEL_WIDTH ** -0.5, 0.0625, ((0, 16),))
    adapter_up_weight = noise(key_of[6], (ADAPTER_COUNT, ADAPTER_RANK, QUERY_FEATURES), ADAPTER_RANK ** -0.5, 0.75, ((2, 16),))
    row_adapter_index = touch_ends(ranked(part_splits[7], (ROWS,), ADAPTER_COUNT, 2), jax.random.fold_in(part_splits[7], 3), 0, ADAPTER_COUNT - 1).astype(jnp.int32)
    adapter_storage_index = jax.random.permutation(key_of[8], ADAPTER_COUNT).astype(jnp.int32)
    cache_length_per_row = draw_cache_length_per_row(jax.random.fold_in(jax.random.fold_in(key_of[11], part), 71), part)
    key_value_cache = draw_key_value_cache(jax.random.fold_in(jax.random.fold_in(key_of[11], part), 71), part)
    return {"hidden_state_input": hidden_state_input, "attention_norm_scale": attention_norm_scale, "query_weight": query_weight, "key_value_weight": key_value_weight, "output_weight": output_weight, "adapter_down_weight": adapter_down_weight, "adapter_up_weight": adapter_up_weight, "row_adapter_index": row_adapter_index, "adapter_storage_index": adapter_storage_index, "cache_length_per_row": cache_length_per_row, "key_value_cache": key_value_cache}


def rms_normed(hidden, attention_norm_scale):
    widened = hidden.astype(jnp.float32)
    factor = lax.rsqrt(lax.optimization_barrier(jnp.mean(widened * widened, axis=-1, keepdims=True)) + 1e-05)
    return (widened * factor * attention_norm_scale.astype(jnp.float32)).astype(jnp.bfloat16)

def attend_row(paired_terms):
    queries, cache_row, length, recent_keys, recent_values = paired_terms
    score_scale = 1.0 / math.sqrt(HD)
    grouped_q = queries.astype(jnp.float32).reshape(KVH, H // KVH, HD)
    cache_keys = cache_row[0].astype(jnp.float32).reshape(CACHE, KVH, HD)
    cache_values = cache_row[1].astype(jnp.float32).reshape(CACHE, KVH, HD)
    new_keys = recent_keys.astype(jnp.float32).reshape(-1, KVH, HD)
    new_values = recent_values.astype(jnp.float32).reshape(-1, KVH, HD)
    cached_scores = jnp.einsum('hgd,chd->hgc', grouped_q, cache_keys) * score_scale
    in_cache = jnp.arange(CACHE, dtype=jnp.int32) < length
    cached_scores = jnp.where(in_cache[None, None, :], cached_scores, -jnp.inf)
    new_scores = jnp.einsum('hgd,nhd->hgn', grouped_q, new_keys) * score_scale
    scores = jnp.concatenate([cached_scores, new_scores], axis=-1)
    peak = lax.optimization_barrier(jnp.max(scores, axis=-1, keepdims=True))
    exp_scores = jnp.exp(scores - peak)
    weights = (exp_scores / lax.optimization_barrier(jnp.sum(exp_scores, axis=-1, keepdims=True))).astype(jnp.bfloat16).astype(jnp.float32)
    mixed = jnp.einsum('hgc,chd->hgd', weights[..., :CACHE], cache_values)
    mixed = mixed + jnp.einsum('hgn,nhd->hgd', weights[..., CACHE:], new_values)
    return mixed.reshape(QUERY_FEATURES).astype(jnp.bfloat16)

def reference(hidden_state_input, attention_norm_scale, query_weight, key_value_weight, output_weight, adapter_down_weight, adapter_up_weight, row_adapter_index, adapter_storage_index, cache_length_per_row, key_value_cache):
    storage_positions = adapter_storage_index[row_adapter_index]
    hidden = hidden_state_input
    keys_new = []
    values_new = []
    results = []
    for decode_step in range(STEPS):
        normalized_hidden = rms_normed(hidden, attention_norm_scale)
        base_q = jnp.dot(normalized_hidden, query_weight, preferred_element_type=jnp.float32)
        fresh_kv = jnp.dot(normalized_hidden, key_value_weight, preferred_element_type=jnp.float32).astype(jnp.bfloat16)
        rank_projected = lax.map(lambda paired_terms: jnp.dot(paired_terms[0], adapter_down_weight[paired_terms[1]], preferred_element_type=jnp.float32), (normalized_hidden, storage_positions)).astype(jnp.bfloat16)
        up_projected = lax.map(lambda paired_terms: jnp.dot(paired_terms[0], adapter_up_weight[paired_terms[1]], preferred_element_type=jnp.float32), (rank_projected, row_adapter_index))
        queries = (base_q + up_projected).astype(jnp.bfloat16)
        keys_new.append(fresh_kv[:, :KV])
        values_new.append(fresh_kv[:, KV:])
        attended = lax.map(attend_row, (queries, key_value_cache, cache_length_per_row, jnp.stack(keys_new, axis=1), jnp.stack(values_new, axis=1)))
        output = jnp.dot(attended, output_weight, preferred_element_type=jnp.float32).astype(jnp.bfloat16)
        hidden = (hidden.astype(jnp.float32) + output.astype(jnp.float32)).astype(jnp.bfloat16)
        results.append(hidden)
    return jnp.stack(results)
```

```python
import functools
import math

import jax
import jax.numpy as jnp
from jax import lax
from jax.experimental import pallas as pl
from jax.experimental.pallas import tpu as pltpu
from jax.sharding import PartitionSpec as P

H = 64
KVH = 8
HD = 128
CACHE = 512
STEPS = 2
GROUP = H // KVH
NEW = 8
AXIS = "replica"


def rms_normed(hidden, attention_norm_scale):
    widened = hidden.astype(jnp.float32)
    factor = lax.rsqrt(jnp.mean(widened * widened, axis=-1, keepdims=True) + 1e-05)
    return (widened * factor * attention_norm_scale.astype(jnp.float32)).astype(jnp.bfloat16)


def everyone(block, count):
    spread = jnp.broadcast_to(block, (count,) + block.shape[1:])
    return lax.all_to_all(spread, AXIS, split_axis=0, concat_axis=0, tiled=True)


def swap(blocks):
    return lax.all_to_all(blocks, AXIS, split_axis=0, concat_axis=0, tiled=True)


def attend_kernel(fresh, length_ref, query_ref, cache_ref, new_keys_ref, new_values_ref, out_ref):
    length = length_ref[0]
    in_cache = lax.broadcasted_iota(jnp.int32, (GROUP, CACHE), 1) < length
    is_new = lax.broadcasted_iota(jnp.int32, (GROUP, NEW), 1) < fresh
    contract_last = (((1,), (1,)), ((), ()))
    for head in range(KVH):
        lanes = slice(head * HD, (head + 1) * HD)
        rows = slice(head * GROUP, (head + 1) * GROUP)
        query = query_ref[rows, :].astype(jnp.bfloat16)
        old = lax.dot_general(
            query, cache_ref[0, 0, :, lanes], contract_last, preferred_element_type=jnp.float32
        ) * (1.0 / math.sqrt(HD))
        new = lax.dot_general(
            query,
            new_keys_ref[:, lanes].astype(jnp.bfloat16),
            contract_last,
            preferred_element_type=jnp.float32,
        ) * (1.0 / math.sqrt(HD))
        old = jnp.where(in_cache, old, -jnp.inf)
        new = jnp.where(is_new, new, -jnp.inf)
        peak = jnp.maximum(
            jnp.max(old, axis=-1, keepdims=True), jnp.max(new, axis=-1, keepdims=True)
        )
        old = jnp.exp(old - peak)
        new = jnp.exp(new - peak)
        total = jnp.sum(old, axis=-1, keepdims=True) + jnp.sum(new, axis=-1, keepdims=True)
        old = (old / total).astype(jnp.bfloat16)
        new = (new / total).astype(jnp.bfloat16)
        out_ref[rows, :] = jnp.dot(
            old, cache_ref[0, 1, :, lanes], preferred_element_type=jnp.float32
        ) + jnp.dot(
            new, new_values_ref[:, lanes].astype(jnp.bfloat16), preferred_element_type=jnp.float32
        )


def attend(queries, key_value_cache, cache_length, new_keys, new_values, fresh):
    return pl.pallas_call(
        functools.partial(attend_kernel, fresh),
        out_shape=jax.ShapeDtypeStruct((H, HD), jnp.float32),
        in_specs=[pl.BlockSpec(memory_space=pltpu.SMEM)]
        + [pl.BlockSpec(memory_space=pltpu.VMEM)] * 4,
        out_specs=pl.BlockSpec(memory_space=pltpu.VMEM),
        compiler_params=pltpu.CompilerParams(vmem_limit_bytes=16 << 20),
        cost_estimate=pl.CostEstimate(flops=4 * H * CACHE * HD, bytes_accessed=2 << 20, transcendentals=0),
        name="attend",
    )(cache_length, queries, key_value_cache, new_keys, new_values)


def shards(
    hidden_state_input,
    attention_norm_scale,
    query_weight,
    key_value_weight,
    output_weight,
    adapter_down_weight,
    adapter_up_weight,
    row_adapter_index,
    adapter_storage_index,
    cache_length_per_row,
    key_value_cache,
):
    count = lax.axis_size(AXIS)
    kept, width, rank = adapter_down_weight.shape
    columns = query_weight.shape[1]
    owner_offset = lax.axis_index(AXIS) * kept

    adapter_of = everyone(jnp.broadcast_to(row_adapter_index[:, None], (1, 128)), count)[:, 0]
    storage_of = adapter_storage_index[adapter_of]
    up_of = adapter_up_weight[adapter_of].reshape(count * rank, columns)
    own_row = jnp.arange(count, dtype=jnp.int32)

    hidden = hidden_state_input
    new_keys = jnp.zeros((NEW, key_value_cache.shape[3]), jnp.float32)
    new_values = new_keys
    results = []
    for step in range(STEPS):
        normed = rms_normed(hidden, attention_norm_scale)
        rows = everyone(normed, count)

        low = jnp.zeros((count, rank), jnp.float32)
        for index in range(kept):
            part = jnp.dot(rows, adapter_down_weight[index], preferred_element_type=jnp.float32)
            low = jnp.where((storage_of == owner_offset + index)[:, None], part, low)
        low = jnp.broadcast_to(low.astype(jnp.bfloat16)[None], (count, count, rank))
        low = jnp.sum(swap(low).astype(jnp.float32), axis=0).astype(jnp.bfloat16)

        query = jnp.dot(rows, query_weight, preferred_element_type=jnp.float32)
        fresh = jnp.dot(rows, key_value_weight, preferred_element_type=jnp.float32)
        spread = jnp.where(
            own_row[:, None, None] == own_row[None, :, None], low[:, None, :], 0
        ).reshape(count, count * rank)
        query = query + jnp.dot(spread, up_of, preferred_element_type=jnp.float32)

        mine = swap(jnp.concatenate([query, fresh], axis=1).astype(jnp.bfloat16))
        query = mine[:, :columns].reshape(H, HD).astype(jnp.float32)
        fresh = mine[:, columns:].reshape(2, -1).astype(jnp.float32)
        new_keys = new_keys.at[step].set(fresh[0])
        new_values = new_values.at[step].set(fresh[1])

        attended = attend(
            query, key_value_cache, cache_length_per_row, new_keys, new_values, step + 1
        )
        features = swap(attended.astype(jnp.bfloat16).reshape(count, columns))
        partial = jnp.dot(features, output_weight, preferred_element_type=jnp.float32)
        parts = swap(partial.astype(jnp.bfloat16))
        out = jnp.sum(parts.astype(jnp.float32), axis=0, keepdims=True).astype(jnp.bfloat16)
        hidden = (hidden.astype(jnp.float32) + out.astype(jnp.float32)).astype(jnp.bfloat16)
        results.append(hidden)
    return jnp.stack(results)


def solution(mesh):
    in_specs = (
        P(("groups", "replica"), None),
        P(),
        P(None, "replica"),
        P(None, "replica"),
        P("replica", None),
        P("replica", None, None),
        P(None, None, "replica"),
        P(("groups", "replica")),
        P(),
        P(("groups", "replica")),
        P(("groups", "replica"), None, None, None),
    )
    out_specs = P(None, ("groups", "replica"), None)
    return jax.shard_map(shards, mesh=mesh, in_specs=in_specs, out_specs=out_specs, check_vma=False)
```

```python
import functools
import math

import jax
import jax.numpy as jnp
from jax import lax
from jax.experimental import pallas as pl
from jax.experimental.pallas import tpu as pltpu
from jax.sharding import PartitionSpec as P

H = 64
KVH = 8
HD = 128
STEPS = 2
GROUP = H // KVH
EPS = 1e-05
AXIS = "replica"
LANES = 128
LAST = (((1,), (1,)), ((), ()))
FIRST = (((0,), (0,)), ((), ()))


def split_of(count):
    far = 1 << (count.bit_length() // 2)
    return far, count // far


def shift(block, distance, count):
    return lax.ppermute(block, AXIS, [(i, i ^ distance) for i in range(count)])


def across_far(blocks, near, count):
    return [blocks[0]] + [shift(b, k * near, count) for k, b in enumerate(blocks) if k]


def across_near(blocks, count):
    return [blocks[0]] + [shift(b, k, count) for k, b in enumerate(blocks) if k]


def call(body, outs, name, scratch=(), vmem=24 << 20, flops=1 << 20, moved=1 << 18):
    def run(*operands, specs=None):
        specs = specs or [pltpu.VMEM] * len(operands)
        return pl.pallas_call(
            body,
            out_shape=outs,
            in_specs=[pl.BlockSpec(memory_space=s) for s in specs],
            out_specs=jax.tree.map(lambda _: pl.BlockSpec(memory_space=pltpu.VMEM), outs),
            scratch_shapes=list(scratch),
            compiler_params=pltpu.CompilerParams(vmem_limit_bytes=vmem),
            cost_estimate=pl.CostEstimate(flops=flops, bytes_accessed=moved, transcendentals=0),
            name=name,
        )(*operands)

    return run


def shape(dims, dtype=jnp.bfloat16):
    return jax.ShapeDtypeStruct(dims, dtype)


def iota(dims, axis):
    return lax.broadcasted_iota(jnp.int32, dims, axis)


def dot(a, b, contract=(((1,), (0,)), ((), ()))):
    return lax.dot_general(a, b, contract, preferred_element_type=jnp.float32)


def normalized(hidden, scale):
    factor = lax.rsqrt(jnp.mean(hidden * hidden, axis=-1, keepdims=True) + EPS)
    return (hidden * factor * scale).astype(jnp.bfloat16)


def first_kernel(hidden_ref, scale_ref, adapter_ref, out_ref):
    width = hidden_ref.shape[1]
    hidden = hidden_ref[...].astype(jnp.float32)
    out_ref[:, :width] = normalized(hidden, scale_ref[...].astype(jnp.float32))
    digit = iota((1, LANES), 1)
    adapter = adapter_ref[0]
    high, low = adapter // 256, adapter % 256
    out_ref[:, width:] = jnp.where(digit == 0, low, jnp.where(digit == 1, high, 0)).astype(
        jnp.float32
    ).astype(jnp.bfloat16)


def stacked_kernel(count_in, *refs):
    for k, ref in enumerate(refs[:count_in]):
        refs[count_in][k : k + 1, :] = ref[...]


def low_kernel(near, far, width, *refs):
    pieces, refs = refs[:near], refs[near:]
    me_ref, member_ref, down_ref, rows_ref, low_ref, held = refs
    count = near * far
    for l in range(near):
        held[l * far : (l + 1) * far, :] = pieces[l][:, :width].astype(jnp.float32)
    rows = held[...].astype(jnp.bfloat16)
    rows_ref[...] = rows
    kept = down_ref.shape[0]
    low = jnp.zeros((count, down_ref.shape[1]), jnp.float32)
    for index in range(kept):
        part = dot(rows, down_ref[index], LAST)
        low = jnp.where(member_ref[:, index : index + 1] > 0, part, low)
    slot = iota((count, count), 1)
    origin = me_ref[0] ^ ((slot % far) * near + slot // far)
    order = (iota((count, count), 0) == origin).astype(jnp.bfloat16)
    low_ref[...] = dot(order, low.astype(jnp.bfloat16)).astype(jnp.bfloat16)


def member_kernel(near, far, width, *refs):
    pieces, (me_ref, storage_ref, member_ref, adapter_ref, held) = refs[:near], refs[near:]
    kept = member_ref.shape[1]
    count = near * far
    for l in range(near):
        held[l * far : (l + 1) * far, :] = pieces[l][:, width:].astype(jnp.float32)
    adapter = (held[:, 0:1] + 256.0 * held[:, 1:2]).astype(jnp.int32)
    adapter_ref[...] = adapter
    table = storage_ref.shape[1]
    chosen = jnp.where(iota((count, table), 1) == adapter, storage_ref[...], 0)
    storage = jnp.sum(chosen.astype(jnp.float32), axis=1, keepdims=True).astype(jnp.int32)
    member_ref[...] = (storage - me_ref[0] * kept == iota((count, kept), 1)).astype(jnp.int32)


def project_kernel(rows_ref, query_hbm, fresh_hbm, query_ref, fresh_ref, query_w, fresh_w, sems):
    chunks = sems.shape[1]
    deep = query_w.shape[0] // chunks
    copies = []
    for c in range(chunks):
        part = pl.ds(c * deep, deep)
        copies.append(
            (
                pltpu.make_async_copy(query_hbm.at[part], query_w.at[part], sems.at[0, c]),
                pltpu.make_async_copy(fresh_hbm.at[part], fresh_w.at[part], sems.at[1, c]),
            )
        )
    for pair in copies:
        for copy in pair:
            copy.start()
    query = jnp.zeros(query_ref.shape, jnp.float32)
    fresh = jnp.zeros(fresh_ref.shape, jnp.float32)
    for c, pair in enumerate(copies):
        for copy in pair:
            copy.wait()
        part = slice(c * deep, (c + 1) * deep)
        rows = rows_ref[:, part]
        query = query + dot(rows, query_w[part, :])
        fresh = fresh + dot(rows, fresh_w[part, :])
    query_ref[...] = query
    fresh_ref[...] = fresh


def up_kernel(near, far, *refs):
    lows, refs = refs[:near], refs[near:]
    me_ref, query_ref, fresh_ref, up_ref = refs[:4]
    outs = refs[4:]
    count = near * far
    rank = lows[0].shape[1]
    columns = query_ref.shape[1]
    low = lows[0][...].astype(jnp.float32)
    for ref in lows[1:]:
        low = low + ref[...].astype(jnp.float32)
    slot = iota((count, count), 0)
    origin = me_ref[0] ^ ((slot % far) * near + slot // far)
    order = (iota((count, count), 1) == origin).astype(jnp.bfloat16)
    low = dot(order, low.astype(jnp.bfloat16)).astype(jnp.bfloat16)
    wide = count * rank
    repeat = (iota((rank, wide), 1) % rank == iota((rank, wide), 0)).astype(jnp.bfloat16)
    spread = jnp.where(
        iota((count, wide), 1) // rank == iota((count, wide), 0), dot(low, repeat), 0.0
    ).astype(jnp.bfloat16)
    query = query_ref[...] + dot(spread, up_ref[...])
    fresh = fresh_ref[...]
    for l in range(near):
        part = slice(l * far, (l + 1) * far)
        outs[l][:, :columns] = query[part].astype(jnp.bfloat16)
        outs[l][:, columns:] = fresh[part].astype(jnp.bfloat16)


def turn_kernel(near, far, *refs):
    pieces, outs, held = refs[:near], refs[near : near + far], refs[-1]
    for l in range(near):
        held[l * far : (l + 1) * far, :] = pieces[l][...].astype(jnp.float32)
    rows = held[...]
    for k in range(far):
        outs[k][...] = jnp.concatenate(
            [rows[l * far + k : l * far + k + 1] for l in range(near)], axis=0
        ).astype(jnp.bfloat16)


def pieces_of(slots, select, whole, size):
    if size >= whole:
        each = size // whole
        total = None
        for c in range(each):
            part = dot(select(each, c), slots[:, c * whole : (c + 1) * whole])
            total = part if total is None else total + part
        return total
    return jnp.concatenate([dot(select(0, p), slots) for p in range(whole // size)], axis=1)


def attend_kernel(near, far, columns, fresh_columns, first, *refs):
    pieces, refs = refs[:far], refs[far:]
    length_ref, me_ref, cache_ref = refs[:3]
    refs = refs[3:]
    if not first:
        past, refs = refs[:2], refs[2:]
    outs, refs = refs[:near], refs[near:]
    if first:
        keep, refs = refs[:2], refs[2:]
    held, scores = refs
    count = near * far
    cache = cache_ref.shape[2]
    me = me_ref[0]
    for k in range(far):
        held[k * near : (k + 1) * near, :] = pieces[k][...].astype(jnp.float32)
    slots = held[...].astype(jnp.bfloat16)
    origin = me ^ iota((H, count), 1)
    head = iota((H, count), 0)

    def query_pick(each, c):
        if each:
            return (head == origin * each + c).astype(jnp.bfloat16)
        return (head * (HD // columns) + c == origin).astype(jnp.bfloat16)

    def fresh_pick(offset):
        def pick(each, c):
            want = head // GROUP + offset
            if each:
                return (want == origin * each + c).astype(jnp.bfloat16)
            return (want * (HD // fresh_columns) + c == origin).astype(jnp.bfloat16)

        return pick

    query = pieces_of(slots[:, :columns], query_pick, HD, columns)
    fresh = slots[:, columns:]
    new = [
        (
            pieces_of(fresh, fresh_pick(0), HD, fresh_columns),
            pieces_of(fresh, fresh_pick(KVH), HD, fresh_columns),
        )
    ]
    if first:
        keep[0][...], keep[1][...] = new[0]
    else:
        new.insert(0, (past[0][...], past[1][...]))
    scale = 1.0 / math.sqrt(HD)
    for j in range(KVH):
        rows = slice(j * GROUP, (j + 1) * GROUP)
        scores[rows, :] = dot(
            query[rows].astype(jnp.bfloat16), cache_ref[0, 0, :, j * HD : (j + 1) * HD], LAST
        )
    in_cache = iota((H, cache), 1) < length_ref[0]
    old = jnp.where(in_cache, scores[...] * scale, -jnp.inf)
    news = [jnp.sum(query * keys, axis=1, keepdims=True) * scale for keys, _ in new]
    peak = jnp.max(old, axis=1, keepdims=True)
    for score in news:
        peak = jnp.maximum(peak, score)
    old = jnp.exp(old - peak)
    news = [jnp.exp(score - peak) for score in news]
    total = jnp.sum(old, axis=1, keepdims=True)
    for score in news:
        total = total + score
    old = old / total
    extra = jnp.zeros((H, HD), jnp.float32)
    for score, (_, values) in zip(news, new):
        extra = extra + (score / total).astype(jnp.bfloat16).astype(jnp.float32) * values
    mixed = jnp.concatenate(
        [
            dot(
                old[j * GROUP : (j + 1) * GROUP].astype(jnp.bfloat16),
                cache_ref[0, 1, :, j * HD : (j + 1) * HD],
            )
            for j in range(KVH)
        ],
        axis=0,
    )
    mixed = (mixed + extra).astype(jnp.bfloat16)
    slot = iota((count, H), 0)
    target = me ^ ((slot % far) * near + slot // far)
    head = iota((count, H), 1)
    if columns >= HD:
        each = columns // HD
        out = [dot((head == target * each + c).astype(jnp.bfloat16), mixed) for c in range(each)]
        out = out[0] if each == 1 else jnp.concatenate(out, axis=1)
    else:
        parts = HD // columns
        out = jnp.zeros((count, columns), jnp.float32)
        for p in range(parts):
            pick = (head * parts + p == target).astype(jnp.bfloat16)
            out = out + dot(pick, mixed[:, p * columns : (p + 1) * columns])
    for l in range(near):
        outs[l][...] = out[l * far : (l + 1) * far].astype(jnp.bfloat16)


def output_kernel(near, far, *refs):
    pieces, refs = refs[:far], refs[far:]
    weight_hbm, refs = refs[0], refs[1:]
    outs, (held, weight, sems) = refs[:near], refs[near:]
    chunks = sems.shape[0]
    wide = weight.shape[1] // chunks
    copies = [
        pltpu.make_async_copy(
            weight_hbm.at[:, pl.ds(c * wide, wide)], weight.at[:, pl.ds(c * wide, wide)], sems.at[c]
        )
        for c in range(chunks)
    ]
    for copy in copies:
        copy.start()
    for k in range(far):
        piece = pieces[k][...].astype(jnp.float32)
        for l in range(near):
            held[l * far + k : l * far + k + 1, :] = piece[l : l + 1]
    rows = held[...].astype(jnp.bfloat16)
    for c, copy in enumerate(copies):
        copy.wait()
        part = slice(c * wide, (c + 1) * wide)
        out = dot(rows, weight[:, part])
        for l in range(near):
            outs[l][:, part] = out[l * far : (l + 1) * far].astype(jnp.bfloat16)


def partial_kernel(near, far, *refs):
    pieces, outs = refs[:near], refs[near:]
    total = pieces[0][...].astype(jnp.float32)
    for ref in pieces[1:]:
        total = total + ref[...].astype(jnp.float32)
    for k in range(far):
        outs[k][...] = total[k : k + 1].astype(jnp.bfloat16)


def finish_kernel(far, last, *refs):
    pieces, refs = refs[:far], refs[far:]
    hidden_ref, scale_ref, out_ref = refs[:3]
    total = pieces[0][...].astype(jnp.float32)
    for ref in pieces[1:]:
        total = total + ref[...].astype(jnp.float32)
    total = total.astype(jnp.bfloat16).astype(jnp.float32)
    hidden = (hidden_ref[...].astype(jnp.float32) + total).astype(jnp.bfloat16)
    out_ref[...] = hidden
    if not last:
        refs[3][...] = normalized(hidden.astype(jnp.float32), scale_ref[...].astype(jnp.float32))


def shards(
    hidden_state_input,
    attention_norm_scale,
    query_weight,
    key_value_weight,
    output_weight,
    adapter_down_weight,
    adapter_up_weight,
    row_adapter_index,
    adapter_storage_index,
    cache_length_per_row,
    key_value_cache,
):
    count = lax.axis_size(AXIS)
    far, near = split_of(count)
    kept, width, rank = adapter_down_weight.shape
    columns = query_weight.shape[1]
    fresh_columns = key_value_weight.shape[1]
    message = columns + fresh_columns
    smem, vmem = pltpu.SMEM, pltpu.VMEM
    me = lax.axis_index(AXIS).astype(jnp.int32).reshape(1)
    down = adapter_down_weight.transpose(0, 2, 1)
    scale = attention_norm_scale[None]
    storage = adapter_storage_index[None]

    hidden = hidden_state_input
    carried = call(first_kernel, shape((1, width + LANES)), "first")(
        hidden, scale, row_adapter_index, specs=[vmem, vmem, smem]
    )
    results = []
    past = ()
    for step in range(STEPS):
        first, last = step == 0, step == STEPS - 1
        carried = across_far([carried] * far, near, count)
        carried = jnp.concatenate(carried, axis=0)
        pieces = across_near([carried] * near, count)
        if first:
            member, adapter = call(
                functools.partial(member_kernel, near, far, width),
                [shape((count, kept), jnp.int32), shape((count, 1), jnp.int32)],
                "member",
                [pltpu.VMEM((count, LANES), jnp.float32)],
            )(*pieces, me, storage, specs=[vmem] * near + [smem, vmem])
            up_of = adapter_up_weight[adapter[:, 0]].reshape(count * rank, columns)
        rows, low = call(
            functools.partial(low_kernel, near, far, width),
            [shape((count, width)), shape((count, rank))],
            "low",
            [pltpu.VMEM((count, width), jnp.float32)],
            moved=2 << 20,
        )(*pieces, me, member, down, specs=[vmem] * near + [smem, vmem, vmem])
        low = across_far([low] * far, near, count)
        low = functools.reduce(lambda a, b: a + b, [x.astype(jnp.float32) for x in low])
        low = low.astype(jnp.bfloat16)
        lows = across_near([low] * near, count)
        chunks = 8
        query, fresh = call(
            project_kernel,
            [shape((count, columns), jnp.float32), shape((count, fresh_columns), jnp.float32)],
            "project",
            [
                pltpu.VMEM((width, columns), jnp.bfloat16),
                pltpu.VMEM((width, fresh_columns), jnp.bfloat16),
                pltpu.SemaphoreType.DMA((2, chunks)),
            ],
            flops=2 * count * width * message,
            moved=2 * width * message,
        )(rows, query_weight, key_value_weight, specs=[vmem, pl.ANY, pl.ANY])
        blocks = call(
            functools.partial(up_kernel, near, far), [shape((far, message))] * near, "up"
        )(*lows, me, query, fresh, up_of, specs=[vmem] * near + [smem, vmem, vmem, vmem])

        turn = functools.partial(turn_kernel, near, far)
        blocks = across_near(blocks, count)
        blocks = call(
            turn, [shape((near, message))] * far, "turn", [pltpu.VMEM((count, message), jnp.float32)]
        )(*blocks)
        blocks = across_far(blocks, near, count)
        outs = [shape((far, columns))] * near
        if first:
            outs = outs + [shape((H, HD), jnp.float32)] * 2
        blocks = call(
            functools.partial(attend_kernel, near, far, columns, fresh_columns, first),
            outs,
            "attend",
            [
                pltpu.VMEM((count, message), jnp.float32),
                pltpu.VMEM((H, key_value_cache.shape[2]), jnp.float32),
            ],
            moved=2 << 20,
        )(
            *blocks,
            cache_length_per_row,
            me,
            key_value_cache,
            *past,
            specs=[vmem] * far + [smem, smem, vmem] + [vmem] * len(past),
        )
        if first:
            past = tuple(blocks[near:])
            blocks = blocks[:near]

        blocks = across_near(blocks, count)
        blocks = call(
            turn, [shape((near, columns))] * far, "turn", [pltpu.VMEM((count, columns), jnp.float32)]
        )(*blocks)
        blocks = across_far(blocks, near, count)
        chunks = 8
        blocks = call(
            functools.partial(output_kernel, near, far),
            [shape((far, width))] * near,
            "output",
            [
                pltpu.VMEM((count, columns), jnp.float32),
                pltpu.VMEM((columns, width), jnp.bfloat16),
                pltpu.SemaphoreType.DMA((chunks,)),
            ],
            flops=2 * count * width * columns,
            moved=2 * width * columns,
        )(*blocks, output_weight, specs=[vmem] * far + [pl.ANY])

        blocks = across_near(blocks, count)
        blocks = call(
            functools.partial(partial_kernel, near, far), [shape((1, width))] * far, "partial"
        )(*blocks)
        blocks = across_far(blocks, near, count)
        outs = [shape((1, width))] * (1 if last else 2)
        outs = call(functools.partial(finish_kernel, far, last), outs, "finish")(
            *blocks, hidden, scale
        )
        hidden = outs[0]
        results.append(hidden)
        if not last:
            carried = outs[1]
    return jnp.stack(results)


def solution(mesh):
    in_specs = (
        P(("groups", "replica"), None),
        P(),
        P(None, "replica"),
        P(None, "replica"),
        P("replica", None),
        P("replica", None, None),
        P(None, None, "replica"),
        P(("groups", "replica")),
        P(),
        P(("groups", "replica")),
        P(("groups", "replica"), None, None, None),
    )
    out_specs = P(None, ("groups", "replica"), None)
    return jax.shard_map(shards, mesh=mesh, in_specs=in_specs, out_specs=out_specs, check_vma=False)
```

```python
import functools
import math

import jax
import jax.numpy as jnp
from jax import lax
from jax.experimental import pallas as pl
from jax.experimental.pallas import tpu as pltpu
from jax.sharding import PartitionSpec as P

H = 64
KVH = 8
HD = 128
STEPS = 2
GROUP = H // KVH
EPS = 1e-05
AXIS = "replica"
LANES = 128
LAST = (((1,), (1,)), ((), ()))
FIRST = (((0,), (0,)), ((), ()))

CORES = 2


def sibling(block, count):
    return lax.ppermute(block, AXIS, [(i, i ^ 1) for i in range(count)])


def chips_swap(blocks, count):
    groups = [[i for i in range(count) if i % CORES == c] for c in range(CORES)]
    return lax.all_to_all(
        blocks, AXIS, split_axis=0, concat_axis=0, axis_index_groups=groups, tiled=True
    )


def call(body, outs, name, scratch=(), vmem=32 << 20, flops=1 << 20, moved=1 << 18):
    def run(*operands, specs=None):
        specs = specs or [pltpu.VMEM] * len(operands)
        return pl.pallas_call(
            body,
            out_shape=outs,
            in_specs=[pl.BlockSpec(memory_space=s) for s in specs],
            out_specs=jax.tree.map(lambda _: pl.BlockSpec(memory_space=pltpu.VMEM), outs),
            scratch_shapes=list(scratch),
            compiler_params=pltpu.CompilerParams(vmem_limit_bytes=vmem),
            cost_estimate=pl.CostEstimate(flops=flops, bytes_accessed=moved, transcendentals=0),
            name=name,
        )(*operands)

    return run


def shape(dims, dtype=jnp.bfloat16):
    return jax.ShapeDtypeStruct(dims, dtype)


def iota(dims, axis):
    return lax.broadcasted_iota(jnp.int32, dims, axis)


def dot(a, b, contract=(((1,), (0,)), ((), ()))):
    return lax.dot_general(a, b, contract, preferred_element_type=jnp.float32)


def normalized(hidden, scale):
    factor = lax.rsqrt(jnp.mean(hidden * hidden, axis=-1, keepdims=True) + EPS)
    return (hidden * factor * scale).astype(jnp.bfloat16)


FOLD = 8


def folded(out_ref, row):
    wide = row.shape[1] // FOLD
    for k in range(out_ref.shape[0]):
        for i in range(FOLD):
            out_ref[k, i : i + 1, :wide] = row[:, i * wide : (i + 1) * wide].astype(out_ref.dtype)


def unfolded(held, ref, start, chips, wide):
    for k in range(chips):
        block = ref[k, :, :wide].astype(jnp.float32)
        for i in range(FOLD):
            held[start + k : start + k + 1, i * wide : (i + 1) * wide] = block[i : i + 1]


def slot_origin(core, dims, axis):
    slot = iota(dims, axis)
    chips = dims[axis] // CORES
    return (slot % chips) * CORES + (core ^ (slot // chips))


def pair_origin(core, dims, axis):
    slot = iota(dims, axis)
    return slot ^ core


def first_kernel(hidden_ref, scale_ref, adapter_ref, out_ref):
    hidden = hidden_ref[...].astype(jnp.float32)
    folded(out_ref, normalized(hidden, scale_ref[...].astype(jnp.float32)).astype(jnp.float32))
    digit = iota((FOLD, LANES), 1)
    adapter = adapter_ref[0]
    high, low = adapter // 256, adapter % 256
    digits = jnp.where(digit == 0, low, jnp.where(digit == 1, high, 0)).astype(jnp.float32)
    wide = hidden_ref.shape[1] // FOLD
    for k in range(out_ref.shape[0]):
        out_ref[k, :, wide:] = digits.astype(jnp.bfloat16)


def low_kernel(chips, own_ref, other_ref, me_ref, member_ref, down_ref, rows_ref, low_ref, away_ref, held):
    count = chips * CORES
    wide = rows_ref.shape[1] // FOLD
    unfolded(held, own_ref, 0, chips, wide)
    unfolded(held, other_ref, chips, chips, wide)
    rows = held[...].astype(jnp.bfloat16)
    rows_ref[...] = rows
    kept = down_ref.shape[0]
    low = jnp.zeros((count, down_ref.shape[1]), jnp.float32)
    for index in range(kept):
        part = dot(rows, down_ref[index], LAST)
        low = jnp.where(member_ref[:, index : index + 1] > 0, part, low)
    low_ref[...] = low.astype(jnp.bfloat16)
    away_ref[...] = jnp.concatenate([low[chips:], low[:chips]], axis=0).astype(jnp.bfloat16)


def member_kernel(chips, own_ref, other_ref, me_ref, storage_ref, member_ref, adapter_ref, held):
    kept = member_ref.shape[1]
    count = chips * CORES
    wide = own_ref.shape[2] - LANES
    for k in range(chips):
        held[k : k + 1, :] = own_ref[k, :, wide:].astype(jnp.float32)[0:1]
        held[chips + k : chips + k + 1, :] = other_ref[k, :, wide:].astype(jnp.float32)[0:1]
    adapter = (held[:, 0:1] + 256.0 * held[:, 1:2]).astype(jnp.int32)
    adapter_ref[...] = adapter
    table = storage_ref.shape[1]
    chosen = jnp.where(iota((count, table), 1) == adapter, storage_ref[...], 0)
    storage = jnp.sum(chosen.astype(jnp.float32), axis=1, keepdims=True).astype(jnp.int32)
    member_ref[...] = (storage - me_ref[0] * kept == iota((count, kept), 1)).astype(jnp.int32)


def spread_kernel(own_ref, other_ref, out_ref):
    total = own_ref[...].astype(jnp.float32) + other_ref[...].astype(jnp.float32)
    for k in range(out_ref.shape[0]):
        out_ref[k] = total.astype(out_ref.dtype)


def project_kernel(rows_ref, query_hbm, fresh_hbm, query_ref, fresh_ref, query_w, fresh_w, sems):
    chunks = sems.shape[1]
    deep = query_w.shape[0] // chunks
    copies = []
    for c in range(chunks):
        part = pl.ds(c * deep, deep)
        copies.append(
            (
                pltpu.make_async_copy(query_hbm.at[part], query_w.at[part], sems.at[0, c]),
                pltpu.make_async_copy(fresh_hbm.at[part], fresh_w.at[part], sems.at[1, c]),
            )
        )
    for pair in copies:
        for copy in pair:
            copy.start()
    query = jnp.zeros(query_ref.shape, jnp.float32)
    fresh = jnp.zeros(fresh_ref.shape, jnp.float32)
    for c, pair in enumerate(copies):
        for copy in pair:
            copy.wait()
        part = slice(c * deep, (c + 1) * deep)
        rows = rows_ref[:, part]
        query = query + dot(rows, query_w[part, :])
        fresh = fresh + dot(rows, fresh_w[part, :])
    query_ref[...] = query
    fresh_ref[...] = fresh


def up_kernel(chips, low_ref, query_ref, fresh_ref, up_ref, own_ref, away_ref):
    count = chips * CORES
    rank = low_ref.shape[2]
    columns = query_ref.shape[1]
    low = low_ref[0].astype(jnp.float32)
    for k in range(1, chips):
        low = low + low_ref[k].astype(jnp.float32)
    low = low.astype(jnp.bfloat16)
    wide = count * rank
    repeat = (iota((rank, wide), 1) % rank == iota((rank, wide), 0)).astype(jnp.bfloat16)
    spread = jnp.where(
        iota((count, wide), 1) // rank == iota((count, wide), 0), dot(low, repeat), 0.0
    ).astype(jnp.bfloat16)
    query = query_ref[...] + dot(spread, up_ref[...])
    fresh = fresh_ref[...]
    for ref, part in ((own_ref, slice(0, chips)), (away_ref, slice(chips, count))):
        ref[:, :columns] = query[part].astype(jnp.bfloat16)
        ref[:, columns:] = fresh[part].astype(jnp.bfloat16)


def pair_kernel(own_ref, other_ref, out_ref):
    own, other = own_ref[...].astype(jnp.float32), other_ref[...].astype(jnp.float32)
    for k in range(out_ref.shape[0]):
        out_ref[k] = jnp.concatenate([own[k : k + 1], other[k : k + 1]], axis=0).astype(out_ref.dtype)


def pieces_of(slots, select, whole, size):
    if size >= whole:
        each = size // whole
        total = None
        for c in range(each):
            part = dot(select(each, c), slots[:, c * whole : (c + 1) * whole])
            total = part if total is None else total + part
        return total
    return jnp.concatenate([dot(select(0, p), slots) for p in range(whole // size)], axis=1)


def attend_kernel(chips, columns, fresh_columns, first, *refs):
    pairs_ref, length_ref, me_ref, cache_hbm = refs[:4]
    refs = refs[4:]
    if not first:
        past, refs = refs[:2], refs[2:]
    own_ref, away_ref = refs[:2]
    refs = refs[2:]
    if first:
        keep, refs = refs[:2], refs[2:]
    held, scores, cache_ref, sems = refs
    copies = [
        pltpu.make_async_copy(cache_hbm.at[0, i], cache_ref.at[0, i], sems.at[i]) for i in range(2)
    ]
    for copy in copies:
        copy.start()
    count = chips * CORES
    cache = cache_ref.shape[2]
    core = me_ref[0] % CORES
    for k in range(chips):
        held[k * CORES : (k + 1) * CORES, :] = pairs_ref[k].astype(jnp.float32)
    slots = held[...].astype(jnp.bfloat16)
    origin = pair_origin(core, (H, count), 1)
    head = iota((H, count), 0)

    def query_pick(each, c):
        if each:
            return (head == origin * each + c).astype(jnp.bfloat16)
        return (head * (HD // columns) + c == origin).astype(jnp.bfloat16)

    def fresh_pick(offset):
        def pick(each, c):
            want = head // GROUP + offset
            if each:
                return (want == origin * each + c).astype(jnp.bfloat16)
            return (want * (HD // fresh_columns) + c == origin).astype(jnp.bfloat16)

        return pick

    query = pieces_of(slots[:, :columns], query_pick, HD, columns)
    fresh = slots[:, columns:]
    new = [
        (
            pieces_of(fresh, fresh_pick(0), HD, fresh_columns),
            pieces_of(fresh, fresh_pick(KVH), HD, fresh_columns),
        )
    ]
    if first:
        keep[0][...], keep[1][...] = new[0]
    else:
        new.insert(0, (past[0][...], past[1][...]))
    scale = 1.0 / math.sqrt(HD)
    copies[0].wait()
    for j in range(KVH):
        rows = slice(j * GROUP, (j + 1) * GROUP)
        scores[rows, :] = dot(
            query[rows].astype(jnp.bfloat16), cache_ref[0, 0, :, j * HD : (j + 1) * HD], LAST
        )
    in_cache = iota((H, cache), 1) < length_ref[0]
    old = jnp.where(in_cache, scores[...] * scale, -jnp.inf)
    news = [jnp.sum(query * keys, axis=1, keepdims=True) * scale for keys, _ in new]
    peak = jnp.max(old, axis=1, keepdims=True)
    for score in news:
        peak = jnp.maximum(peak, score)
    old = jnp.exp(old - peak)
    news = [jnp.exp(score - peak) for score in news]
    total = jnp.sum(old, axis=1, keepdims=True)
    for score in news:
        total = total + score
    old = old / total
    extra = jnp.zeros((H, HD), jnp.float32)
    for score, (_, values) in zip(news, new):
        extra = extra + (score / total).astype(jnp.bfloat16).astype(jnp.float32) * values
    copies[1].wait()
    mixed = jnp.concatenate(
        [
            dot(
                old[j * GROUP : (j + 1) * GROUP].astype(jnp.bfloat16),
                cache_ref[0, 1, :, j * HD : (j + 1) * HD],
            )
            for j in range(KVH)
        ],
        axis=0,
    )
    mixed = (mixed + extra).astype(jnp.bfloat16)
    target = slot_origin(core, (count, H), 0)
    head = iota((count, H), 1)
    if columns >= HD:
        each = columns // HD
        out = [dot((head == target * each + c).astype(jnp.bfloat16), mixed) for c in range(each)]
        out = out[0] if each == 1 else jnp.concatenate(out, axis=1)
    else:
        parts = HD // columns
        out = jnp.zeros((count, columns), jnp.float32)
        for p in range(parts):
            pick = (head * parts + p == target).astype(jnp.bfloat16)
            out = out + dot(pick, mixed[:, p * columns : (p + 1) * columns])
    own_ref[...] = out[:chips].astype(jnp.bfloat16)
    away_ref[...] = out[chips:].astype(jnp.bfloat16)


def output_kernel(chips, pairs_ref, weight_hbm, own_ref, away_ref, held, weight, sems):
    chunks = sems.shape[0]
    wide = weight.shape[1] // chunks
    copies = [
        pltpu.make_async_copy(
            weight_hbm.at[:, pl.ds(c * wide, wide)], weight.at[:, pl.ds(c * wide, wide)], sems.at[c]
        )
        for c in range(chunks)
    ]
    for copy in copies:
        copy.start()
    for k in range(chips):
        pair = pairs_ref[k].astype(jnp.float32)
        for l in range(CORES):
            held[l * chips + k : l * chips + k + 1, :] = pair[l : l + 1]
    rows = held[...].astype(jnp.bfloat16)
    for c, copy in enumerate(copies):
        copy.wait()
        part = slice(c * wide, (c + 1) * wide)
        out = dot(rows, weight[:, part])
        own_ref[:, part] = out[:chips]
        away_ref[:, part] = out[chips:].astype(jnp.bfloat16)


def partial_kernel(own_ref, other_ref, out_ref):
    total = own_ref[...] + other_ref[...].astype(jnp.float32)
    wide = out_ref.shape[2]
    for k in range(out_ref.shape[0]):
        for i in range(FOLD):
            out_ref[k, i : i + 1, :] = total[k : k + 1, i * wide : (i + 1) * wide].astype(
                out_ref.dtype
            )


def finish_kernel(last, parts_ref, hidden_ref, scale_ref, out_ref, *spread):
    total = parts_ref[0].astype(jnp.float32)
    for k in range(1, parts_ref.shape[0]):
        total = total + parts_ref[k].astype(jnp.float32)
    wide = parts_ref.shape[2]
    total = jnp.concatenate([total[i : i + 1] for i in range(FOLD)], axis=1)
    total = total.astype(jnp.bfloat16).astype(jnp.float32)
    hidden = (hidden_ref[...].astype(jnp.float32) + total).astype(jnp.bfloat16)
    out_ref[...] = hidden
    if not last:
        hidden = normalized(hidden.astype(jnp.float32), scale_ref[...].astype(jnp.float32))
        folded(spread[0], hidden.astype(jnp.float32))


def shards(
    hidden_state_input,
    attention_norm_scale,
    query_weight,
    key_value_weight,
    output_weight,
    adapter_down_weight,
    adapter_up_weight,
    row_adapter_index,
    adapter_storage_index,
    cache_length_per_row,
    key_value_cache,
):
    count = lax.axis_size(AXIS)
    chips = count // CORES
    kept, width, rank = adapter_down_weight.shape
    columns = query_weight.shape[1]
    fresh_columns = key_value_weight.shape[1]
    message = columns + fresh_columns
    smem, vmem = pltpu.SMEM, pltpu.VMEM
    large = 52 << 20
    me = lax.axis_index(AXIS).astype(jnp.int32).reshape(1)
    down = adapter_down_weight.transpose(0, 2, 1)
    scale = attention_norm_scale[None]
    storage = adapter_storage_index[None]

    def exchange(own, away):
        wide = own.shape[1]
        other = sibling(away, count)
        pairs = call(pair_kernel, shape((chips, CORES, wide)), "pair")(own, other)
        return chips_swap(pairs, count)

    hidden = hidden_state_input
    carried = call(first_kernel, shape((chips, FOLD, width // FOLD + LANES)), "first")(
        hidden, scale, row_adapter_index, specs=[vmem, vmem, smem]
    )
    results = []
    past = ()
    for step in range(STEPS):
        first, last = step == 0, step == STEPS - 1
        own = chips_swap(carried, count)
        other = sibling(own, count)
        if first:
            member, adapter = call(
                functools.partial(member_kernel, chips),
                [shape((count, kept), jnp.int32), shape((count, 1), jnp.int32)],
                "member",
                [pltpu.VMEM((count, LANES), jnp.float32)],
            )(own, other, me, storage, specs=[vmem, vmem, smem, vmem])
            up_of = adapter_up_weight[adapter[:, 0]].reshape(count * rank, columns)
        rows, low, away = call(
            functools.partial(low_kernel, chips),
            [shape((count, width)), shape((count, rank)), shape((count, rank))],
            "low",
            [pltpu.VMEM((count, width), jnp.float32)],
            moved=2 << 20,
        )(own, other, me, member, down, specs=[vmem, vmem, smem, vmem, vmem])
        low = call(spread_kernel, shape((chips, count, rank)), "spread")(low, sibling(away, count))
        low = chips_swap(low, count)
        chunks = 8
        query, fresh = call(
            project_kernel,
            [shape((count, columns), jnp.float32), shape((count, fresh_columns), jnp.float32)],
            "project",
            [
                pltpu.VMEM((width, columns), jnp.bfloat16),
                pltpu.VMEM((width, fresh_columns), jnp.bfloat16),
                pltpu.SemaphoreType.DMA((2, chunks)),
            ],
            vmem=large,
            flops=2 * count * width * message,
            moved=2 * width * message,
        )(rows, query_weight, key_value_weight, specs=[vmem, pl.ANY, pl.ANY])
        own, away = call(
            functools.partial(up_kernel, chips), [shape((chips, message))] * 2, "up"
        )(low, query, fresh, up_of)

        pairs = exchange(own, away)
        outs = [shape((chips, columns))] * 2
        if first:
            outs = outs + [shape((H, HD), jnp.float32)] * 2
        outs = call(
            functools.partial(attend_kernel, chips, columns, fresh_columns, first),
            outs,
            "attend",
            [
                pltpu.VMEM((count, message), jnp.float32),
                pltpu.VMEM((H, key_value_cache.shape[2]), jnp.float32),
                pltpu.VMEM(key_value_cache.shape, jnp.bfloat16),
                pltpu.SemaphoreType.DMA((2,)),
            ],
            vmem=large,
            moved=2 << 20,
        )(
            pairs,
            cache_length_per_row,
            me,
            key_value_cache,
            *past,
            specs=[vmem, smem, smem, pl.ANY] + [vmem] * len(past),
        )
        if first:
            past = tuple(outs[2:])

        pairs = exchange(outs[0], outs[1])
        chunks = 8
        own, away = call(
            functools.partial(output_kernel, chips),
            [shape((chips, width), jnp.float32), shape((chips, width))],
            "output",
            [
                pltpu.VMEM((count, columns), jnp.float32),
                pltpu.VMEM((columns, width), jnp.bfloat16),
                pltpu.SemaphoreType.DMA((chunks,)),
            ],
            vmem=large,
            flops=2 * count * width * columns,
            moved=2 * width * columns,
        )(pairs, output_weight, specs=[vmem, pl.ANY])

        parts = call(partial_kernel, shape((chips, FOLD, width // FOLD)), "partial")(
            own, sibling(away, count)
        )
        parts = chips_swap(parts, count)
        outs = [shape((1, width))]
        if not last:
            outs = outs + [shape((chips, FOLD, width // FOLD))]
        outs = call(functools.partial(finish_kernel, last), outs, "finish")(parts, hidden, scale)
        hidden = outs[0]
        results.append(hidden)
        if not last:
            carried = outs[1]
    return jnp.stack(results)


def solution(mesh):
    in_specs = (
        P(("groups", "replica"), None),
        P(),
        P(None, "replica"),
        P(None, "replica"),
        P("replica", None),
        P("replica", None, None),
        P(None, None, "replica"),
        P(("groups", "replica")),
        P(),
        P(("groups", "replica")),
        P(("groups", "replica"), None, None, None),
    )
    out_specs = P(None, ("groups", "replica"), None)
    return jax.shard_map(shards, mesh=mesh, in_specs=in_specs, out_specs=out_specs, check_vma=False)
```

```python
import functools
import math

import jax
import jax.numpy as jnp
from jax import lax
from jax.experimental import pallas as pl
from jax.experimental.pallas import tpu as pltpu
from jax.sharding import PartitionSpec as P

H = 64
KVH = 8
HD = 128
STEPS = 2
GROUP = H // KVH
EPS = 1e-05
AXIS = "replica"
LANES = 128
LAST = (((1,), (1,)), ((), ()))
FIRST = (((0,), (0,)), ((), ()))

CORES = 2
FOLD = 8


def split_of(count):
    far = 1 << (count.bit_length() // 2)
    return far, count // far


def shift(block, distance, count):
    return lax.ppermute(block, AXIS, [(i, i ^ distance) for i in range(count)])


def across(block, strides, count):
    return [block] + [shift(block, d, count) for d in strides]


def swap(blocks):
    return lax.all_to_all(blocks, AXIS, split_axis=0, concat_axis=0, tiled=True)


def chips_swap(blocks, count):
    groups = [[i for i in range(count) if i % CORES == c] for c in range(CORES)]
    return lax.all_to_all(
        blocks, AXIS, split_axis=0, concat_axis=0, axis_index_groups=groups, tiled=True
    )


def call(body, outs, name, scratch=(), vmem=20 << 20, flops=1 << 20, moved=1 << 18):
    def run(*operands, specs=None):
        specs = specs or [pltpu.VMEM] * len(operands)
        return pl.pallas_call(
            body,
            out_shape=outs,
            in_specs=[pl.BlockSpec(memory_space=s) for s in specs],
            out_specs=[pl.BlockSpec(memory_space=pltpu.VMEM)] * len(outs),
            scratch_shapes=list(scratch),
            compiler_params=pltpu.CompilerParams(vmem_limit_bytes=vmem),
            cost_estimate=pl.CostEstimate(flops=flops, bytes_accessed=moved, transcendentals=0),
            name=name,
        )(*operands)

    return run


def shape(dims, dtype=jnp.bfloat16):
    return jax.ShapeDtypeStruct(dims, dtype)


def iota(dims, axis):
    return lax.broadcasted_iota(jnp.int32, dims, axis)


def dot(a, b, contract=(((1,), (0,)), ((), ()))):
    return lax.dot_general(a, b, contract, preferred_element_type=jnp.float32)


def normalized(hidden, scale):
    factor = lax.rsqrt(jnp.mean(hidden * hidden, axis=-1, keepdims=True) + EPS)
    return (hidden * factor * scale).astype(jnp.bfloat16)


def folded(out_ref, row):
    wide = row.shape[1] // FOLD
    for k in range(out_ref.shape[0]):
        for i in range(FOLD):
            out_ref[k, i : i + 1, :wide] = row[:, i * wide : (i + 1) * wide].astype(out_ref.dtype)


def first_kernel(hidden_ref, scale_ref, adapter_ref, out_ref):
    width = hidden_ref.shape[1]
    hidden = hidden_ref[...].astype(jnp.float32)
    out_ref[:, :width] = normalized(hidden, scale_ref[...].astype(jnp.float32))
    digit = iota((1, LANES), 1)
    adapter = adapter_ref[0]
    high, low = adapter // 256, adapter % 256
    digits = jnp.where(digit == 0, low, jnp.where(digit == 1, high, 0)).astype(jnp.float32)
    out_ref[:, width:] = digits.astype(jnp.bfloat16)


def stash_kernel(amount, token_ref, *refs):
    sources, refs = refs[:amount], refs[amount:]
    outs, out_token, sems = refs[:amount], refs[amount], refs[-1]
    copies = [
        pltpu.make_async_copy(sources[i], outs[i], sems.at[i]) for i in range(amount)
    ]
    for copy in copies:
        copy.start()
    out_token[...] = token_ref[...] * 0.0
    for copy in copies:
        copy.wait()


def member_kernel(near, far, width, *refs):
    pieces, refs = refs[:near], refs[near:]
    me_ref, storage_ref, up_hbm, member_ref, up_ref, held, sems = refs
    kept = member_ref.shape[1]
    count = near * far
    me = me_ref[0]
    for l in range(near):
        digits = pieces[l][:, width:].astype(jnp.float32)
        for k in range(far):
            held[pl.ds(me ^ (k * near + l), 1), :] = digits[k : k + 1]
    adapter = held[:, 0:1] + 256.0 * held[:, 1:2]
    row = iota((count, 1), 0)
    copies = []
    for r in range(count):
        index = jnp.sum(jnp.where(row == r, adapter, 0.0)).astype(jnp.int32)
        copies.append(pltpu.make_async_copy(up_hbm.at[index], up_ref.at[r], sems.at[r]))
        copies[-1].start()
    table = storage_ref.shape[1]
    chosen = jnp.where(iota((count, table), 1) == adapter.astype(jnp.int32), storage_ref[...], 0)
    storage = jnp.sum(chosen.astype(jnp.float32), axis=1, keepdims=True).astype(jnp.int32)
    member_ref[...] = (storage - me * kept == iota((count, kept), 1)).astype(jnp.int32)
    for copy in copies:
        copy.wait()


def low_terms(held, member_ref, down_ref, rows_ref, low_ref):
    rows = held[...].astype(jnp.bfloat16)
    rows_ref[...] = rows
    low = jnp.zeros(low_ref.shape, jnp.float32)
    for index in range(down_ref.shape[0]):
        part = dot(rows, down_ref[index], LAST)
        low = jnp.where(member_ref[:, index : index + 1] > 0, part, low)
    low_ref[...] = low.astype(jnp.bfloat16)


def low_first_kernel(near, far, *refs):
    pieces, refs = refs[:near], refs[near:]
    me_ref, member_ref, down_ref, rows_ref, low_ref, held = refs
    width = held.shape[1]
    for l in range(near):
        block = pieces[l][:, :width].astype(jnp.float32)
        for k in range(far):
            held[pl.ds(me_ref[0] ^ (k * near + l), 1), :] = block[k : k + 1]
    low_terms(held, member_ref, down_ref, rows_ref, low_ref)


def low_later_kernel(own_ref, other_ref, me_ref, member_ref, down_ref, rows_ref, low_ref, held):
    core = me_ref[0] % CORES
    for ref, flip in ((own_ref, 0), (other_ref, 1)):
        wide = ref.shape[2]
        for k in range(ref.shape[0]):
            block = ref[k].astype(jnp.float32)
            row = pl.ds(k * CORES + (core ^ flip), 1)
            for i in range(FOLD):
                held[row, i * wide : (i + 1) * wide] = block[i : i + 1]
    low_terms(held, member_ref, down_ref, rows_ref, low_ref)


def sum_kernel(*refs):
    total = refs[0][...].astype(jnp.float32)
    for ref in refs[1:-1]:
        total = total + ref[...].astype(jnp.float32)
    refs[-1][...] = total.astype(refs[-1].dtype)


def project_kernel(rows_ref, query_w, fresh_w, query_ref, fresh_ref):
    query_ref[...] = dot(rows_ref[...], query_w[...])
    fresh_ref[...] = dot(rows_ref[...], fresh_w[...])


def up_kernel(parts, *refs):
    lows, (query_ref, fresh_ref, up_ref, out_ref, held) = refs[:parts], refs[parts:]
    count, columns = query_ref.shape
    rank = lows[0].shape[1]
    low = lows[0][...].astype(jnp.float32)
    for ref in lows[1:]:
        low = low + ref[...].astype(jnp.float32)
    low = low.astype(jnp.bfloat16)
    wide = count * rank
    repeat = (iota((rank, wide), 1) % rank == iota((rank, wide), 0)).astype(jnp.bfloat16)
    spread = jnp.where(
        iota((count, wide), 1) // rank == iota((count, wide), 0), dot(low, repeat), 0.0
    ).astype(jnp.bfloat16)
    query = query_ref[...]
    for r in range(count // 2):
        part = slice(2 * r * rank, 2 * (r + 1) * rank)
        query = query + dot(
            spread[:, part],
            jnp.concatenate([up_ref[2 * r], up_ref[2 * r + 1]], axis=0),
        )
    line = out_ref.shape[2]
    lines = columns // line
    held[...] = jnp.zeros(held.shape, jnp.float32)
    for c in range(lines):
        held[:, c, :] = query[:, c * line : (c + 1) * line]
    fresh = fresh_ref[...]
    if fresh.shape[1] < line:
        fresh = jnp.concatenate(
            [fresh, jnp.zeros((count, line - fresh.shape[1]), jnp.float32)], axis=1
        )
    held[:, lines, :] = fresh
    for k in range(count):
        out_ref[k] = held[k].astype(jnp.bfloat16)


def pieces_of(lines, select, whole, size):
    if size >= whole:
        total = dot(select(len(lines), 0), lines[0])
        for c in range(1, len(lines)):
            total = total + dot(select(len(lines), c), lines[c])
        return total
    return jnp.concatenate([dot(select(0, p), lines[0]) for p in range(whole // size)], axis=1)


def attend_kernel(columns, fresh_columns, first, *refs):
    lines_ref, length_ref, cache_ref = refs[:3]
    refs = refs[3:]
    if not first:
        past, refs = refs[:2], refs[2:]
    out_ref, refs = refs[0], refs[1:]
    if first:
        keep, refs = refs[:2], refs[2:]
    held, scores = refs
    count, _, line = lines_ref.shape
    cache = cache_ref.shape[2]
    for k in range(count):
        held[k] = lines_ref[k].astype(jnp.float32)
    each = columns // line
    lines = [held[:, c, :].astype(jnp.bfloat16) for c in range(each + 1)]
    origin = iota((H, count), 1)
    head = iota((H, count), 0)

    def query_pick(each, c):
        if each:
            return (head == origin * each + c).astype(jnp.bfloat16)
        return (head * (HD // columns) + c == origin).astype(jnp.bfloat16)

    def fresh_pick(offset):
        def pick(each, c):
            want = head // GROUP + offset
            if each:
                return (want == origin * each + c).astype(jnp.bfloat16)
            return (want * (HD // fresh_columns) + c == origin).astype(jnp.bfloat16)

        return pick

    query = pieces_of(lines[:each], query_pick, HD, columns)
    fresh = [lines[each][:, :fresh_columns]]
    new = [
        (
            pieces_of(fresh, fresh_pick(0), HD, fresh_columns),
            pieces_of(fresh, fresh_pick(KVH), HD, fresh_columns),
        )
    ]
    if first:
        keep[0][...], keep[1][...] = new[0]
    else:
        new.insert(0, (past[0][...], past[1][...]))
    scale = 1.0 / math.sqrt(HD)
    for j in range(KVH):
        rows = slice(j * GROUP, (j + 1) * GROUP)
        scores[rows, :] = dot(
            query[rows].astype(jnp.bfloat16), cache_ref[0, 0, :, j * HD : (j + 1) * HD], LAST
        )
    in_cache = iota((H, cache), 1) < length_ref[0]
    old = jnp.where(in_cache, scores[...] * scale, -jnp.inf)
    news = [jnp.sum(query * keys, axis=1, keepdims=True) * scale for keys, _ in new]
    peak = jnp.max(old, axis=1, keepdims=True)
    for score in news:
        peak = jnp.maximum(peak, score)
    old = jnp.exp(old - peak)
    news = [jnp.exp(score - peak) for score in news]
    total = jnp.sum(old, axis=1, keepdims=True)
    for score in news:
        total = total + score
    old = old / total
    extra = jnp.zeros((H, HD), jnp.float32)
    for score, (_, values) in zip(news, new):
        extra = extra + (score / total).astype(jnp.bfloat16).astype(jnp.float32) * values
    mixed = jnp.concatenate(
        [
            dot(
                old[j * GROUP : (j + 1) * GROUP].astype(jnp.bfloat16),
                cache_ref[0, 1, :, j * HD : (j + 1) * HD],
            )
            for j in range(KVH)
        ],
        axis=0,
    )
    mixed = mixed + extra
    if columns >= HD:
        for k in range(count):
            out_ref[k] = mixed[k * each : (k + 1) * each].astype(jnp.bfloat16)
    else:
        parts = HD // columns
        out = jnp.zeros((count, columns), jnp.float32)
        for p in range(parts):
            pick = (iota((count, H), 1) * parts + p == iota((count, H), 0)).astype(jnp.bfloat16)
            out = out + dot(pick, mixed[:, p * columns : (p + 1) * columns].astype(jnp.bfloat16))
        for k in range(count):
            out_ref[k] = out[k : k + 1].astype(jnp.bfloat16)


def output_kernel(lines_ref, me_ref, weight_ref, own_ref, away_ref, held):
    count, each, line = lines_ref.shape
    chips = count // CORES
    for k in range(count):
        held[k, :each, :] = lines_ref[k].astype(jnp.float32)
    slot = iota((count, count), 0)
    origin = (slot % chips) * CORES + ((me_ref[0] % CORES) ^ (slot // chips))
    order = (iota((count, count), 1) == origin).astype(jnp.bfloat16)
    rows = jnp.concatenate(
        [dot(order, held[:, c, :].astype(jnp.bfloat16)).astype(jnp.bfloat16) for c in range(each)],
        axis=1,
    )
    width = weight_ref.shape[1]
    wide = width // 8
    for c in range(8):
        part = slice(c * wide, (c + 1) * wide)
        out = dot(rows, weight_ref[:, part])
        own_ref[:, part] = out[:chips]
        away_ref[:, part] = out[chips:].astype(jnp.bfloat16)


def partial_kernel(own_ref, other_ref, out_ref):
    total = own_ref[...] + other_ref[...].astype(jnp.float32)
    wide = out_ref.shape[2]
    for k in range(out_ref.shape[0]):
        for i in range(FOLD):
            out_ref[k, i : i + 1, :] = total[k : k + 1, i * wide : (i + 1) * wide].astype(
                out_ref.dtype
            )


def finish_kernel(last, parts_ref, hidden_ref, scale_ref, out_ref, *spread):
    total = parts_ref[0].astype(jnp.float32)
    for k in range(1, parts_ref.shape[0]):
        total = total + parts_ref[k].astype(jnp.float32)
    total = jnp.concatenate([total[i : i + 1] for i in range(FOLD)], axis=1)
    total = total.astype(jnp.bfloat16).astype(jnp.float32)
    before = hidden_ref[...].astype(jnp.float32)
    hidden = (before + total).astype(jnp.bfloat16).astype(jnp.float32)
    if last:
        out_ref[...] = jnp.concatenate([before, hidden], axis=0).astype(jnp.bfloat16)
    else:
        out_ref[...] = hidden.astype(jnp.bfloat16)
        folded(spread[0], normalized(hidden, scale_ref[...].astype(jnp.float32)).astype(jnp.float32))


def shards(
    hidden_state_input,
    attention_norm_scale,
    query_weight,
    key_value_weight,
    output_weight,
    adapter_down_weight,
    adapter_up_weight,
    row_adapter_index,
    adapter_storage_index,
    cache_length_per_row,
    key_value_cache,
):
    count = lax.axis_size(AXIS)
    chips = count // CORES
    far, near = split_of(count)
    far_steps = [k * near for k in range(1, far)]
    near_steps = list(range(1, near))
    kept, width, rank = adapter_down_weight.shape
    columns = query_weight.shape[1]
    fresh_columns = key_value_weight.shape[1]
    line = min(HD, columns)
    smem, vmem = pltpu.SMEM, pltpu.VMEM
    me = lax.axis_index(AXIS).astype(jnp.int32).reshape(1)
    down = adapter_down_weight.transpose(0, 2, 1)
    scale = attention_norm_scale[None]
    storage = adapter_storage_index[None]

    def stash(token, arrays, limit):
        outs = call(
            functools.partial(stash_kernel, len(arrays)),
            [pltpu.VMEM(a.shape, a.dtype) for a in arrays] + [shape((8, LANES), jnp.float32)],
            "stash",
            [pltpu.SemaphoreType.DMA((len(arrays),))],
            vmem=limit,
            moved=sum(2 * a.size for a in arrays),
        )(token, *arrays, specs=[vmem] + [pl.ANY] * len(arrays))
        return outs[:-1], outs[-1]

    hidden = hidden_state_input
    (carried,) = call(first_kernel, [shape((1, width + LANES))], "first")(
        hidden, scale, row_adapter_index, specs=[vmem, vmem, smem]
    )
    past = ()
    for step in range(STEPS):
        first, last = step == 0, step == STEPS - 1
        outs = [shape((count, width)), shape((count, rank))]
        scratch = [pltpu.VMEM((count, width), jnp.float32)]
        if first:
            token = jnp.zeros((8, LANES), jnp.float32)
            (query_w, output_w, fresh_w, down_w, cache), token = stash(
                token,
                [query_weight, output_weight, key_value_weight, down, key_value_cache],
                41 << 20,
            )
            pieces = lax.optimization_barrier((*across(carried, far_steps, count), token))
            carried = jnp.concatenate(pieces[:-1], axis=0)
            pieces = across(carried, near_steps, count)
            member, up_of = call(
                functools.partial(member_kernel, near, far, width),
                [shape((count, kept), jnp.int32), pltpu.VMEM((count, rank, columns), jnp.bfloat16)],
                "member",
                [pltpu.VMEM((count, LANES), jnp.float32), pltpu.SemaphoreType.DMA((count,))],
                vmem=16 << 20,
            )(*pieces, me, storage, adapter_up_weight, specs=[vmem] * near + [smem, vmem, pl.ANY])
            rows, low = call(
                functools.partial(low_first_kernel, near, far), outs, "low", scratch
            )(*pieces, me, member, down_w, specs=[vmem] * near + [smem, vmem, vmem])
        else:
            own = chips_swap(carried, count)
            rows, low = call(low_later_kernel, outs, "low", scratch)(
                own, shift(own, 1, count), me, member, down_w, specs=[vmem, vmem, smem, vmem, vmem]
            )
        (low,) = call(sum_kernel, [shape((count, rank))], "sum")(*across(low, near_steps, count))
        lows = across(low, far_steps, count)
        query, fresh = call(
            project_kernel,
            [shape((count, columns), jnp.float32), shape((count, fresh_columns), jnp.float32)],
            "project",
            flops=2 * count * width * (columns + fresh_columns),
            moved=2 * width * (columns + fresh_columns),
        )(rows, query_w, fresh_w)
        (lines,) = call(
            functools.partial(up_kernel, far),
            [shape((count, 8, line))],
            "up",
            [pltpu.VMEM((count, 8, line), jnp.float32)],
        )(*lows, query, fresh, up_of)

        lines = swap(lines)
        outs = [shape((count, columns // line, line))]
        if first:
            outs = outs + [shape((H, HD), jnp.float32)] * 2
        outs = call(
            functools.partial(attend_kernel, columns, fresh_columns, first),
            outs,
            "attend",
            [
                pltpu.VMEM((count, 8, line), jnp.float32),
                pltpu.VMEM((H, key_value_cache.shape[2]), jnp.float32),
            ],
            moved=2 << 20,
        )(
            lines,
            cache_length_per_row,
            cache,
            *past,
            specs=[vmem, smem, vmem] + [vmem] * len(past),
        )
        if first:
            past = tuple(outs[1:])

        lines = swap(outs[0])
        own, away = call(
            output_kernel,
            [shape((chips, width), jnp.float32), shape((chips, width))],
            "output",
            [pltpu.VMEM((count, 8, line), jnp.float32)],
            flops=2 * count * width * columns,
            moved=2 * width * columns,
        )(lines, me, output_w, specs=[vmem, smem, vmem])

        (parts,) = call(partial_kernel, [shape((chips, FOLD, width // FOLD))], "partial")(
            own, shift(away, 1, count)
        )
        parts = chips_swap(parts, count)
        outs = [shape((2 if last else 1, width))]
        if not last:
            outs = outs + [shape((chips, FOLD, width // FOLD))]
        outs = call(functools.partial(finish_kernel, last), outs, "finish")(parts, hidden, scale)
        if last:
            return outs[0].reshape(STEPS, 1, width)
        hidden, carried = outs


def solution(mesh):
    in_specs = (
        P(("groups", "replica"), None),
        P(),
        P(None, "replica"),
        P(None, "replica"),
        P("replica", None),
        P("replica", None, None),
        P(None, None, "replica"),
        P(("groups", "replica")),
        P(),
        P(("groups", "replica")),
        P(("groups", "replica"), None, None, None),
    )
    out_specs = P(None, ("groups", "replica"), None)
    return jax.shard_map(shards, mesh=mesh, in_specs=in_specs, out_specs=out_specs, check_vma=False)
```

```python
import functools
import math

import jax
import jax.numpy as jnp
from jax import lax
from jax.experimental import pallas as pl
from jax.experimental.pallas import tpu as pltpu
from jax.sharding import PartitionSpec as P

H = 64
KVH = 8
HD = 128
STEPS = 2
GROUP = H // KVH
EPS = 1e-05
AXIS = "replica"
LANES = 128
LAST = (((1,), (1,)), ((), ()))
FIRST = (((0,), (0,)), ((), ()))

CORES = 2
FOLD = 8


def split_of(count):
    far = 1 << (count.bit_length() // 2)
    return far, count // far


def shift(block, distance, count):
    return lax.ppermute(block, AXIS, [(i, i ^ distance) for i in range(count)])


def across(block, strides, count):
    return [block] + [shift(block, d, count) for d in strides]


def swap(blocks):
    return lax.all_to_all(blocks, AXIS, split_axis=0, concat_axis=0, tiled=True)


def chips_swap(blocks, count):
    groups = [[i for i in range(count) if i % CORES == c] for c in range(CORES)]
    return lax.all_to_all(
        blocks, AXIS, split_axis=0, concat_axis=0, axis_index_groups=groups, tiled=True
    )


def call(body, outs, name, scratch=(), vmem=20 << 20, flops=1 << 20, moved=1 << 18):
    def run(*operands, specs=None):
        specs = specs or [pltpu.VMEM] * len(operands)
        return pl.pallas_call(
            body,
            out_shape=outs,
            in_specs=[pl.BlockSpec(memory_space=s) for s in specs],
            out_specs=[pl.BlockSpec(memory_space=pltpu.VMEM)] * len(outs),
            scratch_shapes=list(scratch),
            compiler_params=pltpu.CompilerParams(vmem_limit_bytes=vmem),
            cost_estimate=pl.CostEstimate(flops=flops, bytes_accessed=moved, transcendentals=0),
            name=name,
        )(*operands)

    return run


def shape(dims, dtype=jnp.bfloat16):
    return jax.ShapeDtypeStruct(dims, dtype)


def iota(dims, axis):
    return lax.broadcasted_iota(jnp.int32, dims, axis)


def dot(a, b, contract=(((1,), (0,)), ((), ()))):
    return lax.dot_general(a, b, contract, preferred_element_type=jnp.float32)


def normalized(hidden, scale):
    factor = lax.rsqrt(jnp.mean(hidden * hidden, axis=-1, keepdims=True) + EPS)
    return (hidden * factor * scale).astype(jnp.bfloat16)


def folded(out_ref, row):
    wide = row.shape[1] // FOLD
    for k in range(out_ref.shape[0]):
        for i in range(FOLD):
            out_ref[k, i : i + 1, :wide] = row[:, i * wide : (i + 1) * wide].astype(out_ref.dtype)


def first_kernel(hidden_ref, scale_ref, adapter_ref, length_ref, out_ref, length_out):
    length_out[...] = jnp.full(length_out.shape, length_ref[0], jnp.int32)
    width = hidden_ref.shape[1]
    hidden = hidden_ref[...].astype(jnp.float32)
    out_ref[:, :width] = normalized(hidden, scale_ref[...].astype(jnp.float32))
    digit = iota((1, LANES), 1)
    adapter = adapter_ref[0]
    high, low = adapter // 256, adapter % 256
    digits = jnp.where(digit == 0, low, jnp.where(digit == 1, high, 0)).astype(jnp.float32)
    out_ref[:, width:] = digits.astype(jnp.bfloat16)


def stash_kernel(amount, token_ref, *refs):
    sources, refs = refs[:amount], refs[amount:]
    outs, out_token, sems = refs[:amount], refs[amount], refs[-1]
    copies = [
        pltpu.make_async_copy(sources[i], outs[i], sems.at[i]) for i in range(amount)
    ]
    for copy in copies:
        copy.start()
    out_token[...] = token_ref[...] * 0.0
    for copy in copies:
        copy.wait()


def member_kernel(near, far, width, *refs):
    pieces, refs = refs[:near], refs[near:]
    me_ref, storage_ref, member_ref, adapter_ref, held = refs
    kept = member_ref.shape[1]
    count = near * far
    me = me_ref[0]
    for l in range(near):
        digits = pieces[l][:, width:].astype(jnp.float32)
        for k in range(far):
            held[pl.ds(me ^ (k * near + l), 1), :] = digits[k : k + 1]
    adapter = (held[:, 0:1] + 256.0 * held[:, 1:2]).astype(jnp.int32)
    adapter_ref[...] = adapter
    table = storage_ref.shape[1]
    chosen = jnp.where(iota((count, table), 1) == adapter, storage_ref[...], 0)
    storage = jnp.sum(chosen.astype(jnp.float32), axis=1, keepdims=True).astype(jnp.int32)
    member_ref[...] = (storage - me * kept == iota((count, kept), 1)).astype(jnp.int32)


def low_terms(held, member_ref, down_ref, rows_ref, low_ref):
    rows = held[...].astype(jnp.bfloat16)
    rows_ref[...] = rows
    low = jnp.zeros(low_ref.shape, jnp.float32)
    for index in range(down_ref.shape[0]):
        part = dot(rows, down_ref[index], LAST)
        low = jnp.where(member_ref[:, index : index + 1] > 0, part, low)
    low_ref[...] = low.astype(jnp.bfloat16)


def low_first_kernel(near, far, *refs):
    pieces, refs = refs[:near], refs[near:]
    me_ref, member_ref, down_ref, rows_ref, low_ref, held = refs
    width = held.shape[1]
    for l in range(near):
        block = pieces[l][:, :width].astype(jnp.float32)
        for k in range(far):
            held[pl.ds(me_ref[0] ^ (k * near + l), 1), :] = block[k : k + 1]
    low_terms(held, member_ref, down_ref, rows_ref, low_ref)


def low_later_kernel(own_ref, other_ref, me_ref, member_ref, down_ref, rows_ref, low_ref, held):
    core = me_ref[0] % CORES
    for ref, flip in ((own_ref, 0), (other_ref, 1)):
        wide = ref.shape[2]
        for k in range(ref.shape[0]):
            block = ref[k].astype(jnp.float32)
            row = pl.ds(k * CORES + (core ^ flip), 1)
            for i in range(FOLD):
                held[row, i * wide : (i + 1) * wide] = block[i : i + 1]
    low_terms(held, member_ref, down_ref, rows_ref, low_ref)


def sum_kernel(*refs):
    total = refs[0][...].astype(jnp.float32)
    for ref in refs[1:-1]:
        total = total + ref[...].astype(jnp.float32)
    refs[-1][...] = total.astype(refs[-1].dtype)


def project_kernel(rows_ref, query_w, fresh_w, query_ref, fresh_ref):
    query_ref[...] = dot(rows_ref[...], query_w[...])
    fresh_ref[...] = dot(rows_ref[...], fresh_w[...])


def up_kernel(parts, *refs):
    lows, (query_ref, fresh_ref, adapter_ref, up_ref, out_ref, held) = refs[:parts], refs[parts:]
    count, columns = query_ref.shape
    rank = lows[0].shape[1]
    low = lows[0][...].astype(jnp.float32)
    for ref in lows[1:]:
        low = low + ref[...].astype(jnp.float32)
    low = low.astype(jnp.bfloat16)
    query = query_ref[...]
    table = up_ref.shape[0]
    some = min(table, 32)
    wide = some * rank
    repeat = (iota((rank, wide), 1) % rank == iota((rank, wide), 0)).astype(jnp.bfloat16)
    wide_low = dot(low, repeat)
    place = iota((count, wide), 1) // rank
    for start in range(0, table, some):
        spread = jnp.where(place + start == adapter_ref[...], wide_low, 0.0).astype(jnp.bfloat16)
        query = query + dot(spread, up_ref[start : start + some].reshape(wide, columns))
    line = out_ref.shape[2]
    lines = columns // line
    held[...] = jnp.zeros(held.shape, jnp.float32)
    for c in range(lines):
        held[:, c, :] = query[:, c * line : (c + 1) * line]
    fresh = fresh_ref[...]
    if fresh.shape[1] < line:
        fresh = jnp.concatenate(
            [fresh, jnp.zeros((count, line - fresh.shape[1]), jnp.float32)], axis=1
        )
    held[:, lines, :] = fresh
    for k in range(count):
        out_ref[k] = held[k].astype(jnp.bfloat16)


def pieces_of(lines, select, whole, size):
    if size >= whole:
        total = dot(select(len(lines), 0), lines[0])
        for c in range(1, len(lines)):
            total = total + dot(select(len(lines), c), lines[c])
        return total
    return jnp.concatenate([dot(select(0, p), lines[0]) for p in range(whole // size)], axis=1)


def attend_kernel(columns, fresh_columns, first, *refs):
    lines_ref, length_ref, cache_ref = refs[:3]
    refs = refs[3:]
    if not first:
        past, refs = refs[:2], refs[2:]
    out_ref, refs = refs[0], refs[1:]
    if first:
        keep, refs = refs[:2], refs[2:]
    held, scores = refs
    count, _, line = lines_ref.shape
    cache = cache_ref.shape[2]
    for k in range(count):
        held[k] = lines_ref[k].astype(jnp.float32)
    each = columns // line
    lines = [held[:, c, :].astype(jnp.bfloat16) for c in range(each + 1)]
    origin = iota((H, count), 1)
    head = iota((H, count), 0)

    def query_pick(each, c):
        if each:
            return (head == origin * each + c).astype(jnp.bfloat16)
        return (head * (HD // columns) + c == origin).astype(jnp.bfloat16)

    def fresh_pick(offset):
        def pick(each, c):
            want = head // GROUP + offset
            if each:
                return (want == origin * each + c).astype(jnp.bfloat16)
            return (want * (HD // fresh_columns) + c == origin).astype(jnp.bfloat16)

        return pick

    query = pieces_of(lines[:each], query_pick, HD, columns)
    fresh = [lines[each][:, :fresh_columns]]
    new = [
        (
            pieces_of(fresh, fresh_pick(0), HD, fresh_columns),
            pieces_of(fresh, fresh_pick(KVH), HD, fresh_columns),
        )
    ]
    if first:
        keep[0][...], keep[1][...] = new[0]
    else:
        new.insert(0, (past[0][...], past[1][...]))
    scale = 1.0 / math.sqrt(HD)
    for j in range(KVH):
        rows = slice(j * GROUP, (j + 1) * GROUP)
        scores[rows, :] = dot(
            query[rows].astype(jnp.bfloat16), cache_ref[0, 0, :, j * HD : (j + 1) * HD], LAST
        )
    in_cache = iota((H, cache), 1) < length_ref[0:1, 0:1]
    old = jnp.where(in_cache, scores[...] * scale, -jnp.inf)
    news = [jnp.sum(query * keys, axis=1, keepdims=True) * scale for keys, _ in new]
    peak = jnp.max(old, axis=1, keepdims=True)
    for score in news:
        peak = jnp.maximum(peak, score)
    old = jnp.exp(old - peak)
    news = [jnp.exp(score - peak) for score in news]
    total = jnp.sum(old, axis=1, keepdims=True)
    for score in news:
        total = total + score
    old = old / total
    extra = jnp.zeros((H, HD), jnp.float32)
    for score, (_, values) in zip(news, new):
        extra = extra + (score / total).astype(jnp.bfloat16).astype(jnp.float32) * values
    mixed = jnp.concatenate(
        [
            dot(
                old[j * GROUP : (j + 1) * GROUP].astype(jnp.bfloat16),
                cache_ref[0, 1, :, j * HD : (j + 1) * HD],
            )
            for j in range(KVH)
        ],
        axis=0,
    )
    mixed = mixed + extra
    if columns >= HD:
        for k in range(count):
            out_ref[k] = mixed[k * each : (k + 1) * each].astype(jnp.bfloat16)
    else:
        parts = HD // columns
        out = jnp.zeros((count, columns), jnp.float32)
        for p in range(parts):
            pick = (iota((count, H), 1) * parts + p == iota((count, H), 0)).astype(jnp.bfloat16)
            out = out + dot(pick, mixed[:, p * columns : (p + 1) * columns].astype(jnp.bfloat16))
        for k in range(count):
            out_ref[k] = out[k : k + 1].astype(jnp.bfloat16)


def output_kernel(lines_ref, me_ref, weight_ref, own_ref, away_ref, held):
    count, each, line = lines_ref.shape
    chips = count // CORES
    for k in range(count):
        held[k, :each, :] = lines_ref[k].astype(jnp.float32)
    slot = iota((count, count), 0)
    origin = (slot % chips) * CORES + ((me_ref[0] % CORES) ^ (slot // chips))
    order = (iota((count, count), 1) == origin).astype(jnp.bfloat16)
    rows = jnp.concatenate(
        [dot(order, held[:, c, :].astype(jnp.bfloat16)).astype(jnp.bfloat16) for c in range(each)],
        axis=1,
    )
    width = weight_ref.shape[1]
    wide = width // 8
    for c in range(8):
        part = slice(c * wide, (c + 1) * wide)
        out = dot(rows, weight_ref[:, part])
        own_ref[:, part] = out[:chips]
        away_ref[:, part] = out[chips:].astype(jnp.bfloat16)


def partial_kernel(own_ref, other_ref, out_ref):
    total = own_ref[...] + other_ref[...].astype(jnp.float32)
    wide = out_ref.shape[2]
    for k in range(out_ref.shape[0]):
        for i in range(FOLD):
            out_ref[k, i : i + 1, :] = total[k : k + 1, i * wide : (i + 1) * wide].astype(
                out_ref.dtype
            )


def finish_kernel(last, parts_ref, hidden_ref, scale_ref, out_ref, *spread):
    total = parts_ref[0].astype(jnp.float32)
    for k in range(1, parts_ref.shape[0]):
        total = total + parts_ref[k].astype(jnp.float32)
    total = jnp.concatenate([total[i : i + 1] for i in range(FOLD)], axis=1)
    total = total.astype(jnp.bfloat16).astype(jnp.float32)
    before = hidden_ref[...].astype(jnp.float32)
    hidden = (before + total).astype(jnp.bfloat16).astype(jnp.float32)
    if last:
        out_ref[...] = jnp.concatenate([before, hidden], axis=0).astype(jnp.bfloat16)
    else:
        out_ref[...] = hidden.astype(jnp.bfloat16)
        folded(spread[0], normalized(hidden, scale_ref[...].astype(jnp.float32)).astype(jnp.float32))


def shards(
    hidden_state_input,
    attention_norm_scale,
    query_weight,
    key_value_weight,
    output_weight,
    adapter_down_weight,
    adapter_up_weight,
    row_adapter_index,
    adapter_storage_index,
    cache_length_per_row,
    key_value_cache,
):
    count = lax.axis_size(AXIS)
    chips = count // CORES
    far, near = split_of(count)
    far_steps = [k * near for k in range(1, far)]
    near_steps = list(range(1, near))
    kept, width, rank = adapter_down_weight.shape
    columns = query_weight.shape[1]
    fresh_columns = key_value_weight.shape[1]
    line = min(HD, columns)
    smem, vmem = pltpu.SMEM, pltpu.VMEM
    me = lax.axis_index(AXIS).astype(jnp.int32).reshape(1)
    down = adapter_down_weight.transpose(0, 2, 1)
    scale = attention_norm_scale[None]
    storage = adapter_storage_index[None]

    def stash(token, arrays, limit):
        outs = call(
            functools.partial(stash_kernel, len(arrays)),
            [pltpu.VMEM(a.shape, a.dtype) for a in arrays] + [shape((8, LANES), jnp.float32)],
            "stash",
            [pltpu.SemaphoreType.DMA((len(arrays),))],
            vmem=limit,
            moved=sum(2 * a.size for a in arrays),
        )(token, *arrays, specs=[vmem] + [pl.ANY] * len(arrays))
        return outs[:-1], outs[-1]

    hidden = hidden_state_input
    carried, length = call(
        first_kernel, [shape((1, width + LANES)), shape((8, LANES), jnp.int32)], "first"
    )(hidden, scale, row_adapter_index, cache_length_per_row, specs=[vmem, vmem, smem, smem])
    past = ()
    for step in range(STEPS):
        first, last = step == 0, step == STEPS - 1
        outs = [shape((count, width)), shape((count, rank))]
        scratch = [pltpu.VMEM((count, width), jnp.float32)]
        if first:
            token = jnp.zeros((8, LANES), jnp.float32)
            (query_w, output_w, fresh_w, down_w, cache, up_w), token = stash(
                token,
                [query_weight, output_weight, key_value_weight, down, key_value_cache, adapter_up_weight],
                38 << 20,
            )
            pieces = lax.optimization_barrier((*across(carried, far_steps, count), token))
            carried = jnp.concatenate(pieces[:-1], axis=0)
            pieces = across(carried, near_steps, count)
            member, adapter = call(
                functools.partial(member_kernel, near, far, width),
                [shape((count, kept), jnp.int32), shape((count, 1), jnp.int32)],
                "member",
                [pltpu.VMEM((count, LANES), jnp.float32)],
            )(*pieces, me, storage, specs=[vmem] * near + [smem, vmem])
            rows, low = call(
                functools.partial(low_first_kernel, near, far), outs, "low", scratch
            )(*pieces, me, member, down_w, specs=[vmem] * near + [smem, vmem, vmem])
        else:
            own = chips_swap(carried, count)
            rows, low = call(low_later_kernel, outs, "low", scratch)(
                own, shift(own, 1, count), me, member, down_w, specs=[vmem, vmem, smem, vmem, vmem]
            )
        (low,) = call(sum_kernel, [shape((count, rank))], "sum")(*across(low, near_steps, count))
        lows = across(low, far_steps, count)
        query, fresh = call(
            project_kernel,
            [shape((count, columns), jnp.float32), shape((count, fresh_columns), jnp.float32)],
            "project",
            flops=2 * count * width * (columns + fresh_columns),
            moved=2 * width * (columns + fresh_columns),
        )(rows, query_w, fresh_w)
        (lines,) = call(
            functools.partial(up_kernel, far),
            [shape((count, 8, line))],
            "up",
            [pltpu.VMEM((count, 8, line), jnp.float32)],
        )(*lows, query, fresh, adapter, up_w)

        lines = swap(lines)
        outs = [shape((count, columns // line, line))]
        if first:
            outs = outs + [shape((H, HD), jnp.float32)] * 2
        outs = call(
            functools.partial(attend_kernel, columns, fresh_columns, first),
            outs,
            "attend",
            [
                pltpu.VMEM((count, 8, line), jnp.float32),
                pltpu.VMEM((H, key_value_cache.shape[2]), jnp.float32),
            ],
            moved=2 << 20,
        )(
            lines,
            length,
            cache,
            *past,
            specs=[vmem] * (3 + len(past)),
        )
        if first:
            past = tuple(outs[1:])

        lines = swap(outs[0])
        own, away = call(
            output_kernel,
            [shape((chips, width), jnp.float32), shape((chips, width))],
            "output",
            [pltpu.VMEM((count, 8, line), jnp.float32)],
            flops=2 * count * width * columns,
            moved=2 * width * columns,
        )(lines, me, output_w, specs=[vmem, smem, vmem])

        (parts,) = call(partial_kernel, [shape((chips, FOLD, width // FOLD))], "partial")(
            own, shift(away, 1, count)
        )
        parts = chips_swap(parts, count)
        outs = [shape((2 if last else 1, width))]
        if not last:
            outs = outs + [shape((chips, FOLD, width // FOLD))]
        outs = call(functools.partial(finish_kernel, last), outs, "finish")(parts, hidden, scale)
        if last:
            return outs[0].reshape(STEPS, 1, width)
        hidden, carried = outs


def solution(mesh):
    in_specs = (
        P(("groups", "replica"), None),
        P(),
        P(None, "replica"),
        P(None, "replica"),
        P("replica", None),
        P("replica", None, None),
        P(None, None, "replica"),
        P(("groups", "replica")),
        P(),
        P(("groups", "replica")),
        P(("groups", "replica"), None, None, None),
    )
    out_specs = P(None, ("groups", "replica"), None)
    return jax.shard_map(shards, mesh=mesh, in_specs=in_specs, out_specs=out_specs, check_vma=False)
```

```python
import functools
import math

import jax
import jax.numpy as jnp
from jax import lax
from jax.experimental import pallas as pl
from jax.experimental.pallas import tpu as pltpu
from jax.sharding import PartitionSpec as P

H = 64
KVH = 8
HD = 128
STEPS = 2
GROUP = H // KVH
EPS = 1e-05
AXIS = "replica"
LANES = 128
LAST = (((1,), (1,)), ((), ()))
FIRST = (((0,), (0,)), ((), ()))

CORES = 2
FOLD = 8


def split_of(count):
    far = 1 << (count.bit_length() // 2)
    return far, count // far


def shift(block, distance, count):
    return lax.ppermute(block, AXIS, [(i, i ^ distance) for i in range(count)])


def across(block, strides, count):
    return [block] + [shift(block, d, count) for d in strides]


def swap(blocks):
    return lax.all_to_all(blocks, AXIS, split_axis=0, concat_axis=0, tiled=True)


def chips_swap(blocks, count):
    groups = [[i for i in range(count) if i % CORES == c] for c in range(CORES)]
    return lax.all_to_all(
        blocks, AXIS, split_axis=0, concat_axis=0, axis_index_groups=groups, tiled=True
    )


def kernel(body, outs, name, scratch=(), vmem=20 << 20, flops=1 << 20, moved=1 << 18):
    def run(*operands, specs=None):
        specs = specs or [pltpu.VMEM] * len(operands)
        return pl.pallas_call(
            body,
            out_shape=outs,
            in_specs=[pl.BlockSpec(memory_space=s) for s in specs],
            out_specs=[pl.BlockSpec(memory_space=pltpu.VMEM)] * len(outs),
            scratch_shapes=list(scratch),
            compiler_params=pltpu.CompilerParams(vmem_limit_bytes=vmem),
            cost_estimate=pl.CostEstimate(flops=flops, bytes_accessed=moved, transcendentals=0),
            name=name,
        )(*operands)

    return run


def shape(dims, dtype=jnp.bfloat16):
    return jax.ShapeDtypeStruct(dims, dtype)


def iota(dims, axis):
    return lax.broadcasted_iota(jnp.int32, dims, axis)


def dot(a, b, contract=(((1,), (0,)), ((), ()))):
    return lax.dot_general(a, b, contract, preferred_element_type=jnp.float32)


def normalized(hidden, scale):
    factor = lax.rsqrt(jnp.mean(hidden * hidden, axis=-1, keepdims=True) + EPS)
    return (hidden * factor * scale).astype(jnp.bfloat16)


def folded(out_ref, row):
    wide = row.shape[1] // FOLD
    for k in range(out_ref.shape[0]):
        for i in range(FOLD):
            out_ref[k, i : i + 1, :wide] = row[:, i * wide : (i + 1) * wide].astype(out_ref.dtype)


def first_kernel(hidden_ref, scale_ref, adapter_ref, length_ref, out_ref, length_out):
    length_out[...] = jnp.full(length_out.shape, length_ref[0], jnp.int32)
    width = hidden_ref.shape[1]
    hidden = hidden_ref[...].astype(jnp.float32)
    out_ref[:, :width] = normalized(hidden, scale_ref[...].astype(jnp.float32))
    digit = iota((1, LANES), 1)
    adapter = adapter_ref[0]
    length = length_ref[0]
    digits = jnp.where(digit == 0, adapter % 256, jnp.where(digit == 1, adapter // 256, 0))
    digits = jnp.where(digit == 2, length % 256, jnp.where(digit == 3, length // 256, digits))
    digits = digits.astype(jnp.float32)
    out_ref[:, width:] = digits.astype(jnp.bfloat16)


def stash_kernel(amount, token_ref, *refs):
    sources, refs = refs[:amount], refs[amount:]
    outs, out_token, sems = refs[:amount], refs[amount], refs[-1]
    copies = [
        pltpu.make_async_copy(sources[i], outs[i], sems.at[i]) for i in range(amount)
    ]
    for copy in copies:
        copy.start()
    out_token[...] = token_ref[...] * 0.0
    for copy in copies:
        copy.wait()


def member_kernel(near, far, width, *refs):
    pieces = refs[:near]
    me_ref, storage_ref = refs[near : near + 2]
    member_ref, adapter_ref, lengths_ref, held = refs[-4:]
    kept = member_ref.shape[1]
    count = near * far
    me = me_ref[0]
    for l in range(near):
        digits = pieces[l][:, width:].astype(jnp.float32)
        for k in range(far):
            held[pl.ds(me ^ (k * near + l), 1), :] = digits[k : k + 1]
    adapter = (held[:, 0:1] + 256.0 * held[:, 1:2]).astype(jnp.int32)
    adapter_ref[...] = adapter
    lengths_ref[...] = (held[:, 2:3] + 256.0 * held[:, 3:4]).astype(jnp.int32)
    table = storage_ref.shape[1]
    chosen = jnp.where(iota((count, table), 1) == adapter, storage_ref[...], 0)
    storage = jnp.sum(chosen.astype(jnp.float32), axis=1, keepdims=True).astype(jnp.int32)
    member_ref[...] = (storage - me * kept == iota((count, kept), 1)).astype(jnp.int32)


def low_terms(held, member_ref, down_ref, fresh_w, rows_ref, low_ref, fresh_ref):
    rows = held[...].astype(jnp.bfloat16)
    rows_ref[...] = rows
    low = jnp.zeros(low_ref.shape, jnp.float32)
    for index in range(down_ref.shape[0]):
        part = dot(rows, down_ref[index], LAST)
        low = jnp.where(member_ref[:, index : index + 1] > 0, part, low)
    low_ref[...] = low.astype(jnp.bfloat16)
    fresh_ref[...] = dot(rows, fresh_w[...]).astype(jnp.bfloat16)


def low_first_kernel(near, far, *refs):
    pieces = refs[:near]
    me_ref, member_ref, down_ref, fresh_w = refs[near : near + 4]
    rows_ref, low_ref, fresh_ref, held = refs[-4:]
    width = held.shape[1]
    for l in range(near):
        block = pieces[l][:, :width].astype(jnp.float32)
        for k in range(far):
            held[pl.ds(me_ref[0] ^ (k * near + l), 1), :] = block[k : k + 1]
    low_terms(held, member_ref, down_ref, fresh_w, rows_ref, low_ref, fresh_ref)


def low_later_kernel(own_ref, other_ref, me_ref, member_ref, down_ref, fresh_w, *refs):
    rows_ref, low_ref, fresh_ref, held = refs
    core = me_ref[0] % CORES
    for ref, flip in ((own_ref, 0), (other_ref, 1)):
        wide = ref.shape[2]
        for k in range(ref.shape[0]):
            block = ref[k].astype(jnp.float32)
            row = pl.ds(k * CORES + (core ^ flip), 1)
            for i in range(FOLD):
                held[row, i * wide : (i + 1) * wide] = block[i : i + 1]
    low_terms(held, member_ref, down_ref, fresh_w, rows_ref, low_ref, fresh_ref)


def join_kernel(amount, *refs):
    rows = [ref[...].astype(jnp.float32) for ref in refs[:amount]]
    refs[-1][...] = jnp.concatenate(rows, axis=0).astype(refs[-1].dtype)


def sum_kernel(amount, *refs):
    total = refs[0][...].astype(jnp.float32)
    for ref in refs[1:amount]:
        total = total + ref[...].astype(jnp.float32)
    refs[-1][...] = total.astype(refs[-1].dtype)


def project_kernel(rows_ref, query_w, *refs):
    query_ref = refs[-1]
    query_ref[...] = dot(rows_ref[...], query_w[...])


def up_terms(lows, query_ref, adapter_ref, up_ref):
    count, columns = query_ref.shape
    rank = lows[0].shape[1]
    low = lows[0][...].astype(jnp.float32)
    for ref in lows[1:]:
        low = low + ref[...].astype(jnp.float32)
    low = low.astype(jnp.bfloat16)
    query = query_ref[...]
    table = up_ref.shape[0]
    some = min(table, 32)
    wide = some * rank
    repeat = (iota((rank, wide), 1) % rank == iota((rank, wide), 0)).astype(jnp.bfloat16)
    wide_low = dot(low, repeat)
    place = iota((count, wide), 1) // rank
    for start in range(0, table, some):
        spread = jnp.where(place + start == adapter_ref[...], wide_low, 0.0).astype(jnp.bfloat16)
        query = query + dot(spread, up_ref[start : start + some].reshape(wide, columns))
    return query


def up_kernel(parts, *refs):
    lows, (query_ref, fresh_ref, adapter_ref, up_ref, out_ref, held) = refs[:parts], refs[parts:]
    count, columns = query_ref.shape
    query = up_terms(lows, query_ref, adapter_ref, up_ref)
    line = out_ref.shape[2]
    lines = columns // line
    held[...] = jnp.zeros(held.shape, jnp.float32)
    for c in range(lines):
        held[:, c, :] = query[:, c * line : (c + 1) * line]
    fresh = fresh_ref[...].astype(jnp.float32)
    if fresh.shape[1] < line:
        fresh = jnp.concatenate(
            [fresh, jnp.zeros((count, line - fresh.shape[1]), jnp.float32)], axis=1
        )
    held[:, lines, :] = fresh
    for k in range(count):
        out_ref[k] = held[k].astype(jnp.bfloat16)


def pieces_of(lines, select, whole, size):
    if size >= whole:
        total = dot(select(len(lines), 0), lines[0])
        for c in range(1, len(lines)):
            total = total + dot(select(len(lines), c), lines[c])
        return total
    return jnp.concatenate([dot(select(0, p), lines[0]) for p in range(whole // size)], axis=1)


def attend_kernel(columns, fresh_columns, first, *refs):
    lines_ref, length_ref, cache_ref = refs[:3]
    refs = refs[3:]
    if not first:
        past, refs = refs[:2], refs[2:]
    out_ref, refs = refs[0], refs[1:]
    if first:
        keep, refs = refs[:2], refs[2:]
    held, scores = refs
    count, _, line = lines_ref.shape
    cache = cache_ref.shape[2]
    for k in range(count):
        held[k] = lines_ref[k].astype(jnp.float32)
    each = columns // line
    lines = [held[:, c, :].astype(jnp.bfloat16) for c in range(each + 1)]
    origin = iota((H, count), 1)
    head = iota((H, count), 0)

    def query_pick(each, c):
        if each:
            return (head == origin * each + c).astype(jnp.bfloat16)
        return (head * (HD // columns) + c == origin).astype(jnp.bfloat16)

    def fresh_pick(offset):
        def pick(each, c):
            want = head // GROUP + offset
            if each:
                return (want == origin * each + c).astype(jnp.bfloat16)
            return (want * (HD // fresh_columns) + c == origin).astype(jnp.bfloat16)

        return pick

    query = pieces_of(lines[:each], query_pick, HD, columns)
    fresh = [lines[each][:, :fresh_columns]]
    new = [
        (
            pieces_of(fresh, fresh_pick(0), HD, fresh_columns),
            pieces_of(fresh, fresh_pick(KVH), HD, fresh_columns),
        )
    ]
    if first:
        keep[0][...], keep[1][...] = new[0]
    else:
        new.insert(0, (past[0][...], past[1][...]))
    scale = 1.0 / math.sqrt(HD)
    for j in range(KVH):
        rows = slice(j * GROUP, (j + 1) * GROUP)
        scores[rows, :] = dot(
            query[rows].astype(jnp.bfloat16), cache_ref[0, 0, :, j * HD : (j + 1) * HD], LAST
        )
    in_cache = iota((H, cache), 1) < length_ref[0:1, 0:1]
    old = jnp.where(in_cache, scores[...] * scale, -jnp.inf)
    news = [jnp.sum(query * keys, axis=1, keepdims=True) * scale for keys, _ in new]
    peak = jnp.max(old, axis=1, keepdims=True)
    for score in news:
        peak = jnp.maximum(peak, score)
    old = jnp.exp(old - peak)
    news = [jnp.exp(score - peak) for score in news]
    total = jnp.sum(old, axis=1, keepdims=True)
    for score in news:
        total = total + score
    old = old / total
    extra = jnp.zeros((H, HD), jnp.float32)
    for score, (_, values) in zip(news, new):
        extra = extra + (score / total).astype(jnp.bfloat16).astype(jnp.float32) * values
    mixed = jnp.concatenate(
        [
            dot(
                old[j * GROUP : (j + 1) * GROUP].astype(jnp.bfloat16),
                cache_ref[0, 1, :, j * HD : (j + 1) * HD],
            )
            for j in range(KVH)
        ],
        axis=0,
    )
    mixed = mixed + extra
    if columns >= HD:
        for k in range(count):
            out_ref[k] = mixed[k * each : (k + 1) * each].astype(jnp.bfloat16)
    else:
        parts = HD // columns
        out = jnp.zeros((count, columns), jnp.float32)
        for p in range(parts):
            pick = (iota((count, H), 1) * parts + p == iota((count, H), 0)).astype(jnp.bfloat16)
            out = out + dot(pick, mixed[:, p * columns : (p + 1) * columns].astype(jnp.bfloat16))
        for k in range(count):
            out_ref[k] = out[k : k + 1].astype(jnp.bfloat16)


def output_terms(held, each, core, weight_ref, own_ref, away_ref):
    count = held.shape[0]
    chips = count // CORES
    slot = iota((count, count), 0)
    origin = (slot % chips) * CORES + (core ^ (slot // chips))
    order = (iota((count, count), 1) == origin).astype(jnp.bfloat16)
    rows = jnp.concatenate(
        [dot(order, held[:, c, :].astype(jnp.bfloat16)).astype(jnp.bfloat16) for c in range(each)],
        axis=1,
    )
    width = weight_ref.shape[1]
    wide = width // 8
    for c in range(8):
        part = slice(c * wide, (c + 1) * wide)
        out = dot(rows, weight_ref[:, part])
        own_ref[:, part] = out[:chips]
        away_ref[:, part] = out[chips:].astype(jnp.bfloat16)


def output_kernel(lines_ref, me_ref, weight_ref, own_ref, away_ref, held):
    count, each, line = lines_ref.shape
    for k in range(count):
        held[k, :each, :] = lines_ref[k].astype(jnp.float32)
    output_terms(held, each, me_ref[0] % CORES, weight_ref, own_ref, away_ref)


def cut_kernel(me_ref, cache_hbm, *refs):
    outs, sems = refs[:-1], refs[-1]
    copies = []
    for d, out in enumerate(outs):
        lanes = pl.ds(pl.multiple_of(((me_ref[0] // CORES) ^ d) * HD, HD), HD)
        copies.append(pltpu.make_async_copy(cache_hbm.at[0, :, :, lanes], out, sems.at[d]))
    for copy in copies:
        copy.start()
    for copy in copies:
        copy.wait()


def heads_kernel(parts, steps, *refs):
    lows, refs = refs[:parts], refs[parts:]
    query_ref, adapter_ref, up_ref, lengths_ref, me_ref, weight_ref = refs[:6]
    news, refs = refs[6 : 6 + 2 * steps], refs[6 + 2 * steps :]
    own_ref, away_ref, held, mixed_ref, new_ref = refs[-5:]
    blocks = refs[:-5]
    count, columns = query_ref.shape
    chips = count // CORES
    each = columns // HD
    lines = held.shape[1]
    chip, core = me_ref[0] // CORES, me_ref[0] % CORES
    query = up_terms(lows, query_ref, adapter_ref, up_ref).astype(jnp.bfloat16)
    held[...] = jnp.zeros(held.shape, jnp.float32)
    for c in range(each):
        held[:, c, :] = query[:, c * HD : (c + 1) * HD].astype(jnp.float32)
    for t in range(steps):
        mine, other = news[2 * t][...].astype(jnp.float32), news[2 * t + 1][...].astype(jnp.float32)
        new_ref[2 * t] = jnp.where(core == 0, mine, other)
        new_ref[2 * t + 1] = jnp.where(core == 0, other, mine)
    scale = 1.0 / math.sqrt(HD)
    rows = [((chip ^ (b % chips)) * CORES) + (core ^ (b // chips)) for b in range(count)]
    old, fresh = [], [[] for _ in range(steps)]
    for row, block in zip(rows, blocks):
        query = held[row]
        score = dot(query.astype(jnp.bfloat16), block[0], LAST) * scale
        length = lengths_ref[pl.ds(row, 1), :]
        old.append(jnp.where(iota(score.shape, 1) < length, score, -jnp.inf))
        for t in range(steps):
            keys = new_ref[2 * t, pl.ds(row, 1), :]
            fresh[t].append(jnp.sum(query * keys, axis=1, keepdims=True) * scale)
    old = jnp.concatenate(old, axis=0)
    fresh = [jnp.concatenate(scores, axis=0) for scores in fresh]
    peak = jnp.max(old, axis=1, keepdims=True)
    for scores in fresh:
        peak = jnp.maximum(peak, scores)
    old = jnp.exp(old - peak)
    fresh = [jnp.exp(scores - peak) for scores in fresh]
    total = jnp.sum(old, axis=1, keepdims=True)
    for scores in fresh:
        total = total + scores
    old = (old / total).astype(jnp.bfloat16).astype(jnp.float32)
    fresh = [(scores / total).astype(jnp.bfloat16).astype(jnp.float32) for scores in fresh]
    for b, (row, block) in enumerate(zip(rows, blocks)):
        part = slice(b * lines, (b + 1) * lines)
        mixed = dot(old[part].astype(jnp.bfloat16), block[1])
        for t in range(steps):
            mixed = mixed + fresh[t][part] * new_ref[2 * t + 1, pl.ds(row, 1), :]
        mixed_ref[row] = mixed
    output_terms(mixed_ref, each, core, weight_ref, own_ref, away_ref)


def partial_kernel(own_ref, other_ref, out_ref):
    total = own_ref[...] + other_ref[...].astype(jnp.float32)
    wide = out_ref.shape[2]
    for k in range(out_ref.shape[0]):
        for i in range(FOLD):
            out_ref[k, i : i + 1, :] = total[k : k + 1, i * wide : (i + 1) * wide].astype(
                out_ref.dtype
            )


def finish_kernel(last, parts_ref, hidden_ref, scale_ref, out_ref, *spread):
    total = parts_ref[0].astype(jnp.float32)
    for k in range(1, parts_ref.shape[0]):
        total = total + parts_ref[k].astype(jnp.float32)
    total = jnp.concatenate([total[i : i + 1] for i in range(FOLD)], axis=1)
    total = total.astype(jnp.bfloat16).astype(jnp.float32)
    before = hidden_ref[...].astype(jnp.float32)
    hidden = (before + total).astype(jnp.bfloat16).astype(jnp.float32)
    if last:
        out_ref[...] = jnp.concatenate([before, hidden], axis=0).astype(jnp.bfloat16)
    else:
        out_ref[...] = hidden.astype(jnp.bfloat16)
        folded(spread[0], normalized(hidden, scale_ref[...].astype(jnp.float32)).astype(jnp.float32))


def shards(
    hidden_state_input,
    attention_norm_scale,
    query_weight,
    key_value_weight,
    output_weight,
    adapter_down_weight,
    adapter_up_weight,
    row_adapter_index,
    adapter_storage_index,
    cache_length_per_row,
    key_value_cache,
):
    count = lax.axis_size(AXIS)
    chips = count // CORES
    far, near = split_of(count)
    far_steps = [k * near for k in range(1, far)]
    near_steps = list(range(1, near))
    kept, width, rank = adapter_down_weight.shape
    columns = query_weight.shape[1]
    fresh_columns = key_value_weight.shape[1]
    line = min(HD, columns)
    smem, vmem = pltpu.SMEM, pltpu.VMEM
    call = functools.partial(kernel, vmem=min(20 << 20, (count * 3 // 4) << 20))
    me = lax.axis_index(AXIS).astype(jnp.int32).reshape(1)
    down = adapter_down_weight.transpose(0, 2, 1)
    scale = attention_norm_scale[None]
    storage = adapter_storage_index[None]

    def stash(token, arrays, limit):
        outs = call(
            functools.partial(stash_kernel, len(arrays)),
            [pltpu.VMEM(a.shape, a.dtype) for a in arrays] + [shape((8, LANES), jnp.float32)],
            "stash",
            [pltpu.SemaphoreType.DMA((len(arrays),))],
            vmem=limit,
            moved=sum(2 * a.size for a in arrays),
        )(token, *arrays, specs=[vmem] + [pl.ANY] * len(arrays))
        return outs[:-1], outs[-1]

    past, held_cache, moved = [], [], []

    def after(*distances):
        return [moved[d - 1] for d in distances] if moved else []


    def by_rows(step, lows, query, fresh):
        first = step == 0
        (lines,) = call(
            functools.partial(up_kernel, far),
            [shape((count, 8, line))],
            "up",
            [pltpu.VMEM((count, 8, line), jnp.float32)],
        )(*lows, query, fresh, adapter, up_w)

        lines = swap(lines)
        outs = [shape((count, columns // line, line))]
        if first:
            outs = outs + [shape((H, HD), jnp.float32)] * 2
        outs = call(
            functools.partial(attend_kernel, columns, fresh_columns, first),
            outs,
            "attend",
            [
                pltpu.VMEM((count, 8, line), jnp.float32),
                pltpu.VMEM((H, key_value_cache.shape[2]), jnp.float32),
            ],
            moved=2 << 20,
        )(
            lines,
            length,
            held_cache[0],
            *past,
            specs=[vmem] * (3 + len(past)),
        )
        if first:
            past.extend(outs[1:])

        lines = swap(outs[0])
        own, away = call(
            output_kernel,
            [shape((chips, width), jnp.float32), shape((chips, width))],
            "output",
            [pltpu.VMEM((count, 8, line), jnp.float32)],
            flops=2 * count * width * columns,
            moved=2 * width * columns,
        )(lines, me, output_w, specs=[vmem, smem, vmem])
        return own, away

    hidden = hidden_state_input
    carried, length = call(
        first_kernel, [shape((1, width + LANES)), shape((8, LANES), jnp.int32)], "first"
    )(hidden, scale, row_adapter_index, cache_length_per_row, specs=[vmem, vmem, smem, smem])
    news, blocks = [], []
    by_heads = columns * CORES == GROUP * HD and count == CORES * KVH
    for step in range(STEPS):
        first, last = step == 0, step == STEPS - 1
        low_outs = [shape((count, width)), shape((count, rank)), shape((count, fresh_columns))]
        scratch = [pltpu.VMEM((count, width), jnp.float32)]
        if first:
            token = jnp.zeros((8, LANES), jnp.float32)
            arrays = [query_weight, output_weight, key_value_weight, down, adapter_up_weight]
            if by_heads:
                blocks = call(
                    cut_kernel,
                    [shape((2, key_value_cache.shape[2], HD))] * chips,
                    "cut",
                    [pltpu.SemaphoreType.DMA((chips,))],
                )(me, key_value_cache, specs=[smem, pl.ANY])
                moved.extend(shift(b, CORES * d, count) for d, b in enumerate(blocks) if d)
                blocks = [blocks[0]] + moved
                blocks = blocks + [shift(b, 1, count) for b in blocks]
            else:
                arrays.append(key_value_cache)
            outs, token = stash(token, arrays, 30 << 20)
            query_w, output_w, fresh_w, down_w, up_w = outs[:5]
            held_cache.append(outs[-1])
            pieces = across(carried, far_steps, count)
            (carried,) = call(
                functools.partial(join_kernel, far), [shape((far, width + LANES))], "join"
            )(*pieces, *after(1, 2), specs=[vmem] * far + [pl.ANY] * len(after(1, 2)))
            pieces = across(carried, near_steps, count)
            member, adapter, lengths = call(
                functools.partial(member_kernel, near, far, width),
                [shape((count, kept), jnp.int32)] + [shape((count, 1), jnp.int32)] * 2,
                "member",
                [pltpu.VMEM((count, LANES), jnp.float32)],
            )(
                *pieces,
                me,
                storage,
                *after(4, 6),
                specs=[vmem] * near + [smem, vmem] + [pl.ANY] * len(after(4, 6)),
            )
            rows, low, fresh = call(
                functools.partial(low_first_kernel, near, far), low_outs, "low", scratch
            )(
                *pieces,
                me,
                member,
                down_w,
                fresh_w,
                specs=[vmem] * near + [smem] + [vmem] * 3,
            )
        else:
            own = chips_swap(carried, count)
            rows, low, fresh = call(low_later_kernel, low_outs, "low", scratch)(
                own,
                shift(own, 1, count),
                me,
                member,
                down_w,
                fresh_w,
                specs=[vmem, vmem, smem, vmem, vmem, vmem],
            )
        behind = after(5) if first else []
        (low,) = call(functools.partial(sum_kernel, near), [shape((count, rank))], "sum")(
            *across(low, near_steps, count),
            *behind,
            specs=[vmem] * near + [pl.ANY] * len(behind),
        )
        lows = across(low, far_steps, count)
        behind = after(3) if first else []
        (query,) = call(
            project_kernel,
            [shape((count, columns), jnp.float32)],
            "project",
            flops=2 * count * width * columns,
            moved=2 * width * columns,
        )(rows, query_w, *behind, specs=[vmem] * 2 + [pl.ANY] * len(behind))
        if by_heads:
            fresh = lax.ppermute(fresh, AXIS, [(i, 2 * (i % KVH) + i // KVH) for i in range(count)])
            news = news + [fresh, shift(fresh, 1, count)]
            own, away = call(
                functools.partial(heads_kernel, far, step + 1),
                [shape((chips, width), jnp.float32), shape((chips, width))],
                "heads",
                [pltpu.VMEM((count, 8, HD), jnp.float32)] * 2
                + [pltpu.VMEM((2 * (step + 1), count, HD), jnp.float32)],
                flops=2 * count * width * columns,
                moved=2 * width * columns,
            )(
                *lows,
                query,
                adapter,
                up_w,
                lengths,
                me,
                output_w,
                *news,
                *blocks,
                specs=[vmem] * (far + 4) + [smem] + [vmem] * (1 + len(news) + len(blocks)),
            )
        else:
            own, away = by_rows(step, lows, query, fresh)

        (parts,) = call(partial_kernel, [shape((chips, FOLD, width // FOLD))], "partial")(
            own, shift(away, 1, count)
        )
        parts = chips_swap(parts, count)
        outs = [shape((2 if last else 1, width))]
        if not last:
            outs = outs + [shape((chips, FOLD, width // FOLD))]
        outs = call(functools.partial(finish_kernel, last), outs, "finish")(parts, hidden, scale)
        if last:
            return outs[0].reshape(STEPS, 1, width)
        hidden, carried = outs


def solution(mesh):
    in_specs = (
        P(("groups", "replica"), None),
        P(),
        P(None, "replica"),
        P(None, "replica"),
        P("replica", None),
        P("replica", None, None),
        P(None, None, "replica"),
        P(("groups", "replica")),
        P(),
        P(("groups", "replica")),
        P(("groups", "replica"), None, None, None),
    )
    out_specs = P(None, ("groups", "replica"), None)
    return jax.shard_map(shards, mesh=mesh, in_specs=in_specs, out_specs=out_specs, check_vma=False)
```

```python
import functools
import math

import jax
import jax.numpy as jnp
from jax import lax
from jax.experimental import pallas as pl
from jax.experimental.pallas import tpu as pltpu
from jax.sharding import PartitionSpec as P

H = 64
KVH = 8
HD = 128
STEPS = 2
GROUP = H // KVH
EPS = 1e-05
AXIS = "replica"
LANES = 128
LAST = (((1,), (1,)), ((), ()))
FIRST = (((0,), (0,)), ((), ()))

CORES = 2
FOLD = 8


def split_of(count):
    far = 1 << (count.bit_length() // 2)
    return far, count // far


def shift(block, distance, count):
    return lax.ppermute(block, AXIS, [(i, i ^ distance) for i in range(count)])


def across(block, strides, count):
    return [block] + [shift(block, d, count) for d in strides]


def swap(blocks):
    return lax.all_to_all(blocks, AXIS, split_axis=0, concat_axis=0, tiled=True)


def chips_swap(blocks, count):
    groups = [[i for i in range(count) if i % CORES == c] for c in range(CORES)]
    return lax.all_to_all(
        blocks, AXIS, split_axis=0, concat_axis=0, axis_index_groups=groups, tiled=True
    )


def kernel(body, outs, name, scratch=(), vmem=20 << 20, flops=1 << 20, moved=1 << 18):
    def run(*operands, specs=None):
        specs = specs or [pltpu.VMEM] * len(operands)
        return pl.pallas_call(
            body,
            out_shape=outs,
            in_specs=[pl.BlockSpec(memory_space=s) for s in specs],
            out_specs=[pl.BlockSpec(memory_space=pltpu.VMEM)] * len(outs),
            scratch_shapes=list(scratch),
            compiler_params=pltpu.CompilerParams(vmem_limit_bytes=vmem),
            cost_estimate=pl.CostEstimate(flops=flops, bytes_accessed=moved, transcendentals=0),
            name=name,
        )(*operands)

    return run


def shape(dims, dtype=jnp.bfloat16):
    return jax.ShapeDtypeStruct(dims, dtype)


def iota(dims, axis):
    return lax.broadcasted_iota(jnp.int32, dims, axis)


def dot(a, b, contract=(((1,), (0,)), ((), ()))):
    return lax.dot_general(a, b, contract, preferred_element_type=jnp.float32)


def normalized(hidden, scale):
    factor = lax.rsqrt(jnp.mean(hidden * hidden, axis=-1, keepdims=True) + EPS)
    return (hidden * factor * scale).astype(jnp.bfloat16)


def folded(out_ref, row):
    wide = row.shape[1] // FOLD
    for k in range(out_ref.shape[0]):
        for i in range(FOLD):
            out_ref[k, i : i + 1, :wide] = row[:, i * wide : (i + 1) * wide].astype(out_ref.dtype)


def first_kernel(hidden_ref, scale_ref, adapter_ref, length_ref, out_ref, length_out):
    length_out[...] = jnp.full(length_out.shape, length_ref[0], jnp.int32)
    width = hidden_ref.shape[1]
    hidden = hidden_ref[...].astype(jnp.float32)
    out_ref[:, :width] = normalized(hidden, scale_ref[...].astype(jnp.float32))
    digit = iota((1, LANES), 1)
    adapter = adapter_ref[0]
    length = length_ref[0]
    digits = jnp.where(digit == 0, adapter % 256, jnp.where(digit == 1, adapter // 256, 0))
    digits = jnp.where(digit == 2, length % 256, jnp.where(digit == 3, length // 256, digits))
    digits = digits.astype(jnp.float32)
    out_ref[:, width:] = digits.astype(jnp.bfloat16)


def stash_kernel(amount, token_ref, *refs):
    sources, refs = refs[:amount], refs[amount:]
    outs, out_token, sems = refs[:amount], refs[amount], refs[-1]
    copies = [
        pltpu.make_async_copy(sources[i], outs[i], sems.at[i]) for i in range(amount)
    ]
    for copy in copies:
        copy.start()
    out_token[...] = token_ref[...] * 0.0
    for copy in copies:
        copy.wait()


def member_kernel(near, far, width, *refs):
    pieces = refs[:near]
    me_ref, storage_ref = refs[near : near + 2]
    member_ref, adapter_ref, lengths_ref, held = refs[-4:]
    kept = member_ref.shape[1]
    count = near * far
    me = me_ref[0]
    for l in range(near):
        digits = pieces[l][:, width:].astype(jnp.float32)
        for k in range(far):
            held[pl.ds(me ^ (k * near + l), 1), :] = digits[k : k + 1]
    adapter = (held[:, 0:1] + 256.0 * held[:, 1:2]).astype(jnp.int32)
    adapter_ref[...] = adapter
    lengths_ref[...] = (held[:, 2:3] + 256.0 * held[:, 3:4]).astype(jnp.int32)
    table = storage_ref.shape[1]
    chosen = jnp.where(iota((count, table), 1) == adapter, storage_ref[...], 0)
    storage = jnp.sum(chosen.astype(jnp.float32), axis=1, keepdims=True).astype(jnp.int32)
    member_ref[...] = (storage - me * kept == iota((count, kept), 1)).astype(jnp.int32)


def low_terms(held, member_ref, down_ref, fresh_w, rows_ref, *outs):
    rows = held[...].astype(jnp.bfloat16)
    rows_ref[...] = rows
    rank = down_ref.shape[1]
    low = jnp.zeros((rows.shape[0], rank), jnp.float32)
    for index in range(down_ref.shape[0]):
        part = dot(rows, down_ref[index], LAST)
        low = jnp.where(member_ref[:, index : index + 1] > 0, part, low)
    fresh = dot(rows, fresh_w[...]).astype(jnp.bfloat16)
    if len(outs) == 2:
        outs[0][...] = low.astype(jnp.bfloat16)
        outs[1][...] = fresh
    else:
        outs[0][:, :rank] = low.astype(jnp.bfloat16)
        outs[0][:, rank:LANES] = jnp.zeros((rows.shape[0], LANES - rank), jnp.bfloat16)
        outs[0][:, LANES:] = fresh


def low_first_kernel(near, far, *refs):
    pieces = refs[:near]
    me_ref, member_ref, down_ref, fresh_w = refs[near : near + 4]
    outs, held = refs[near + 4 : -1], refs[-1]
    width = held.shape[1]
    for l in range(near):
        block = pieces[l][:, :width].astype(jnp.float32)
        for k in range(far):
            held[pl.ds(me_ref[0] ^ (k * near + l), 1), :] = block[k : k + 1]
    low_terms(held, member_ref, down_ref, fresh_w, *outs)


def low_later_kernel(own_ref, other_ref, me_ref, member_ref, down_ref, fresh_w, *refs):
    outs, held = refs[:-1], refs[-1]
    core = me_ref[0] % CORES
    for ref, flip in ((own_ref, 0), (other_ref, 1)):
        wide = ref.shape[2]
        for k in range(ref.shape[0]):
            block = ref[k].astype(jnp.float32)
            row = pl.ds(k * CORES + (core ^ flip), 1)
            for i in range(FOLD):
                held[row, i * wide : (i + 1) * wide] = block[i : i + 1]
    low_terms(held, member_ref, down_ref, fresh_w, *outs)


def join_kernel(amount, *refs):
    rows = [ref[...].astype(jnp.float32) for ref in refs[:amount]]
    refs[-1][...] = jnp.concatenate(rows, axis=0).astype(refs[-1].dtype)


def sum_kernel(amount, *refs):
    total = refs[0][...].astype(jnp.float32)
    for ref in refs[1:amount]:
        total = total + ref[...].astype(jnp.float32)
    refs[-1][...] = total.astype(refs[-1].dtype)


def project_kernel(rows_ref, query_w, query_ref):
    query_ref[...] = dot(rows_ref[...], query_w[...])


def up_terms(lows, query_ref, adapter_ref, up_ref):
    count, columns = query_ref.shape
    rank = lows[0].shape[1]
    low = functools.reduce(lambda a, b: a + b, lows).astype(jnp.bfloat16)
    query = query_ref[...]
    table = up_ref.shape[0]
    some = min(table, 32)
    wide = some * rank
    repeat = (iota((rank, wide), 1) % rank == iota((rank, wide), 0)).astype(jnp.bfloat16)
    wide_low = dot(low, repeat)
    place = iota((count, wide), 1) // rank
    for start in range(0, table, some):
        spread = jnp.where(place + start == adapter_ref[...], wide_low, 0.0).astype(jnp.bfloat16)
        query = query + dot(spread, up_ref[start : start + some].reshape(wide, columns))
    return query


def up_kernel(parts, *refs):
    lows, (query_ref, fresh_ref, adapter_ref, up_ref, out_ref, held) = refs[:parts], refs[parts:]
    count, columns = query_ref.shape
    lows = [ref[...].astype(jnp.float32) for ref in lows]
    query = up_terms(lows, query_ref, adapter_ref, up_ref)
    line = out_ref.shape[2]
    lines = columns // line
    held[...] = jnp.zeros(held.shape, jnp.float32)
    for c in range(lines):
        held[:, c, :] = query[:, c * line : (c + 1) * line]
    fresh = fresh_ref[...].astype(jnp.float32)
    if fresh.shape[1] < line:
        fresh = jnp.concatenate(
            [fresh, jnp.zeros((count, line - fresh.shape[1]), jnp.float32)], axis=1
        )
    held[:, lines, :] = fresh
    for k in range(count):
        out_ref[k] = held[k].astype(jnp.bfloat16)


def pieces_of(lines, select, whole, size):
    if size >= whole:
        total = dot(select(len(lines), 0), lines[0])
        for c in range(1, len(lines)):
            total = total + dot(select(len(lines), c), lines[c])
        return total
    return jnp.concatenate([dot(select(0, p), lines[0]) for p in range(whole // size)], axis=1)


def attend_kernel(columns, fresh_columns, first, *refs):
    lines_ref, length_ref, cache_ref = refs[:3]
    refs = refs[3:]
    if not first:
        past, refs = refs[:2], refs[2:]
    out_ref, refs = refs[0], refs[1:]
    if first:
        keep, refs = refs[:2], refs[2:]
    held, scores = refs
    count, _, line = lines_ref.shape
    cache = cache_ref.shape[2]
    for k in range(count):
        held[k] = lines_ref[k].astype(jnp.float32)
    each = columns // line
    lines = [held[:, c, :].astype(jnp.bfloat16) for c in range(each + 1)]
    origin = iota((H, count), 1)
    head = iota((H, count), 0)

    def query_pick(each, c):
        if each:
            return (head == origin * each + c).astype(jnp.bfloat16)
        return (head * (HD // columns) + c == origin).astype(jnp.bfloat16)

    def fresh_pick(offset):
        def pick(each, c):
            want = head // GROUP + offset
            if each:
                return (want == origin * each + c).astype(jnp.bfloat16)
            return (want * (HD // fresh_columns) + c == origin).astype(jnp.bfloat16)

        return pick

    query = pieces_of(lines[:each], query_pick, HD, columns)
    fresh = [lines[each][:, :fresh_columns]]
    new = [
        (
            pieces_of(fresh, fresh_pick(0), HD, fresh_columns),
            pieces_of(fresh, fresh_pick(KVH), HD, fresh_columns),
        )
    ]
    if first:
        keep[0][...], keep[1][...] = new[0]
    else:
        new.insert(0, (past[0][...], past[1][...]))
    scale = 1.0 / math.sqrt(HD)
    for j in range(KVH):
        rows = slice(j * GROUP, (j + 1) * GROUP)
        scores[rows, :] = dot(
            query[rows].astype(jnp.bfloat16), cache_ref[0, 0, :, j * HD : (j + 1) * HD], LAST
        )
    in_cache = iota((H, cache), 1) < length_ref[0:1, 0:1]
    old = jnp.where(in_cache, scores[...] * scale, -jnp.inf)
    news = [jnp.sum(query * keys, axis=1, keepdims=True) * scale for keys, _ in new]
    peak = jnp.max(old, axis=1, keepdims=True)
    for score in news:
        peak = jnp.maximum(peak, score)
    old = jnp.exp(old - peak)
    news = [jnp.exp(score - peak) for score in news]
    total = jnp.sum(old, axis=1, keepdims=True)
    for score in news:
        total = total + score
    old = old / total
    extra = jnp.zeros((H, HD), jnp.float32)
    for score, (_, values) in zip(news, new):
        extra = extra + (score / total).astype(jnp.bfloat16).astype(jnp.float32) * values
    mixed = jnp.concatenate(
        [
            dot(
                old[j * GROUP : (j + 1) * GROUP].astype(jnp.bfloat16),
                cache_ref[0, 1, :, j * HD : (j + 1) * HD],
            )
            for j in range(KVH)
        ],
        axis=0,
    )
    mixed = mixed + extra
    if columns >= HD:
        for k in range(count):
            out_ref[k] = mixed[k * each : (k + 1) * each].astype(jnp.bfloat16)
    else:
        parts = HD // columns
        out = jnp.zeros((count, columns), jnp.float32)
        for p in range(parts):
            pick = (iota((count, H), 1) * parts + p == iota((count, H), 0)).astype(jnp.bfloat16)
            out = out + dot(pick, mixed[:, p * columns : (p + 1) * columns].astype(jnp.bfloat16))
        for k in range(count):
            out_ref[k] = out[k : k + 1].astype(jnp.bfloat16)


def output_terms(rows, core, weight_ref, own_ref, away_ref):
    count = rows.shape[0]
    chips = count // CORES
    slot = iota((count, count), 0)
    origin = (slot % chips) * CORES + (core ^ (slot // chips))
    order = (iota((count, count), 1) == origin).astype(jnp.bfloat16)
    rows = dot(order, rows).astype(jnp.bfloat16)
    width = weight_ref.shape[1]
    wide = width // 8
    for c in range(8):
        part = slice(c * wide, (c + 1) * wide)
        out = dot(rows, weight_ref[:, part])
        own_ref[:, part] = out[:chips]
        away_ref[:, part] = out[chips:].astype(jnp.bfloat16)


def output_kernel(lines_ref, me_ref, weight_ref, own_ref, away_ref, held):
    count, each, line = lines_ref.shape
    for k in range(count):
        held[k, :each, :] = lines_ref[k].astype(jnp.float32)
    rows = [held[:, c, :].astype(jnp.bfloat16) for c in range(each)]
    output_terms(jnp.concatenate(rows, axis=1), me_ref[0] % CORES, weight_ref, own_ref, away_ref)


def cut_kernel(half, me_ref, cache_hbm, *refs):
    outs, sems = refs[:-1], refs[-1]
    chip = me_ref[0] // CORES
    copies = []
    for d, out in enumerate(outs):
        for side in range(2):
            lanes = pl.ds(pl.multiple_of((chip ^ d ^ (side * half)) * HD, HD), HD)
            copies.append(
                pltpu.make_async_copy(
                    cache_hbm.at[0, :, :, lanes], out.at[side], sems.at[2 * d + side]
                )
            )
    for copy in copies:
        copy.start()
    for copy in copies:
        copy.wait()


def gate_kernel(*_):
    pass


def merge_kernel(amount, *refs):
    out_ref, sems = refs[-2:]
    copies = [pltpu.make_async_copy(refs[i], out_ref.at[i], sems.at[i]) for i in range(amount)]
    for copy in copies:
        copy.start()
    for copy in copies:
        copy.wait()


def pack_kernel(near, *refs):
    out_ref = refs[-1]
    total = refs[0][:, :LANES].astype(jnp.float32)
    for ref in refs[1:near]:
        total = total + ref[:, :LANES].astype(jnp.float32)
    out_ref[:, :LANES] = total.astype(jnp.bfloat16)
    for l in range(near):
        out_ref[:, (l + 1) * LANES : (l + 2) * LANES] = refs[l][:, LANES:]


def ask_kernel(parts, rank, *refs):
    lows = [ref[:, :rank].astype(jnp.float32) for ref in refs[:parts]]
    query_ref, adapter_ref, up_ref, me_ref, own_ref, away_ref = refs[parts:]
    query = up_terms(lows, query_ref, adapter_ref, up_ref)
    some = own_ref.shape[0]
    side = me_ref[0] // some
    low, high = query[:some], query[some:]
    own_ref[...] = jnp.where(side == 0, low, high).astype(jnp.bfloat16)
    away_ref[...] = jnp.where(side == 0, high, low).astype(jnp.bfloat16)


def halves_kernel(parts, near, steps, *refs):
    own_ref, other_ref, lengths_ref, me_ref = refs[:4]
    lows, refs = refs[4 : 4 + parts], refs[4 + parts :]
    if steps > 1:
        past_ref, refs = refs[0], refs[1:]
    mine_ref, away_ref, new_ref, held, all_ref, mixed_ref = refs[-6:]
    blocks = refs[:-6]
    blocks = [*blocks[:-2], *(blocks[-2].at[d] for d in range(len(blocks) - 3)), blocks[-1]]
    some, columns = own_ref.shape
    each = columns // HD
    lines = held.shape[2]
    me = me_ref[0]
    chip, core = me // CORES, me % CORES
    half = KVH // 2
    side = me // some
    held[...] = jnp.zeros(held.shape, jnp.float32)
    for s, ref in enumerate((own_ref, other_ref)):
        query = ref[...].astype(jnp.float32)
        for c in range(each):
            held[s, :, c, :] = query[:, c * HD : (c + 1) * HD]
    for k in range(parts):
        for l in range(near):
            all_ref[k * near + l] = lows[k][:, (l + 1) * LANES : (l + 2) * LANES].astype(jnp.float32)
    for s in range(2):
        for v in range(2):
            holder = (chip ^ (s * half)) + v * KVH
            new_ref[steps - 1, s, v] = all_ref[me ^ holder, pl.ds(pl.multiple_of(side * some, some), some), :]
    for t in range(steps - 1):
        new_ref[t] = past_ref[t]
    scale = 1.0 / math.sqrt(HD)
    rows = [((chip ^ d) % half) * CORES + (core ^ l) for l in range(CORES) for d in range(half)]
    old, fresh = [], [[] for _ in range(steps)]
    for row, block in zip(rows, blocks):
        length = lengths_ref[pl.ds(side * some + row, 1), :]
        for s in range(2):
            query = held[s, row]
            score = dot(query.astype(jnp.bfloat16), block[s, 0], LAST) * scale
            old.append(jnp.where(iota(score.shape, 1) < length, score, -jnp.inf))
            for t in range(steps):
                keys = new_ref[t, s, 0, pl.ds(row, 1), :]
                fresh[t].append(jnp.sum(query * keys, axis=1, keepdims=True) * scale)
    old = jnp.concatenate(old, axis=0)
    fresh = [jnp.concatenate(scores, axis=0) for scores in fresh]
    peak = jnp.max(old, axis=1, keepdims=True)
    for scores in fresh:
        peak = jnp.maximum(peak, scores)
    old = jnp.exp(old - peak)
    fresh = [jnp.exp(scores - peak) for scores in fresh]
    total = jnp.sum(old, axis=1, keepdims=True)
    for scores in fresh:
        total = total + scores
    old = (old / total).astype(jnp.bfloat16).astype(jnp.float32)
    fresh = [(scores / total).astype(jnp.bfloat16).astype(jnp.float32) for scores in fresh]
    for b, (row, block) in enumerate(zip(rows, blocks)):
        for s in range(2):
            part = slice((2 * b + s) * lines, (2 * b + s + 1) * lines)
            mixed = dot(old[part].astype(jnp.bfloat16), block[s, 1])
            for t in range(steps):
                mixed = mixed + fresh[t][part] * new_ref[t, s, 1, pl.ds(row, 1), :]
            mixed_ref[s, row] = mixed
    for c in range(each):
        part = slice(c * HD, (c + 1) * HD)
        mine_ref[:, part] = mixed_ref[0, :, c, :].astype(jnp.bfloat16)
        away_ref[:, part] = mixed_ref[1, :, c, :].astype(jnp.bfloat16)


def joined_kernel(mine_ref, other_ref, me_ref, weight_ref, own_ref, away_ref):
    some = mine_ref.shape[0]
    mine, other = mine_ref[...].astype(jnp.float32), other_ref[...].astype(jnp.float32)
    side = me_ref[0] // some
    rows = jnp.concatenate(
        [jnp.where(side == 0, mine, other), jnp.where(side == 0, other, mine)], axis=0
    ).astype(jnp.bfloat16)
    output_terms(rows, me_ref[0] % CORES, weight_ref, own_ref, away_ref)


def partial_kernel(own_ref, other_ref, out_ref):
    total = own_ref[...] + other_ref[...].astype(jnp.float32)
    wide = out_ref.shape[2]
    for k in range(out_ref.shape[0]):
        for i in range(FOLD):
            out_ref[k, i : i + 1, :] = total[k : k + 1, i * wide : (i + 1) * wide].astype(
                out_ref.dtype
            )


def finish_kernel(last, parts_ref, hidden_ref, scale_ref, out_ref, *spread):
    total = parts_ref[0].astype(jnp.float32)
    for k in range(1, parts_ref.shape[0]):
        total = total + parts_ref[k].astype(jnp.float32)
    total = jnp.concatenate([total[i : i + 1] for i in range(FOLD)], axis=1)
    total = total.astype(jnp.bfloat16).astype(jnp.float32)
    before = hidden_ref[...].astype(jnp.float32)
    hidden = (before + total).astype(jnp.bfloat16).astype(jnp.float32)
    if last:
        out_ref[...] = jnp.concatenate([before, hidden], axis=0).astype(jnp.bfloat16)
    else:
        out_ref[...] = hidden.astype(jnp.bfloat16)
        folded(spread[0], normalized(hidden, scale_ref[...].astype(jnp.float32)).astype(jnp.float32))


def shards(
    hidden_state_input,
    attention_norm_scale,
    query_weight,
    key_value_weight,
    output_weight,
    adapter_down_weight,
    adapter_up_weight,
    row_adapter_index,
    adapter_storage_index,
    cache_length_per_row,
    key_value_cache,
):
    count = lax.axis_size(AXIS)
    chips = count // CORES
    far, near = split_of(count)
    far_steps = [k * near for k in range(1, far)]
    near_steps = list(range(1, near))
    kept, width, rank = adapter_down_weight.shape
    columns = query_weight.shape[1]
    fresh_columns = key_value_weight.shape[1]
    line = min(HD, columns)
    smem, vmem = pltpu.SMEM, pltpu.VMEM
    call = functools.partial(kernel, vmem=min(20 << 20, (count * 3 // 4) << 20))
    me = lax.axis_index(AXIS).astype(jnp.int32).reshape(1)
    down = adapter_down_weight.transpose(0, 2, 1)
    scale = attention_norm_scale[None]
    storage = adapter_storage_index[None]

    def gate(arrays, *behind):
        return pl.pallas_call(
            gate_kernel,
            out_shape=[shape(a.shape, a.dtype) for a in arrays],
            in_specs=[pl.BlockSpec(memory_space=pl.ANY)] * (len(arrays) + len(behind)),
            out_specs=[pl.BlockSpec(memory_space=pl.ANY)] * len(arrays),
            input_output_aliases={i: i for i in range(len(arrays))},
            compiler_params=pltpu.CompilerParams(vmem_limit_bytes=1 << 20),
            name="gate",
        )(*arrays, *behind)

    def stash(token, arrays, limit):
        outs = call(
            functools.partial(stash_kernel, len(arrays)),
            [pltpu.VMEM(a.shape, a.dtype) for a in arrays] + [shape((8, LANES), jnp.float32)],
            "stash",
            [pltpu.SemaphoreType.DMA((len(arrays),))],
            vmem=limit,
            moved=sum(2 * a.size for a in arrays),
        )(token, *arrays, specs=[vmem] + [pl.ANY] * len(arrays))
        return outs[:-1], outs[-1]

    past, held_cache, blocks = [], [], []

    def after(*numbers):
        return [blocks[d] for d in numbers] if blocks else []


    def by_rows(step, lows, query, fresh):
        first = step == 0
        (lines,) = call(
            functools.partial(up_kernel, far),
            [shape((count, 8, line))],
            "up",
            [pltpu.VMEM((count, 8, line), jnp.float32)],
        )(*lows, query, fresh, adapter, up_w)

        lines = swap(lines)
        outs = [shape((count, columns // line, line))]
        if first:
            outs = outs + [shape((H, HD), jnp.float32)] * 2
        outs = call(
            functools.partial(attend_kernel, columns, fresh_columns, first),
            outs,
            "attend",
            [
                pltpu.VMEM((count, 8, line), jnp.float32),
                pltpu.VMEM((H, key_value_cache.shape[2]), jnp.float32),
            ],
            moved=2 << 20,
        )(
            lines,
            length,
            held_cache[0],
            *past,
            specs=[vmem] * (3 + len(past)),
        )
        if first:
            past.extend(outs[1:])

        lines = swap(outs[0])
        own, away = call(
            output_kernel,
            [shape((chips, width), jnp.float32), shape((chips, width))],
            "output",
            [pltpu.VMEM((count, 8, line), jnp.float32)],
            flops=2 * count * width * columns,
            moved=2 * width * columns,
        )(lines, me, output_w, specs=[vmem, smem, vmem])
        return own, away

    hidden = hidden_state_input
    carried, length = call(
        first_kernel, [shape((1, width + LANES)), shape((8, LANES), jnp.int32)], "first"
    )(hidden, scale, row_adapter_index, cache_length_per_row, specs=[vmem, vmem, smem, smem])
    fresh_past = []
    by_halves = columns * CORES == GROUP * HD and count == CORES * KVH and fresh_columns == LANES
    for step in range(STEPS):
        first, last = step == 0, step == STEPS - 1
        low_outs = [shape((count, width))]
        if by_halves:
            low_outs = low_outs + [shape((count, LANES + fresh_columns))]
        else:
            low_outs = low_outs + [shape((count, rank)), shape((count, fresh_columns))]
        scratch = [pltpu.VMEM((count, width), jnp.float32)]
        if first:
            token = jnp.zeros((8, LANES), jnp.float32)
            arrays = [query_weight, output_weight, key_value_weight, down, adapter_up_weight]
            if by_halves:
                half = chips // 2
                cut = call(
                    functools.partial(cut_kernel, half),
                    [shape((2, 2, key_value_cache.shape[2], HD))] * half,
                    "cut",
                    [pltpu.SemaphoreType.DMA((2 * half,))],
                    vmem=56 << 20,
                )(me, key_value_cache, specs=[smem, pl.ANY])
                blocks.extend([cut[0]] + [shift(cut[d], CORES * d, count) for d in range(1, half - 1)])
            else:
                arrays.append(key_value_cache)
            outs, token = stash(token, arrays, 30 << 20)
            query_w, output_w, fresh_w, down_w, up_w = outs[:5]
            held_cache.append(outs[-1])
            pieces = across(carried, far_steps, count)
            (carried,) = call(
                functools.partial(join_kernel, far), [shape((far, width + LANES))], "join"
            )(*pieces, token, *after(1, 2), specs=[vmem] * (far + 1) + [pl.ANY] * len(after(1, 2)))
            if by_halves:
                (still,) = gate([cut[half - 1]], carried)
                blocks.append(shift(still, CORES * (half - 1), count))
                (merged,) = call(
                    functools.partial(merge_kernel, half - 1),
                    [shape((half - 1, *cut[0].shape))],
                    "merge",
                    [pltpu.SemaphoreType.DMA((half - 1,))],
                )(*blocks[:-1], carried, specs=[pl.ANY] * half)
                blocks.append(shift(merged, 1, count))
            pieces = across(carried, near_steps, count)
            member, adapter, lengths = call(
                functools.partial(member_kernel, near, far, width),
                [shape((count, kept), jnp.int32)] + [shape((count, 1), jnp.int32)] * 2,
                "member",
                [pltpu.VMEM((count, LANES), jnp.float32)],
            )(
                *pieces,
                me,
                storage,
                *after(4),
                specs=[vmem] * near + [smem, vmem] + [pl.ANY] * len(after(4)),
            )
            rows, low, *fresh = call(
                functools.partial(low_first_kernel, near, far), low_outs, "low", scratch
            )(
                *pieces,
                me,
                member,
                down_w,
                fresh_w,
                specs=[vmem] * near + [smem] + [vmem] * 3,
            )
        else:
            own = chips_swap(carried, count)
            rows, low, *fresh = call(low_later_kernel, low_outs, "low", scratch)(
                own,
                shift(own, 1, count),
                me,
                member,
                down_w,
                fresh_w,
                specs=[vmem, vmem, smem, vmem, vmem, vmem],
            )
        if first and by_halves:
            (still,) = gate([blocks[half - 1]], rows)
            blocks[half - 1] = still
            blocks.append(shift(still, 1, count))
        lows = across(low, near_steps, count)
        behind = after(3) if first else []
        if by_halves:
            body, dims = pack_kernel, (count, (near + 1) * LANES)
        else:
            body, dims = sum_kernel, (count, rank)
        (low,) = call(functools.partial(body, near), [shape(dims)], "sum")(
            *lows, *behind, specs=[vmem] * near + [pl.ANY] * len(behind)
        )
        lows = across(low, far_steps, count)
        (query,) = call(
            project_kernel,
            [shape((count, columns), jnp.float32)],
            "project",
            flops=2 * count * width * columns,
            moved=2 * width * columns,
        )(rows, query_w)
        if by_halves:
            some = count // 2
            rows_half = shape((some, columns))
            own, away = call(functools.partial(ask_kernel, far, rank), [rows_half] * 2, "ask")(
                *lows, query, adapter, up_w, me, specs=[vmem] * (far + 3) + [smem]
            )
            new = (step + 1, 2, 2, some, HD)
            mine, away, *fresh_past = call(
                functools.partial(halves_kernel, far, near, step + 1),
                [rows_half, rows_half, shape(new, jnp.float32)],
                "attend",
                [
                    pltpu.VMEM((2, some, 8, HD), jnp.float32),
                    pltpu.VMEM((count, count, LANES), jnp.float32),
                    pltpu.VMEM((2, some, 8, HD), jnp.float32),
                ],
                moved=4 << 20,
            )(
                own,
                shift(away, some, count),
                lengths,
                me,
                *lows,
                *fresh_past,
                *blocks,
                specs=[vmem] * 3 + [smem] + [vmem] * (far + len(fresh_past) + len(blocks)),
            )
            own, away = call(
                joined_kernel,
                [shape((chips, width), jnp.float32), shape((chips, width))],
                "output",
                flops=2 * count * width * columns,
                moved=2 * width * columns,
            )(mine, shift(away, some, count), me, output_w, specs=[vmem, vmem, smem, vmem])
        else:
            own, away = by_rows(step, lows, query, fresh[0])

        (parts,) = call(partial_kernel, [shape((chips, FOLD, width // FOLD))], "partial")(
            own, shift(away, 1, count)
        )
        parts = chips_swap(parts, count)
        outs = [shape((2 if last else 1, width))]
        if not last:
            outs = outs + [shape((chips, FOLD, width // FOLD))]
        outs = call(functools.partial(finish_kernel, last), outs, "finish")(parts, hidden, scale)
        if last:
            return outs[0].reshape(STEPS, 1, width)
        hidden, carried = outs


def solution(mesh):
    in_specs = (
        P(("groups", "replica"), None),
        P(),
        P(None, "replica"),
        P(None, "replica"),
        P("replica", None),
        P("replica", None, None),
        P(None, None, "replica"),
        P(("groups", "replica")),
        P(),
        P(("groups", "replica")),
        P(("groups", "replica"), None, None, None),
    )
    out_specs = P(None, ("groups", "replica"), None)
    return jax.shard_map(shards, mesh=mesh, in_specs=in_specs, out_specs=out_specs, check_vma=False)
```

```python
import functools
import math

import jax
import jax.numpy as jnp
from jax import lax
from jax.experimental import pallas as pl
from jax.experimental.pallas import tpu as pltpu
from jax.sharding import PartitionSpec as P

H = 64
KVH = 8
HD = 128
STEPS = 2
GROUP = H // KVH
EPS = 1e-05
AXIS = "replica"
LANES = 128
LAST = (((1,), (1,)), ((), ()))
FIRST = (((0,), (0,)), ((), ()))

CORES = 2
FOLD = 8


def split_of(count):
    far = 1 << (count.bit_length() // 2)
    return far, count // far


def shift(block, distance, count):
    return lax.ppermute(block, AXIS, [(i, i ^ distance) for i in range(count)])


def across(block, strides, count):
    return [block] + [shift(block, d, count) for d in strides]


def swap(blocks):
    return lax.all_to_all(blocks, AXIS, split_axis=0, concat_axis=0, tiled=True)


def chips_swap(blocks, count):
    groups = [[i for i in range(count) if i % CORES == c] for c in range(CORES)]
    return lax.all_to_all(
        blocks, AXIS, split_axis=0, concat_axis=0, axis_index_groups=groups, tiled=True
    )


def kernel(body, outs, name, scratch=(), vmem=20 << 20, flops=1 << 20, moved=1 << 18):
    def run(*operands, specs=None):
        specs = specs or [pltpu.VMEM] * len(operands)
        return pl.pallas_call(
            body,
            out_shape=outs,
            in_specs=[pl.BlockSpec(memory_space=s) for s in specs],
            out_specs=[pl.BlockSpec(memory_space=pltpu.VMEM)] * len(outs),
            scratch_shapes=list(scratch),
            compiler_params=pltpu.CompilerParams(vmem_limit_bytes=vmem),
            cost_estimate=pl.CostEstimate(flops=flops, bytes_accessed=moved, transcendentals=0),
            name=name,
        )(*operands)

    return run


def shape(dims, dtype=jnp.bfloat16):
    return jax.ShapeDtypeStruct(dims, dtype)


def iota(dims, axis):
    return lax.broadcasted_iota(jnp.int32, dims, axis)


def dot(a, b, contract=(((1,), (0,)), ((), ()))):
    return lax.dot_general(a, b, contract, preferred_element_type=jnp.float32)


def normalized(hidden, scale):
    factor = lax.rsqrt(jnp.mean(hidden * hidden, axis=-1, keepdims=True) + EPS)
    return (hidden * factor * scale).astype(jnp.bfloat16)


def folded(out_ref, row):
    wide = row.shape[1] // FOLD
    for k in range(out_ref.shape[0]):
        for i in range(FOLD):
            out_ref[k, i : i + 1, :wide] = row[:, i * wide : (i + 1) * wide].astype(out_ref.dtype)


def first_kernel(hidden_ref, scale_ref, adapter_ref, length_ref, out_ref, length_out):
    length_out[...] = jnp.full(length_out.shape, length_ref[0], jnp.int32)
    width = hidden_ref.shape[1]
    hidden = hidden_ref[...].astype(jnp.float32)
    out_ref[:, :width] = normalized(hidden, scale_ref[...].astype(jnp.float32))
    digit = iota((1, LANES), 1)
    adapter = adapter_ref[0]
    length = length_ref[0]
    digits = jnp.where(digit == 0, adapter % 256, jnp.where(digit == 1, adapter // 256, 0))
    digits = jnp.where(digit == 2, length % 256, jnp.where(digit == 3, length // 256, digits))
    digits = digits.astype(jnp.float32)
    out_ref[:, width:] = digits.astype(jnp.bfloat16)


def stash_kernel(amount, token_ref, *refs):
    sources, refs = refs[:amount], refs[amount:]
    outs, out_token, sems = refs[:amount], refs[amount], refs[-1]
    copies = [
        pltpu.make_async_copy(sources[i], outs[i], sems.at[i]) for i in range(amount)
    ]
    for copy in copies:
        copy.start()
    out_token[...] = token_ref[...] * 0.0
    for copy in copies:
        copy.wait()


def member_kernel(near, far, width, *refs):
    pieces = refs[:near]
    me_ref, storage_ref = refs[near : near + 2]
    member_ref, adapter_ref, lengths_ref, held = refs[-4:]
    kept = member_ref.shape[1]
    count = near * far
    me = me_ref[0]
    for l in range(near):
        digits = pieces[l][:, width:].astype(jnp.float32)
        for k in range(far):
            held[pl.ds(me ^ (k * near + l), 1), :] = digits[k : k + 1]
    adapter = (held[:, 0:1] + 256.0 * held[:, 1:2]).astype(jnp.int32)
    adapter_ref[...] = adapter
    lengths_ref[...] = (held[:, 2:3] + 256.0 * held[:, 3:4]).astype(jnp.int32)
    table = storage_ref.shape[1]
    chosen = jnp.where(iota((count, table), 1) == adapter, storage_ref[...], 0)
    storage = jnp.sum(chosen.astype(jnp.float32), axis=1, keepdims=True).astype(jnp.int32)
    member_ref[...] = (storage - me * kept == iota((count, kept), 1)).astype(jnp.int32)


def low_terms(held, member_ref, down_ref, fresh_w, rows_ref, *outs):
    rows = held[...].astype(jnp.bfloat16)
    rows_ref[...] = rows
    rank = down_ref.shape[1]
    low = jnp.zeros((rows.shape[0], rank), jnp.float32)
    for index in range(down_ref.shape[0]):
        part = dot(rows, down_ref[index], LAST)
        low = jnp.where(member_ref[:, index : index + 1] > 0, part, low)
    fresh = dot(rows, fresh_w[...]).astype(jnp.bfloat16)
    if len(outs) == 2:
        outs[0][...] = low.astype(jnp.bfloat16)
        outs[1][...] = fresh
    else:
        outs[0][:, :rank] = low.astype(jnp.bfloat16)
        outs[0][:, rank:LANES] = jnp.zeros((rows.shape[0], LANES - rank), jnp.bfloat16)
        outs[0][:, LANES:] = fresh


def low_first_kernel(near, far, *refs):
    pieces = refs[:near]
    me_ref, member_ref, down_ref, fresh_w = refs[near : near + 4]
    outs, held = refs[near + 4 : -1], refs[-1]
    width = held.shape[1]
    for l in range(near):
        block = pieces[l][:, :width].astype(jnp.float32)
        for k in range(far):
            held[pl.ds(me_ref[0] ^ (k * near + l), 1), :] = block[k : k + 1]
    low_terms(held, member_ref, down_ref, fresh_w, *outs)


def low_later_kernel(own_ref, other_ref, me_ref, member_ref, down_ref, fresh_w, *refs):
    outs, held = refs[:-1], refs[-1]
    core = me_ref[0] % CORES
    for ref, flip in ((own_ref, 0), (other_ref, 1)):
        wide = ref.shape[2]
        for k in range(ref.shape[0]):
            block = ref[k].astype(jnp.float32)
            row = pl.ds(k * CORES + (core ^ flip), 1)
            for i in range(FOLD):
                held[row, i * wide : (i + 1) * wide] = block[i : i + 1]
    low_terms(held, member_ref, down_ref, fresh_w, *outs)


def join_kernel(amount, *refs):
    rows = [ref[...].astype(jnp.float32) for ref in refs[:amount]]
    refs[-1][...] = jnp.concatenate(rows, axis=0).astype(refs[-1].dtype)


def sum_kernel(amount, *refs):
    total = refs[0][...].astype(jnp.float32)
    for ref in refs[1:amount]:
        total = total + ref[...].astype(jnp.float32)
    refs[-1][...] = total.astype(refs[-1].dtype)


def project_kernel(rows_ref, query_w, query_ref):
    query_ref[...] = dot(rows_ref[...], query_w[...])


def up_terms(lows, query_ref, adapter_ref, up_ref):
    count, columns = query_ref.shape
    rank = lows[0].shape[1]
    low = functools.reduce(lambda a, b: a + b, lows).astype(jnp.bfloat16)
    query = query_ref[...]
    table = up_ref.shape[0]
    some = min(table, 32)
    wide = some * rank
    repeat = (iota((rank, wide), 1) % rank == iota((rank, wide), 0)).astype(jnp.bfloat16)
    wide_low = dot(low, repeat)
    place = iota((count, wide), 1) // rank
    for start in range(0, table, some):
        spread = jnp.where(place + start == adapter_ref[...], wide_low, 0.0).astype(jnp.bfloat16)
        query = query + dot(spread, up_ref[start : start + some].reshape(wide, columns))
    return query


def up_kernel(parts, *refs):
    lows, (query_ref, fresh_ref, adapter_ref, up_ref, out_ref, held) = refs[:parts], refs[parts:]
    count, columns = query_ref.shape
    lows = [ref[...].astype(jnp.float32) for ref in lows]
    query = up_terms(lows, query_ref, adapter_ref, up_ref)
    line = out_ref.shape[2]
    lines = columns // line
    held[...] = jnp.zeros(held.shape, jnp.float32)
    for c in range(lines):
        held[:, c, :] = query[:, c * line : (c + 1) * line]
    fresh = fresh_ref[...].astype(jnp.float32)
    if fresh.shape[1] < line:
        fresh = jnp.concatenate(
            [fresh, jnp.zeros((count, line - fresh.shape[1]), jnp.float32)], axis=1
        )
    held[:, lines, :] = fresh
    for k in range(count):
        out_ref[k] = held[k].astype(jnp.bfloat16)


def pieces_of(lines, select, whole, size):
    if size >= whole:
        total = dot(select(len(lines), 0), lines[0])
        for c in range(1, len(lines)):
            total = total + dot(select(len(lines), c), lines[c])
        return total
    return jnp.concatenate([dot(select(0, p), lines[0]) for p in range(whole // size)], axis=1)


def attend_kernel(columns, fresh_columns, first, *refs):
    lines_ref, length_ref, cache_ref = refs[:3]
    refs = refs[3:]
    if not first:
        past, refs = refs[:2], refs[2:]
    out_ref, refs = refs[0], refs[1:]
    if first:
        keep, refs = refs[:2], refs[2:]
    held, scores = refs
    count, _, line = lines_ref.shape
    cache = cache_ref.shape[2]
    for k in range(count):
        held[k] = lines_ref[k].astype(jnp.float32)
    each = columns // line
    lines = [held[:, c, :].astype(jnp.bfloat16) for c in range(each + 1)]
    origin = iota((H, count), 1)
    head = iota((H, count), 0)

    def query_pick(each, c):
        if each:
            return (head == origin * each + c).astype(jnp.bfloat16)
        return (head * (HD // columns) + c == origin).astype(jnp.bfloat16)

    def fresh_pick(offset):
        def pick(each, c):
            want = head // GROUP + offset
            if each:
                return (want == origin * each + c).astype(jnp.bfloat16)
            return (want * (HD // fresh_columns) + c == origin).astype(jnp.bfloat16)

        return pick

    query = pieces_of(lines[:each], query_pick, HD, columns)
    fresh = [lines[each][:, :fresh_columns]]
    new = [
        (
            pieces_of(fresh, fresh_pick(0), HD, fresh_columns),
            pieces_of(fresh, fresh_pick(KVH), HD, fresh_columns),
        )
    ]
    if first:
        keep[0][...], keep[1][...] = new[0]
    else:
        new.insert(0, (past[0][...], past[1][...]))
    scale = 1.0 / math.sqrt(HD)
    for j in range(KVH):
        rows = slice(j * GROUP, (j + 1) * GROUP)
        scores[rows, :] = dot(
            query[rows].astype(jnp.bfloat16), cache_ref[0, 0, :, j * HD : (j + 1) * HD], LAST
        )
    in_cache = iota((H, cache), 1) < length_ref[0:1, 0:1]
    old = jnp.where(in_cache, scores[...] * scale, -jnp.inf)
    news = [jnp.sum(query * keys, axis=1, keepdims=True) * scale for keys, _ in new]
    peak = jnp.max(old, axis=1, keepdims=True)
    for score in news:
        peak = jnp.maximum(peak, score)
    old = jnp.exp(old - peak)
    news = [jnp.exp(score - peak) for score in news]
    total = jnp.sum(old, axis=1, keepdims=True)
    for score in news:
        total = total + score
    old = old / total
    extra = jnp.zeros((H, HD), jnp.float32)
    for score, (_, values) in zip(news, new):
        extra = extra + (score / total).astype(jnp.bfloat16).astype(jnp.float32) * values
    mixed = jnp.concatenate(
        [
            dot(
                old[j * GROUP : (j + 1) * GROUP].astype(jnp.bfloat16),
                cache_ref[0, 1, :, j * HD : (j + 1) * HD],
            )
            for j in range(KVH)
        ],
        axis=0,
    )
    mixed = mixed + extra
    if columns >= HD:
        for k in range(count):
            out_ref[k] = mixed[k * each : (k + 1) * each].astype(jnp.bfloat16)
    else:
        parts = HD // columns
        out = jnp.zeros((count, columns), jnp.float32)
        for p in range(parts):
            pick = (iota((count, H), 1) * parts + p == iota((count, H), 0)).astype(jnp.bfloat16)
            out = out + dot(pick, mixed[:, p * columns : (p + 1) * columns].astype(jnp.bfloat16))
        for k in range(count):
            out_ref[k] = out[k : k + 1].astype(jnp.bfloat16)


def output_terms(rows, core, weight_ref, own_ref, away_ref):
    count = rows.shape[0]
    chips = count // CORES
    slot = iota((count, count), 0)
    origin = (slot % chips) * CORES + (core ^ (slot // chips))
    order = (iota((count, count), 1) == origin).astype(jnp.bfloat16)
    rows = dot(order, rows).astype(jnp.bfloat16)
    width = weight_ref.shape[1]
    wide = width // 8
    for c in range(8):
        part = slice(c * wide, (c + 1) * wide)
        out = dot(rows, weight_ref[:, part])
        own_ref[:, part] = out[:chips]
        away_ref[:, part] = out[chips:].astype(jnp.bfloat16)


def output_kernel(lines_ref, me_ref, weight_ref, own_ref, away_ref, held):
    count, each, line = lines_ref.shape
    for k in range(count):
        held[k, :each, :] = lines_ref[k].astype(jnp.float32)
    rows = [held[:, c, :].astype(jnp.bfloat16) for c in range(each)]
    output_terms(jnp.concatenate(rows, axis=1), me_ref[0] % CORES, weight_ref, own_ref, away_ref)


def cut_kernel(half, me_ref, cache_hbm, *refs):
    outs, sems = refs[:-1], refs[-1]
    chip = me_ref[0] // CORES
    copies = []
    for d, out in enumerate(outs):
        for side in range(2):
            lanes = pl.ds(pl.multiple_of((chip ^ d ^ (side * half)) * HD, HD), HD)
            copies.append(
                pltpu.make_async_copy(
                    cache_hbm.at[0, :, :, lanes], out.at[side], sems.at[2 * d + side]
                )
            )
    for copy in copies:
        copy.start()
    for copy in copies:
        copy.wait()


def late_kernel(row_ref, _, out_ref):
    out_ref[...] = row_ref[...]


def merge_kernel(amount, *refs):
    out_ref, sems = refs[-2:]
    copies = [pltpu.make_async_copy(refs[i], out_ref.at[i], sems.at[i]) for i in range(amount)]
    for copy in copies:
        copy.start()
    for copy in copies:
        copy.wait()


def pack_kernel(near, *refs):
    out_ref = refs[-1]
    total = refs[0][:, :LANES].astype(jnp.float32)
    for ref in refs[1:near]:
        total = total + ref[:, :LANES].astype(jnp.float32)
    out_ref[:, :LANES] = total.astype(jnp.bfloat16)
    for l in range(near):
        out_ref[:, (l + 1) * LANES : (l + 2) * LANES] = refs[l][:, LANES:]


def ask_kernel(parts, rank, *refs):
    lows = [ref[:, :rank].astype(jnp.float32) for ref in refs[:parts]]
    query_ref, adapter_ref, up_ref, me_ref, own_ref, away_ref = refs[parts:]
    query = up_terms(lows, query_ref, adapter_ref, up_ref)
    some = own_ref.shape[0]
    side = me_ref[0] // some
    low, high = query[:some], query[some:]
    own_ref[...] = jnp.where(side == 0, low, high).astype(jnp.bfloat16)
    away_ref[...] = jnp.where(side == 0, high, low).astype(jnp.bfloat16)


def halves_kernel(parts, near, steps, *refs):
    own_ref, other_ref, lengths_ref, me_ref = refs[:4]
    lows, refs = refs[4 : 4 + parts], refs[4 + parts :]
    if steps > 1:
        past_ref, refs = refs[0], refs[1:]
    mine_ref, away_ref, new_ref, held, all_ref, mixed_ref = refs[-6:]
    blocks = refs[:-6]
    blocks = [*blocks[:-1], *(blocks[-1].at[d] for d in range(len(blocks) - 1))]
    some, columns = own_ref.shape
    each = columns // HD
    lines = held.shape[2]
    me = me_ref[0]
    chip, core = me // CORES, me % CORES
    half = KVH // 2
    side = me // some
    held[...] = jnp.zeros(held.shape, jnp.float32)
    for s, ref in enumerate((own_ref, other_ref)):
        query = ref[...].astype(jnp.float32)
        for c in range(each):
            held[s, :, c, :] = query[:, c * HD : (c + 1) * HD]
    for k in range(parts):
        for l in range(near):
            all_ref[k * near + l] = lows[k][:, (l + 1) * LANES : (l + 2) * LANES].astype(jnp.float32)
    for s in range(2):
        for v in range(2):
            holder = (chip ^ (s * half)) + v * KVH
            new_ref[steps - 1, s, v] = all_ref[me ^ holder, pl.ds(pl.multiple_of(side * some, some), some), :]
    for t in range(steps - 1):
        new_ref[t] = past_ref[t]
    scale = 1.0 / math.sqrt(HD)
    rows = [((chip ^ d) % half) * CORES + (core ^ l) for l in range(CORES) for d in range(half)]
    old, fresh = [], [[] for _ in range(steps)]
    for row, block in zip(rows, blocks):
        length = lengths_ref[pl.ds(side * some + row, 1), :]
        for s in range(2):
            query = held[s, row]
            score = dot(query.astype(jnp.bfloat16), block[s, 0], LAST) * scale
            old.append(jnp.where(iota(score.shape, 1) < length, score, -jnp.inf))
            for t in range(steps):
                keys = new_ref[t, s, 0, pl.ds(row, 1), :]
                fresh[t].append(jnp.sum(query * keys, axis=1, keepdims=True) * scale)
    old = jnp.concatenate(old, axis=0)
    fresh = [jnp.concatenate(scores, axis=0) for scores in fresh]
    peak = jnp.max(old, axis=1, keepdims=True)
    for scores in fresh:
        peak = jnp.maximum(peak, scores)
    old = jnp.exp(old - peak)
    fresh = [jnp.exp(scores - peak) for scores in fresh]
    total = jnp.sum(old, axis=1, keepdims=True)
    for scores in fresh:
        total = total + scores
    old = (old / total).astype(jnp.bfloat16).astype(jnp.float32)
    fresh = [(scores / total).astype(jnp.bfloat16).astype(jnp.float32) for scores in fresh]
    for b, (row, block) in enumerate(zip(rows, blocks)):
        for s in range(2):
            part = slice((2 * b + s) * lines, (2 * b + s + 1) * lines)
            mixed = dot(old[part].astype(jnp.bfloat16), block[s, 1])
            for t in range(steps):
                mixed = mixed + fresh[t][part] * new_ref[t, s, 1, pl.ds(row, 1), :]
            mixed_ref[s, row] = mixed
    for c in range(each):
        part = slice(c * HD, (c + 1) * HD)
        mine_ref[:, part] = mixed_ref[0, :, c, :].astype(jnp.bfloat16)
        away_ref[:, part] = mixed_ref[1, :, c, :].astype(jnp.bfloat16)


def joined_kernel(mine_ref, other_ref, me_ref, weight_ref, own_ref, away_ref):
    some = mine_ref.shape[0]
    mine, other = mine_ref[...].astype(jnp.float32), other_ref[...].astype(jnp.float32)
    side = me_ref[0] // some
    rows = jnp.concatenate(
        [jnp.where(side == 0, mine, other), jnp.where(side == 0, other, mine)], axis=0
    ).astype(jnp.bfloat16)
    output_terms(rows, me_ref[0] % CORES, weight_ref, own_ref, away_ref)


def partial_kernel(own_ref, other_ref, out_ref):
    total = own_ref[...] + other_ref[...].astype(jnp.float32)
    wide = out_ref.shape[2]
    for k in range(out_ref.shape[0]):
        for i in range(FOLD):
            out_ref[k, i : i + 1, :] = total[k : k + 1, i * wide : (i + 1) * wide].astype(
                out_ref.dtype
            )


def finish_kernel(last, parts_ref, hidden_ref, scale_ref, out_ref, *spread):
    total = parts_ref[0].astype(jnp.float32)
    for k in range(1, parts_ref.shape[0]):
        total = total + parts_ref[k].astype(jnp.float32)
    total = jnp.concatenate([total[i : i + 1] for i in range(FOLD)], axis=1)
    total = total.astype(jnp.bfloat16).astype(jnp.float32)
    before = hidden_ref[...].astype(jnp.float32)
    hidden = (before + total).astype(jnp.bfloat16).astype(jnp.float32)
    if last:
        out_ref[...] = jnp.concatenate([before, hidden], axis=0).astype(jnp.bfloat16)
    else:
        out_ref[...] = hidden.astype(jnp.bfloat16)
        folded(spread[0], normalized(hidden, scale_ref[...].astype(jnp.float32)).astype(jnp.float32))


def shards(
    hidden_state_input,
    attention_norm_scale,
    query_weight,
    key_value_weight,
    output_weight,
    adapter_down_weight,
    adapter_up_weight,
    row_adapter_index,
    adapter_storage_index,
    cache_length_per_row,
    key_value_cache,
):
    count = lax.axis_size(AXIS)
    chips = count // CORES
    far, near = split_of(count)
    far_steps = [k * near for k in range(1, far)]
    near_steps = list(range(1, near))
    kept, width, rank = adapter_down_weight.shape
    columns = query_weight.shape[1]
    fresh_columns = key_value_weight.shape[1]
    line = min(HD, columns)
    smem, vmem = pltpu.SMEM, pltpu.VMEM
    call = functools.partial(kernel, vmem=min(20 << 20, (count * 3 // 4) << 20))
    me = lax.axis_index(AXIS).astype(jnp.int32).reshape(1)
    down = adapter_down_weight.transpose(0, 2, 1)
    scale = attention_norm_scale[None]
    storage = adapter_storage_index[None]

    def stash(token, arrays, limit):
        outs = call(
            functools.partial(stash_kernel, len(arrays)),
            [pltpu.VMEM(a.shape, a.dtype) for a in arrays] + [shape((8, LANES), jnp.float32)],
            "stash",
            [pltpu.SemaphoreType.DMA((len(arrays),))],
            vmem=limit,
            moved=sum(2 * a.size for a in arrays),
        )(token, *arrays, specs=[vmem] + [pl.ANY] * len(arrays))
        return outs[:-1], outs[-1]

    past, held_cache, blocks = [], [], []

    def after(*numbers):
        return [blocks[d] for d in numbers] if blocks else []


    def by_rows(step, lows, query, fresh):
        first = step == 0
        (lines,) = call(
            functools.partial(up_kernel, far),
            [shape((count, 8, line))],
            "up",
            [pltpu.VMEM((count, 8, line), jnp.float32)],
        )(*lows, query, fresh, adapter, up_w)

        lines = swap(lines)
        outs = [shape((count, columns // line, line))]
        if first:
            outs = outs + [shape((H, HD), jnp.float32)] * 2
        outs = call(
            functools.partial(attend_kernel, columns, fresh_columns, first),
            outs,
            "attend",
            [
                pltpu.VMEM((count, 8, line), jnp.float32),
                pltpu.VMEM((H, key_value_cache.shape[2]), jnp.float32),
            ],
            moved=2 << 20,
        )(
            lines,
            length,
            held_cache[0],
            *past,
            specs=[vmem] * (3 + len(past)),
        )
        if first:
            past.extend(outs[1:])

        lines = swap(outs[0])
        own, away = call(
            output_kernel,
            [shape((chips, width), jnp.float32), shape((chips, width))],
            "output",
            [pltpu.VMEM((count, 8, line), jnp.float32)],
            flops=2 * count * width * columns,
            moved=2 * width * columns,
        )(lines, me, output_w, specs=[vmem, smem, vmem])
        return own, away

    hidden = hidden_state_input
    carried, length = call(
        first_kernel, [shape((1, width + LANES)), shape((8, LANES), jnp.int32)], "first"
    )(hidden, scale, row_adapter_index, cache_length_per_row, specs=[vmem, vmem, smem, smem])
    fresh_past = []
    by_halves = columns * CORES == GROUP * HD and count == CORES * KVH and fresh_columns == LANES
    for step in range(STEPS):
        first, last = step == 0, step == STEPS - 1
        low_outs = [shape((count, width))]
        if by_halves:
            low_outs = low_outs + [shape((count, LANES + fresh_columns))]
        else:
            low_outs = low_outs + [shape((count, rank)), shape((count, fresh_columns))]
        scratch = [pltpu.VMEM((count, width), jnp.float32)]
        if first:
            token = jnp.zeros((8, LANES), jnp.float32)
            arrays = [query_weight, output_weight, key_value_weight, down, adapter_up_weight]
            if by_halves:
                half = chips // 2
                cut = call(
                    functools.partial(cut_kernel, half),
                    [pltpu.VMEM((2, 2, key_value_cache.shape[2], HD), jnp.bfloat16)] * half,
                    "cut",
                    [pltpu.SemaphoreType.DMA((2 * half,))],
                    vmem=58 << 20,
                )(me, key_value_cache, specs=[smem, pl.ANY])
                blocks.extend([cut[0]] + [shift(cut[d], CORES * d, count) for d in range(1, half)])
            else:
                arrays.append(key_value_cache)
            outs, token = stash(token, arrays, 30 << 20)
            query_w, output_w, fresh_w, down_w, up_w = outs[:5]
            held_cache.append(outs[-1])
            late = carried
            if by_halves:
                (late,) = call(late_kernel, [shape(carried.shape)], "late")(carried, token)
            pieces = [carried, shift(late, near, count)]
            pieces = pieces + [shift(carried, d, count) for d in far_steps[1:]]
            (carried,) = call(
                functools.partial(join_kernel, far), [shape((far, width + LANES))], "join"
            )(*pieces, token, *after(1, 2, 3), specs=[vmem] * (far + 1) + [pl.ANY] * len(after(1, 2, 3)))
            pieces = across(carried, near_steps, count)
            member, adapter, lengths = call(
                functools.partial(member_kernel, near, far, width),
                [shape((count, kept), jnp.int32)] + [shape((count, 1), jnp.int32)] * 2,
                "member",
                [pltpu.VMEM((count, LANES), jnp.float32)],
            )(
                *pieces,
                me,
                storage,
                *after(),
                specs=[vmem] * near + [smem, vmem] + [pl.ANY] * len(after()),
            )
            if by_halves:
                (merged,) = call(
                    functools.partial(merge_kernel, half),
                    [shape((half, *cut[0].shape))],
                    "merge",
                    [pltpu.SemaphoreType.DMA((half,))],
                )(*blocks, member, specs=[pl.ANY] * (half + 1))
                blocks.append(shift(merged, 1, count))
            rows, low, *fresh = call(
                functools.partial(low_first_kernel, near, far), low_outs, "low", scratch
            )(
                *pieces,
                me,
                member,
                down_w,
                fresh_w,
                specs=[vmem] * near + [smem] + [vmem] * 3,
            )
        else:
            own = chips_swap(carried, count)
            rows, low, *fresh = call(low_later_kernel, low_outs, "low", scratch)(
                own,
                shift(own, 1, count),
                me,
                member,
                down_w,
                fresh_w,
                specs=[vmem, vmem, smem, vmem, vmem, vmem],
            )
        lows = across(low, near_steps, count)
        behind = after() if first else []
        if by_halves:
            body, dims = pack_kernel, (count, (near + 1) * LANES)
        else:
            body, dims = sum_kernel, (count, rank)
        (low,) = call(functools.partial(body, near), [shape(dims)], "sum")(
            *lows, *behind, specs=[vmem] * near + [pl.ANY] * len(behind)
        )
        lows = across(low, far_steps, count)
        (query,) = call(
            project_kernel,
            [shape((count, columns), jnp.float32)],
            "project",
            flops=2 * count * width * columns,
            moved=2 * width * columns,
        )(rows, query_w)
        if by_halves:
            some = count // 2
            rows_half = shape((some, columns))
            own, away = call(functools.partial(ask_kernel, far, rank), [rows_half] * 2, "ask")(
                *lows, query, adapter, up_w, me, specs=[vmem] * (far + 3) + [smem]
            )
            new = (step + 1, 2, 2, some, HD)
            mine, away, *fresh_past = call(
                functools.partial(halves_kernel, far, near, step + 1),
                [rows_half, rows_half, shape(new, jnp.float32)],
                "attend",
                [
                    pltpu.VMEM((2, some, 8, HD), jnp.float32),
                    pltpu.VMEM((count, count, LANES), jnp.float32),
                    pltpu.VMEM((2, some, 8, HD), jnp.float32),
                ],
                moved=4 << 20,
            )(
                own,
                shift(away, some, count),
                lengths,
                me,
                *lows,
                *fresh_past,
                *blocks,
                specs=[vmem] * 3 + [smem] + [vmem] * (far + len(fresh_past) + len(blocks)),
            )
            own, away = call(
                joined_kernel,
                [shape((chips, width), jnp.float32), shape((chips, width))],
                "output",
                flops=2 * count * width * columns,
                moved=2 * width * columns,
            )(mine, shift(away, some, count), me, output_w, specs=[vmem, vmem, smem, vmem])
        else:
            own, away = by_rows(step, lows, query, fresh[0])

        (parts,) = call(partial_kernel, [shape((chips, FOLD, width // FOLD))], "partial")(
            own, shift(away, 1, count)
        )
        parts = chips_swap(parts, count)
        outs = [shape((2 if last else 1, width))]
        if not last:
            outs = outs + [shape((chips, FOLD, width // FOLD))]
        outs = call(functools.partial(finish_kernel, last), outs, "finish")(parts, hidden, scale)
        if last:
            return outs[0].reshape(STEPS, 1, width)
        hidden, carried = outs


def solution(mesh):
    in_specs = (
        P(("groups", "replica"), None),
        P(),
        P(None, "replica"),
        P(None, "replica"),
        P("replica", None),
        P("replica", None, None),
        P(None, None, "replica"),
        P(("groups", "replica")),
        P(),
        P(("groups", "replica")),
        P(("groups", "replica"), None, None, None),
    )
    out_specs = P(None, ("groups", "replica"), None)
    return jax.shard_map(shards, mesh=mesh, in_specs=in_specs, out_specs=out_specs, check_vma=False)
```

```python
import functools
import math

import jax
import jax.numpy as jnp
from jax import lax
from jax.experimental import pallas as pl
from jax.experimental.pallas import tpu as pltpu
from jax.sharding import PartitionSpec as P

H = 64
KVH = 8
HD = 128
STEPS = 2
GROUP = H // KVH
EPS = 1e-05
AXIS = "replica"
LANES = 128
LAST = (((1,), (1,)), ((), ()))
FIRST = (((0,), (0,)), ((), ()))

CORES = 2
FOLD = 8


def split_of(count):
    far = 1 << (count.bit_length() // 2)
    return far, count // far


def shift(block, distance, count):
    return lax.ppermute(block, AXIS, [(i, i ^ distance) for i in range(count)])


def across(block, strides, count):
    return [block] + [shift(block, d, count) for d in strides]


def swap(blocks):
    return lax.all_to_all(blocks, AXIS, split_axis=0, concat_axis=0, tiled=True)


def chips_swap(blocks, count):
    groups = [[i for i in range(count) if i % CORES == c] for c in range(CORES)]
    return lax.all_to_all(
        blocks, AXIS, split_axis=0, concat_axis=0, axis_index_groups=groups, tiled=True
    )


def call(body, outs, name, scratch=(), vmem=20 << 20, flops=1 << 20, moved=1 << 18):
    def run(*operands, specs=None):
        specs = specs or [pltpu.VMEM] * len(operands)
        return pl.pallas_call(
            body,
            out_shape=outs,
            in_specs=[pl.BlockSpec(memory_space=s) for s in specs],
            out_specs=[pl.BlockSpec(memory_space=pltpu.VMEM)] * len(outs),
            scratch_shapes=list(scratch),
            compiler_params=pltpu.CompilerParams(vmem_limit_bytes=vmem),
            cost_estimate=pl.CostEstimate(flops=flops, bytes_accessed=moved, transcendentals=0),
            name=name,
        )(*operands)

    return run


def shape(dims, dtype=jnp.bfloat16):
    return jax.ShapeDtypeStruct(dims, dtype)


def iota(dims, axis):
    return lax.broadcasted_iota(jnp.int32, dims, axis)


def dot(a, b, contract=(((1,), (0,)), ((), ()))):
    return lax.dot_general(a, b, contract, preferred_element_type=jnp.float32)


def normalized(hidden, scale):
    factor = lax.rsqrt(jnp.mean(hidden * hidden, axis=-1, keepdims=True) + EPS)
    return (hidden * factor * scale).astype(jnp.bfloat16)


def row_of(ref):
    lines = ref[...].astype(jnp.float32)
    return jnp.concatenate([lines[i : i + 1] for i in range(lines.shape[0])], axis=1)


def folded(out_ref, row):
    wide = row.shape[1] // FOLD
    for k in range(out_ref.shape[0]):
        for i in range(FOLD):
            out_ref[k, i : i + 1, :wide] = row[:, i * wide : (i + 1) * wide].astype(out_ref.dtype)


def first_kernel(hidden_ref, scale_ref, adapter_ref, length_ref, out_ref, length_out):
    length_out[...] = jnp.full(length_out.shape, length_ref[0], jnp.int32)
    width = hidden_ref.shape[1]
    hidden = hidden_ref[...].astype(jnp.float32)
    out_ref[:, :width] = normalized(hidden, row_of(scale_ref))
    digit = iota((1, LANES), 1)
    adapter = adapter_ref[0]
    high, low = adapter // 256, adapter % 256
    digits = jnp.where(digit == 0, low, jnp.where(digit == 1, high, 0)).astype(jnp.float32)
    out_ref[:, width:] = digits.astype(jnp.bfloat16)


def stash_kernel(amount, token_ref, *refs):
    sources, refs = refs[:amount], refs[amount:]
    outs, out_token, sems = refs[:amount], refs[amount], refs[-1]
    copies = [
        pltpu.make_async_copy(sources[i], outs[i], sems.at[i]) for i in range(amount)
    ]
    for copy in copies:
        copy.start()
    out_token[...] = token_ref[...]
    for copy in copies:
        copy.wait()


def member_kernel(near, far, width, *refs):
    pieces, refs = refs[:near], refs[near:]
    me_ref, storage_ref, _, member_ref, adapter_ref, held = refs
    kept = member_ref.shape[1]
    count = near * far
    me = me_ref[0]
    for l in range(near):
        digits = pieces[l][:, width:].astype(jnp.float32)
        for k in range(far):
            held[pl.ds(me ^ (k * near + l), 1), :] = digits[k : k + 1]
    adapter = (held[:, 0:1] + 256.0 * held[:, 1:2]).astype(jnp.int32)
    adapter_ref[...] = adapter
    table = storage_ref.shape[1]
    chosen = jnp.where(iota((count, table), 1) == adapter, storage_ref[...], 0)
    storage = jnp.sum(chosen.astype(jnp.float32), axis=1, keepdims=True).astype(jnp.int32)
    member_ref[...] = (storage - me * kept == iota((count, kept), 1)).astype(jnp.int32)


def low_terms(held, member_ref, down_ref, rows_ref, low_ref):
    rows = held[...].astype(jnp.bfloat16)
    rows_ref[...] = rows
    low = jnp.zeros(low_ref.shape, jnp.float32)
    for index in range(down_ref.shape[0]):
        part = dot(rows, down_ref[index], LAST)
        low = jnp.where(member_ref[:, index : index + 1] > 0, part, low)
    low_ref[...] = low.astype(jnp.bfloat16)


def low_first_kernel(near, far, *refs):
    pieces, refs = refs[:near], refs[near:]
    me_ref, member_ref, down_ref, rows_ref, low_ref, held = refs
    width = held.shape[1]
    for l in range(near):
        block = pieces[l][:, :width].astype(jnp.float32)
        for k in range(far):
            held[pl.ds(me_ref[0] ^ (k * near + l), 1), :] = block[k : k + 1]
    low_terms(held, member_ref, down_ref, rows_ref, low_ref)


def low_later_kernel(own_ref, other_ref, me_ref, member_ref, down_ref, rows_ref, low_ref, held):
    core = me_ref[0] % CORES
    for ref, flip in ((own_ref, 0), (other_ref, 1)):
        wide = ref.shape[2]
        for k in range(ref.shape[0]):
            block = ref[k].astype(jnp.float32)
            row = pl.ds(k * CORES + (core ^ flip), 1)
            for i in range(FOLD):
                held[row, i * wide : (i + 1) * wide] = block[i : i + 1]
    low_terms(held, member_ref, down_ref, rows_ref, low_ref)


def join_kernel(amount, *refs):
    rows = [ref[...].astype(jnp.float32) for ref in refs[:amount]]
    refs[-1][...] = jnp.concatenate(rows, axis=0).astype(refs[-1].dtype)


def sum_kernel(*refs):
    total = refs[0][...].astype(jnp.float32)
    for ref in refs[1:-1]:
        total = total + ref[...].astype(jnp.float32)
    refs[-1][...] = total.astype(refs[-1].dtype)


def project_kernel(rows_ref, query_w, fresh_w, query_ref, fresh_ref):
    query_ref[...] = dot(rows_ref[...], query_w[...])
    fresh_ref[...] = dot(rows_ref[...], fresh_w[...])


def up_kernel(parts, *refs):
    lows, (query_ref, fresh_ref, adapter_ref, up_ref, out_ref, held) = refs[:parts], refs[parts:]
    count, columns = query_ref.shape
    rank = lows[0].shape[1]
    low = lows[0][...].astype(jnp.float32)
    for ref in lows[1:]:
        low = low + ref[...].astype(jnp.float32)
    low = low.astype(jnp.bfloat16)
    query = query_ref[...]
    table = up_ref.shape[0]
    some = min(table, 32)
    wide = some * rank
    repeat = (iota((rank, wide), 1) % rank == iota((rank, wide), 0)).astype(jnp.bfloat16)
    wide_low = dot(low, repeat)
    place = iota((count, wide), 1) // rank
    for start in range(0, table, some):
        spread = jnp.where(place + start == adapter_ref[...], wide_low, 0.0).astype(jnp.bfloat16)
        query = query + dot(spread, up_ref[start : start + some].reshape(wide, columns))
    line = out_ref.shape[2]
    lines = columns // line
    held[...] = jnp.zeros(held.shape, jnp.float32)
    for c in range(lines):
        held[:, c, :] = query[:, c * line : (c + 1) * line]
    fresh = fresh_ref[...]
    if fresh.shape[1] < line:
        fresh = jnp.concatenate(
            [fresh, jnp.zeros((count, line - fresh.shape[1]), jnp.float32)], axis=1
        )
    held[:, lines, :] = fresh
    for k in range(count):
        out_ref[k] = held[k].astype(jnp.bfloat16)


def pieces_of(lines, select, whole, size):
    if size >= whole:
        total = dot(select(len(lines), 0), lines[0])
        for c in range(1, len(lines)):
            total = total + dot(select(len(lines), c), lines[c])
        return total
    return jnp.concatenate([dot(select(0, p), lines[0]) for p in range(whole // size)], axis=1)


def attend_kernel(columns, fresh_columns, first, *refs):
    lines_ref, length_ref, cache_ref = refs[:3]
    refs = refs[3:]
    if not first:
        past, refs = refs[:2], refs[2:]
    out_ref, refs = refs[0], refs[1:]
    if first:
        keep, refs = refs[:2], refs[2:]
    held, scores = refs
    count, _, line = lines_ref.shape
    cache = cache_ref.shape[2]
    for k in range(count):
        held[k] = lines_ref[k].astype(jnp.float32)
    each = columns // line
    lines = [held[:, c, :].astype(jnp.bfloat16) for c in range(each + 1)]
    origin = iota((H, count), 1)
    head = iota((H, count), 0)

    def query_pick(each, c):
        if each:
            return (head == origin * each + c).astype(jnp.bfloat16)
        return (head * (HD // columns) + c == origin).astype(jnp.bfloat16)

    def fresh_pick(offset):
        def pick(each, c):
            want = head // GROUP + offset
            if each:
                return (want == origin * each + c).astype(jnp.bfloat16)
            return (want * (HD // fresh_columns) + c == origin).astype(jnp.bfloat16)

        return pick

    query = pieces_of(lines[:each], query_pick, HD, columns)
    fresh = [lines[each][:, :fresh_columns]]
    new = [
        (
            pieces_of(fresh, fresh_pick(0), HD, fresh_columns),
            pieces_of(fresh, fresh_pick(KVH), HD, fresh_columns),
        )
    ]
    if first:
        keep[0][...], keep[1][...] = new[0]
    else:
        new.insert(0, (past[0][...], past[1][...]))
    scale = 1.0 / math.sqrt(HD)
    for j in range(KVH):
        rows = slice(j * GROUP, (j + 1) * GROUP)
        scores[rows, :] = dot(
            query[rows].astype(jnp.bfloat16), cache_ref[0, 0, :, j * HD : (j + 1) * HD], LAST
        )
    in_cache = iota((H, cache), 1) < length_ref[0:1, 0:1]
    old = jnp.where(in_cache, scores[...] * scale, -jnp.inf)
    news = [jnp.sum(query * keys, axis=1, keepdims=True) * scale for keys, _ in new]
    peak = jnp.max(old, axis=1, keepdims=True)
    for score in news:
        peak = jnp.maximum(peak, score)
    old = jnp.exp(old - peak)
    news = [jnp.exp(score - peak) for score in news]
    total = jnp.sum(old, axis=1, keepdims=True)
    for score in news:
        total = total + score
    old = old / total
    extra = jnp.zeros((H, HD), jnp.float32)
    for score, (_, values) in zip(news, new):
        extra = extra + (score / total).astype(jnp.bfloat16).astype(jnp.float32) * values
    mixed = jnp.concatenate(
        [
            dot(
                old[j * GROUP : (j + 1) * GROUP].astype(jnp.bfloat16),
                cache_ref[0, 1, :, j * HD : (j + 1) * HD],
            )
            for j in range(KVH)
        ],
        axis=0,
    )
    mixed = mixed + extra
    if columns >= HD:
        for k in range(count):
            out_ref[k] = mixed[k * each : (k + 1) * each].astype(jnp.bfloat16)
    else:
        parts = HD // columns
        out = jnp.zeros((count, columns), jnp.float32)
        for p in range(parts):
            pick = (iota((count, H), 1) * parts + p == iota((count, H), 0)).astype(jnp.bfloat16)
            out = out + dot(pick, mixed[:, p * columns : (p + 1) * columns].astype(jnp.bfloat16))
        for k in range(count):
            out_ref[k] = out[k : k + 1].astype(jnp.bfloat16)


def output_kernel(lines_ref, me_ref, weight_ref, own_ref, away_ref, held):
    count, each, line = lines_ref.shape
    chips = count // CORES
    for k in range(count):
        held[k, :each, :] = lines_ref[k].astype(jnp.float32)
    slot = iota((count, count), 0)
    origin = (slot % chips) * CORES + ((me_ref[0] % CORES) ^ (slot // chips))
    order = (iota((count, count), 1) == origin).astype(jnp.bfloat16)
    rows = jnp.concatenate(
        [dot(order, held[:, c, :].astype(jnp.bfloat16)).astype(jnp.bfloat16) for c in range(each)],
        axis=1,
    )
    width = weight_ref.shape[1]
    wide = width // 8
    for c in range(8):
        part = slice(c * wide, (c + 1) * wide)
        out = dot(rows, weight_ref[:, part])
        own_ref[:, part] = out[:chips]
        away_ref[:, part] = out[chips:].astype(jnp.bfloat16)


def partial_kernel(own_ref, other_ref, out_ref):
    total = own_ref[...] + other_ref[...].astype(jnp.float32)
    wide = out_ref.shape[2]
    for k in range(out_ref.shape[0]):
        for i in range(FOLD):
            out_ref[k, i : i + 1, :] = total[k : k + 1, i * wide : (i + 1) * wide].astype(
                out_ref.dtype
            )


def finish_kernel(last, parts_ref, hidden_ref, scale_ref, out_ref, *spread):
    total = parts_ref[0].astype(jnp.float32)
    for k in range(1, parts_ref.shape[0]):
        total = total + parts_ref[k].astype(jnp.float32)
    total = jnp.concatenate([total[i : i + 1] for i in range(FOLD)], axis=1)
    total = total.astype(jnp.bfloat16).astype(jnp.float32)
    before = hidden_ref[...].astype(jnp.float32)
    hidden = (before + total).astype(jnp.bfloat16).astype(jnp.float32)
    if last:
        out_ref[...] = jnp.concatenate([before, hidden], axis=0).astype(jnp.bfloat16)
    else:
        out_ref[...] = hidden.astype(jnp.bfloat16)
        folded(spread[0], normalized(hidden, row_of(scale_ref)).astype(jnp.float32))


def shards(
    hidden_state_input,
    attention_norm_scale,
    query_weight,
    key_value_weight,
    output_weight,
    adapter_down_weight,
    adapter_up_weight,
    row_adapter_index,
    adapter_storage_index,
    cache_length_per_row,
    key_value_cache,
):
    count = lax.axis_size(AXIS)
    chips = count // CORES
    far, near = split_of(count)
    far_steps = [k * near for k in range(1, far)]
    near_steps = list(range(1, near))
    kept, width, rank = adapter_down_weight.shape
    columns = query_weight.shape[1]
    fresh_columns = key_value_weight.shape[1]
    line = min(HD, columns)
    smem, vmem = pltpu.SMEM, pltpu.VMEM
    me = lax.axis_index(AXIS).astype(jnp.int32).reshape(1)
    down = adapter_down_weight.transpose(0, 2, 1)
    scale = attention_norm_scale.reshape(-1, LANES)
    storage = adapter_storage_index[None]

    def stash(token, arrays):
        outs = call(
            functools.partial(stash_kernel, len(arrays)),
            [pltpu.VMEM(a.shape, a.dtype) for a in arrays] + [shape((8, LANES), jnp.int32)],
            "stash",
            [pltpu.SemaphoreType.DMA((len(arrays),))],
            moved=sum(2 * a.size for a in arrays),
        )(
            token,
            *(pltpu.with_memory_space_constraint(a, pltpu.HBM) for a in arrays),
            specs=[vmem] + [pltpu.HBM] * len(arrays),
        )
        return outs[:-1], outs[-1]

    hidden = hidden_state_input
    carried, length = call(
        first_kernel, [shape((1, width + LANES)), shape((8, LANES), jnp.int32)], "first"
    )(hidden, scale, row_adapter_index, cache_length_per_row, specs=[vmem, vmem, smem, smem])
    past = ()
    for step in range(STEPS):
        first, last = step == 0, step == STEPS - 1
        outs = [shape((count, width)), shape((count, rank))]
        scratch = [pltpu.VMEM((count, width), jnp.float32)]
        if first:
            early = [query_weight, key_value_weight, down]
            (query_w, fresh_w, down_w), token = stash(length, early)
            pieces = across(carried, far_steps, count)
            (carried,) = call(
                functools.partial(join_kernel, far), [shape((far, width + LANES))], "join"
            )(*pieces, token)
            later = [output_weight, key_value_cache, adapter_up_weight]
            (output_w, cache, up_w), token = stash(token, later)
            pieces = across(carried, near_steps, count)
            member, adapter = call(
                functools.partial(member_kernel, near, far, width),
                [shape((count, kept), jnp.int32), shape((count, 1), jnp.int32)],
                "member",
                [pltpu.VMEM((count, LANES), jnp.float32)],
            )(*pieces, me, storage, token, specs=[vmem] * near + [smem, vmem, vmem])
            rows, low = call(
                functools.partial(low_first_kernel, near, far), outs, "low", scratch
            )(*pieces, me, member, down_w, specs=[vmem] * near + [smem, vmem, vmem])
        else:
            own = chips_swap(carried, count)
            rows, low = call(low_later_kernel, outs, "low", scratch)(
                own, shift(own, 1, count), me, member, down_w, specs=[vmem, vmem, smem, vmem, vmem]
            )
        (low,) = call(sum_kernel, [shape((count, rank))], "sum")(*across(low, near_steps, count))
        lows = across(low, far_steps, count)
        query, fresh = call(
            project_kernel,
            [shape((count, columns), jnp.float32), shape((count, fresh_columns), jnp.float32)],
            "project",
            flops=2 * count * width * (columns + fresh_columns),
            moved=2 * width * (columns + fresh_columns),
        )(rows, query_w, fresh_w)
        (lines,) = call(
            functools.partial(up_kernel, far),
            [shape((count, 8, line))],
            "up",
            [pltpu.VMEM((count, 8, line), jnp.float32)],
        )(*lows, query, fresh, adapter, up_w)

        lines = swap(lines)
        outs = [shape((count, columns // line, line))]
        if first:
            outs = outs + [shape((H, HD), jnp.float32)] * 2
        outs = call(
            functools.partial(attend_kernel, columns, fresh_columns, first),
            outs,
            "attend",
            [
                pltpu.VMEM((count, 8, line), jnp.float32),
                pltpu.VMEM((H, key_value_cache.shape[2]), jnp.float32),
            ],
            moved=2 << 20,
        )(
            lines,
            length,
            cache,
            *past,
            specs=[vmem] * (3 + len(past)),
        )
        if first:
            past = tuple(outs[1:])

        lines = swap(outs[0])
        own, away = call(
            output_kernel,
            [shape((chips, width), jnp.float32), shape((chips, width))],
            "output",
            [pltpu.VMEM((count, 8, line), jnp.float32)],
            flops=2 * count * width * columns,
            moved=2 * width * columns,
        )(lines, me, output_w, specs=[vmem, smem, vmem])

        (parts,) = call(partial_kernel, [shape((chips, FOLD, width // FOLD))], "partial")(
            own, shift(away, 1, count)
        )
        parts = chips_swap(parts, count)
        outs = [shape((2 if last else 1, width))]
        if not last:
            outs = outs + [shape((chips, FOLD, width // FOLD))]
        outs = call(functools.partial(finish_kernel, last), outs, "finish")(parts, hidden, scale)
        if last:
            return outs[0].reshape(STEPS, 1, width)
        hidden, carried = outs


def solution(mesh):
    in_specs = (
        P(("groups", "replica"), None),
        P(),
        P(None, "replica"),
        P(None, "replica"),
        P("replica", None),
        P("replica", None, None),
        P(None, None, "replica"),
        P(("groups", "replica")),
        P(),
        P(("groups", "replica")),
        P(("groups", "replica"), None, None, None),
    )
    out_specs = P(None, ("groups", "replica"), None)
    return jax.shard_map(shards, mesh=mesh, in_specs=in_specs, out_specs=out_specs, check_vma=False)
```

```python
import functools
import math

import jax
import jax.numpy as jnp
from jax import lax
from jax.experimental import pallas as pl
from jax.experimental.pallas import tpu as pltpu
from jax.sharding import PartitionSpec as P

H = 64
KVH = 8
HD = 128
STEPS = 2
GROUP = H // KVH
EPS = 1e-05
AXIS = "replica"
LANES = 128
LAST = (((1,), (1,)), ((), ()))
FIRST = (((0,), (0,)), ((), ()))

CORES = 2
FOLD = 8


def split_of(count):
    far = 1 << (count.bit_length() // 2)
    return far, count // far


def shift(block, distance, count):
    return lax.ppermute(block, AXIS, [(i, i ^ distance) for i in range(count)])


def across(block, strides, count):
    return [block] + [shift(block, d, count) for d in strides]


def swap(blocks):
    return lax.all_to_all(blocks, AXIS, split_axis=0, concat_axis=0, tiled=True)


def chips_swap(blocks, count):
    groups = [[i for i in range(count) if i % CORES == c] for c in range(CORES)]
    return lax.all_to_all(
        blocks, AXIS, split_axis=0, concat_axis=0, axis_index_groups=groups, tiled=True
    )


def call(body, outs, name, scratch=(), vmem=20 << 20, flops=1 << 20, moved=1 << 18):
    def run(*operands, specs=None):
        specs = specs or [pltpu.VMEM] * len(operands)
        return pl.pallas_call(
            body,
            out_shape=outs,
            in_specs=[pl.BlockSpec(memory_space=s) for s in specs],
            out_specs=[pl.BlockSpec(memory_space=pltpu.VMEM)] * len(outs),
            scratch_shapes=list(scratch),
            compiler_params=pltpu.CompilerParams(vmem_limit_bytes=vmem),
            cost_estimate=pl.CostEstimate(flops=flops, bytes_accessed=moved, transcendentals=0),
            name=name,
        )(*operands)

    return run


def shape(dims, dtype=jnp.bfloat16):
    return jax.ShapeDtypeStruct(dims, dtype)


def iota(dims, axis):
    return lax.broadcasted_iota(jnp.int32, dims, axis)


def dot(a, b, contract=(((1,), (0,)), ((), ()))):
    return lax.dot_general(a, b, contract, preferred_element_type=jnp.float32)


def normalized(hidden, scale):
    factor = lax.rsqrt(jnp.mean(hidden * hidden, axis=-1, keepdims=True) + EPS)
    return (hidden * factor * scale).astype(jnp.bfloat16)


def row_of(ref):
    lines = ref[...].astype(jnp.float32)
    return jnp.concatenate([lines[i : i + 1] for i in range(lines.shape[0])], axis=1)


def folded(out_ref, row):
    wide = row.shape[1] // FOLD
    for k in range(out_ref.shape[0]):
        for i in range(FOLD):
            out_ref[k, i : i + 1, :wide] = row[:, i * wide : (i + 1) * wide].astype(out_ref.dtype)


def first_kernel(hidden_ref, scale_ref, adapter_ref, length_ref, _, out_ref, length_out):
    length_out[...] = jnp.full(length_out.shape, length_ref[0], jnp.int32)
    width = hidden_ref.shape[1]
    hidden = hidden_ref[...].astype(jnp.float32)
    out_ref[:, :width] = normalized(hidden, row_of(scale_ref))
    digit = iota((1, LANES), 1)
    adapter = adapter_ref[0]
    high, low = adapter // 256, adapter % 256
    digits = jnp.where(digit == 0, low, jnp.where(digit == 1, high, 0)).astype(jnp.float32)
    out_ref[:, width:] = digits.astype(jnp.bfloat16)


def stash_kernel(amount, token_ref, *refs):
    sources, refs = refs[:amount], refs[amount:]
    outs, out_token, sems = refs[:amount], refs[amount], refs[-1]
    copies = [
        pltpu.make_async_copy(sources[i], outs[i], sems.at[i]) for i in range(amount)
    ]
    for copy in copies:
        copy.start()
    out_token[...] = token_ref[...]
    for copy in copies:
        copy.wait()


def member_kernel(near, far, width, *refs):
    pieces, refs = refs[:near], refs[near:]
    me_ref, storage_ref, _, member_ref, adapter_ref, held = refs
    kept = member_ref.shape[1]
    count = near * far
    me = me_ref[0]
    for l in range(near):
        digits = pieces[l][:, width:].astype(jnp.float32)
        for k in range(far):
            held[pl.ds(me ^ (k * near + l), 1), :] = digits[k : k + 1]
    adapter = (held[:, 0:1] + 256.0 * held[:, 1:2]).astype(jnp.int32)
    adapter_ref[...] = adapter
    table = storage_ref.shape[1]
    chosen = jnp.where(iota((count, table), 1) == adapter, storage_ref[...], 0)
    storage = jnp.sum(chosen.astype(jnp.float32), axis=1, keepdims=True).astype(jnp.int32)
    member_ref[...] = (storage - me * kept == iota((count, kept), 1)).astype(jnp.int32)


def low_terms(held, member_ref, down_ref, rows_ref, low_ref):
    rows = held[...].astype(jnp.bfloat16)
    rows_ref[...] = rows
    low = jnp.zeros(low_ref.shape, jnp.float32)
    for index in range(down_ref.shape[0]):
        part = dot(rows, down_ref[index], LAST)
        low = jnp.where(member_ref[:, index : index + 1] > 0, part, low)
    low_ref[...] = low.astype(jnp.bfloat16)


def low_first_kernel(near, far, *refs):
    pieces, refs = refs[:near], refs[near:]
    me_ref, member_ref, down_ref, rows_ref, low_ref, held = refs
    width = held.shape[1]
    for l in range(near):
        block = pieces[l][:, :width].astype(jnp.float32)
        for k in range(far):
            held[pl.ds(me_ref[0] ^ (k * near + l), 1), :] = block[k : k + 1]
    low_terms(held, member_ref, down_ref, rows_ref, low_ref)


def low_later_kernel(own_ref, other_ref, me_ref, member_ref, down_ref, rows_ref, low_ref, held):
    core = me_ref[0] % CORES
    for ref, flip in ((own_ref, 0), (other_ref, 1)):
        wide = ref.shape[2]
        for k in range(ref.shape[0]):
            block = ref[k].astype(jnp.float32)
            row = pl.ds(k * CORES + (core ^ flip), 1)
            for i in range(FOLD):
                held[row, i * wide : (i + 1) * wide] = block[i : i + 1]
    low_terms(held, member_ref, down_ref, rows_ref, low_ref)


def join_kernel(amount, *refs):
    rows = [ref[...].astype(jnp.float32) for ref in refs[:amount]]
    refs[-1][...] = jnp.concatenate(rows, axis=0).astype(refs[-1].dtype)


def sum_kernel(*refs):
    total = refs[0][...].astype(jnp.float32)
    for ref in refs[1:-1]:
        total = total + ref[...].astype(jnp.float32)
    refs[-1][...] = total.astype(refs[-1].dtype)


def project_kernel(rows_ref, query_w, fresh_w, query_ref, fresh_ref):
    query_ref[...] = dot(rows_ref[...], query_w[...])
    fresh_ref[...] = dot(rows_ref[...], fresh_w[...])


def up_kernel(parts, *refs):
    lows, (query_ref, fresh_ref, adapter_ref, up_ref, out_ref, held) = refs[:parts], refs[parts:]
    count, columns = query_ref.shape
    rank = lows[0].shape[1]
    low = lows[0][...].astype(jnp.float32)
    for ref in lows[1:]:
        low = low + ref[...].astype(jnp.float32)
    low = low.astype(jnp.bfloat16)
    query = query_ref[...]
    table = up_ref.shape[0]
    some = min(table, 32)
    wide = some * rank
    repeat = (iota((rank, wide), 1) % rank == iota((rank, wide), 0)).astype(jnp.bfloat16)
    wide_low = dot(low, repeat)
    place = iota((count, wide), 1) // rank
    for start in range(0, table, some):
        spread = jnp.where(place + start == adapter_ref[...], wide_low, 0.0).astype(jnp.bfloat16)
        query = query + dot(spread, up_ref[start : start + some].reshape(wide, columns))
    line = out_ref.shape[2]
    lines = columns // line
    held[...] = jnp.zeros(held.shape, jnp.float32)
    for c in range(lines):
        held[:, c, :] = query[:, c * line : (c + 1) * line]
    fresh = fresh_ref[...]
    if fresh.shape[1] < line:
        fresh = jnp.concatenate(
            [fresh, jnp.zeros((count, line - fresh.shape[1]), jnp.float32)], axis=1
        )
    held[:, lines, :] = fresh
    for k in range(count):
        out_ref[k] = held[k].astype(jnp.bfloat16)


def pieces_of(lines, select, whole, size):
    if size >= whole:
        total = dot(select(len(lines), 0), lines[0])
        for c in range(1, len(lines)):
            total = total + dot(select(len(lines), c), lines[c])
        return total
    return jnp.concatenate([dot(select(0, p), lines[0]) for p in range(whole // size)], axis=1)


def attend_kernel(columns, fresh_columns, first, *refs):
    lines_ref, length_ref, cache_ref = refs[:3]
    refs = refs[3:]
    if not first:
        past, refs = refs[:2], refs[2:]
    out_ref, refs = refs[0], refs[1:]
    if first:
        keep, refs = refs[:2], refs[2:]
    held, scores = refs
    count, _, line = lines_ref.shape
    cache = cache_ref.shape[2]
    for k in range(count):
        held[k] = lines_ref[k].astype(jnp.float32)
    each = columns // line
    lines = [held[:, c, :].astype(jnp.bfloat16) for c in range(each + 1)]
    origin = iota((H, count), 1)
    head = iota((H, count), 0)

    def query_pick(each, c):
        if each:
            return (head == origin * each + c).astype(jnp.bfloat16)
        return (head * (HD // columns) + c == origin).astype(jnp.bfloat16)

    def fresh_pick(offset):
        def pick(each, c):
            want = head // GROUP + offset
            if each:
                return (want == origin * each + c).astype(jnp.bfloat16)
            return (want * (HD // fresh_columns) + c == origin).astype(jnp.bfloat16)

        return pick

    query = pieces_of(lines[:each], query_pick, HD, columns)
    fresh = [lines[each][:, :fresh_columns]]
    new = [
        (
            pieces_of(fresh, fresh_pick(0), HD, fresh_columns),
            pieces_of(fresh, fresh_pick(KVH), HD, fresh_columns),
        )
    ]
    if first:
        keep[0][...], keep[1][...] = new[0]
    else:
        new.insert(0, (past[0][...], past[1][...]))
    scale = 1.0 / math.sqrt(HD)
    for j in range(KVH):
        rows = slice(j * GROUP, (j + 1) * GROUP)
        scores[rows, :] = dot(
            query[rows].astype(jnp.bfloat16), cache_ref[0, 0, :, j * HD : (j + 1) * HD], LAST
        )
    in_cache = iota((H, cache), 1) < length_ref[0:1, 0:1]
    old = jnp.where(in_cache, scores[...] * scale, -jnp.inf)
    news = [jnp.sum(query * keys, axis=1, keepdims=True) * scale for keys, _ in new]
    peak = jnp.max(old, axis=1, keepdims=True)
    for score in news:
        peak = jnp.maximum(peak, score)
    old = jnp.exp(old - peak)
    news = [jnp.exp(score - peak) for score in news]
    total = jnp.sum(old, axis=1, keepdims=True)
    for score in news:
        total = total + score
    old = old / total
    extra = jnp.zeros((H, HD), jnp.float32)
    for score, (_, values) in zip(news, new):
        extra = extra + (score / total).astype(jnp.bfloat16).astype(jnp.float32) * values
    mixed = jnp.concatenate(
        [
            dot(
                old[j * GROUP : (j + 1) * GROUP].astype(jnp.bfloat16),
                cache_ref[0, 1, :, j * HD : (j + 1) * HD],
            )
            for j in range(KVH)
        ],
        axis=0,
    )
    mixed = mixed + extra
    if columns >= HD:
        for k in range(count):
            out_ref[k] = mixed[k * each : (k + 1) * each].astype(jnp.bfloat16)
    else:
        parts = HD // columns
        out = jnp.zeros((count, columns), jnp.float32)
        for p in range(parts):
            pick = (iota((count, H), 1) * parts + p == iota((count, H), 0)).astype(jnp.bfloat16)
            out = out + dot(pick, mixed[:, p * columns : (p + 1) * columns].astype(jnp.bfloat16))
        for k in range(count):
            out_ref[k] = out[k : k + 1].astype(jnp.bfloat16)


def output_kernel(lines_ref, me_ref, weight_ref, own_ref, away_ref, held):
    count, each, line = lines_ref.shape
    chips = count // CORES
    for k in range(count):
        held[k, :each, :] = lines_ref[k].astype(jnp.float32)
    slot = iota((count, count), 0)
    origin = (slot % chips) * CORES + ((me_ref[0] % CORES) ^ (slot // chips))
    order = (iota((count, count), 1) == origin).astype(jnp.bfloat16)
    rows = jnp.concatenate(
        [dot(order, held[:, c, :].astype(jnp.bfloat16)).astype(jnp.bfloat16) for c in range(each)],
        axis=1,
    )
    width = weight_ref.shape[1]
    wide = width // 8
    for c in range(8):
        part = slice(c * wide, (c + 1) * wide)
        out = dot(rows, weight_ref[:, part])
        own_ref[:, part] = out[:chips]
        away_ref[:, part] = out[chips:].astype(jnp.bfloat16)


def partial_kernel(own_ref, other_ref, out_ref):
    total = own_ref[...] + other_ref[...].astype(jnp.float32)
    wide = out_ref.shape[2]
    for k in range(out_ref.shape[0]):
        for i in range(FOLD):
            out_ref[k, i : i + 1, :] = total[k : k + 1, i * wide : (i + 1) * wide].astype(
                out_ref.dtype
            )


def finish_kernel(last, parts_ref, hidden_ref, scale_ref, out_ref, *spread):
    total = parts_ref[0].astype(jnp.float32)
    for k in range(1, parts_ref.shape[0]):
        total = total + parts_ref[k].astype(jnp.float32)
    total = jnp.concatenate([total[i : i + 1] for i in range(FOLD)], axis=1)
    total = total.astype(jnp.bfloat16).astype(jnp.float32)
    before = hidden_ref[...].astype(jnp.float32)
    hidden = (before + total).astype(jnp.bfloat16).astype(jnp.float32)
    if last:
        out_ref[...] = jnp.concatenate([before, hidden], axis=0).astype(jnp.bfloat16)
    else:
        out_ref[...] = hidden.astype(jnp.bfloat16)
        folded(spread[0], normalized(hidden, row_of(scale_ref)).astype(jnp.float32))


def shards(
    hidden_state_input,
    attention_norm_scale,
    query_weight,
    key_value_weight,
    output_weight,
    adapter_down_weight,
    adapter_up_weight,
    row_adapter_index,
    adapter_storage_index,
    cache_length_per_row,
    key_value_cache,
):
    count = lax.axis_size(AXIS)
    chips = count // CORES
    far, near = split_of(count)
    far_steps = [k * near for k in range(1, far)]
    near_steps = list(range(1, near))
    kept, width, rank = adapter_down_weight.shape
    columns = query_weight.shape[1]
    fresh_columns = key_value_weight.shape[1]
    line = min(HD, columns)
    smem, vmem = pltpu.SMEM, pltpu.VMEM
    me = lax.axis_index(AXIS).astype(jnp.int32).reshape(1)
    down = adapter_down_weight.transpose(0, 2, 1)
    scale = attention_norm_scale.reshape(-1, LANES)
    storage = adapter_storage_index[None]

    def stash(token, arrays):
        outs = call(
            functools.partial(stash_kernel, len(arrays)),
            [pltpu.VMEM(a.shape, a.dtype) for a in arrays] + [shape((8, LANES), jnp.int32)],
            "stash",
            [pltpu.SemaphoreType.DMA((len(arrays),))],
            moved=sum(2 * a.size for a in arrays),
        )(
            token,
            *(pltpu.with_memory_space_constraint(a, pltpu.HBM) for a in arrays),
            specs=[vmem] + [pltpu.HBM] * len(arrays),
        )
        return outs[:-1], outs[-1]

    hidden = hidden_state_input
    carried, length = call(
        first_kernel, [shape((1, width + LANES)), shape((8, LANES), jnp.int32)], "first"
    )(
        hidden,
        scale,
        row_adapter_index,
        cache_length_per_row,
        me,
        specs=[vmem, vmem, smem, smem, smem],
    )
    past = ()
    for step in range(STEPS):
        first, last = step == 0, step == STEPS - 1
        outs = [shape((count, width)), shape((count, rank))]
        scratch = [pltpu.VMEM((count, width), jnp.float32)]
        if first:
            early = [query_weight, key_value_weight, down]
            (query_w, fresh_w, down_w), token = stash(length, early)
            pieces = across(carried, far_steps, count)
            (carried,) = call(
                functools.partial(join_kernel, far), [shape((far, width + LANES))], "join"
            )(*pieces, token)
            later = [output_weight, key_value_cache, adapter_up_weight]
            (output_w, cache, up_w), token = stash(token, later)
            pieces = across(carried, near_steps, count)
            member, adapter = call(
                functools.partial(member_kernel, near, far, width),
                [shape((count, kept), jnp.int32), shape((count, 1), jnp.int32)],
                "member",
                [pltpu.VMEM((count, LANES), jnp.float32)],
            )(*pieces, me, storage, token, specs=[vmem] * near + [smem, vmem, vmem])
            rows, low = call(
                functools.partial(low_first_kernel, near, far), outs, "low", scratch
            )(*pieces, me, member, down_w, specs=[vmem] * near + [smem, vmem, vmem])
        else:
            own = chips_swap(carried, count)
            rows, low = call(low_later_kernel, outs, "low", scratch)(
                own, shift(own, 1, count), me, member, down_w, specs=[vmem, vmem, smem, vmem, vmem]
            )
        (low,) = call(sum_kernel, [shape((count, rank))], "sum")(*across(low, near_steps, count))
        lows = across(low, far_steps, count)
        query, fresh = call(
            project_kernel,
            [shape((count, columns), jnp.float32), shape((count, fresh_columns), jnp.float32)],
            "project",
            flops=2 * count * width * (columns + fresh_columns),
            moved=2 * width * (columns + fresh_columns),
        )(rows, query_w, fresh_w)
        (lines,) = call(
            functools.partial(up_kernel, far),
            [shape((count, 8, line))],
            "up",
            [pltpu.VMEM((count, 8, line), jnp.float32)],
        )(*lows, query, fresh, adapter, up_w)

        lines = swap(lines)
        outs = [shape((count, columns // line, line))]
        if first:
            outs = outs + [shape((H, HD), jnp.float32)] * 2
        outs = call(
            functools.partial(attend_kernel, columns, fresh_columns, first),
            outs,
            "attend",
            [
                pltpu.VMEM((count, 8, line), jnp.float32),
                pltpu.VMEM((H, key_value_cache.shape[2]), jnp.float32),
            ],
            moved=2 << 20,
        )(
            lines,
            length,
            cache,
            *past,
            specs=[vmem] * (3 + len(past)),
        )
        if first:
            past = tuple(outs[1:])

        lines = swap(outs[0])
        own, away = call(
            output_kernel,
            [shape((chips, width), jnp.float32), shape((chips, width))],
            "output",
            [pltpu.VMEM((count, 8, line), jnp.float32)],
            flops=2 * count * width * columns,
            moved=2 * width * columns,
        )(lines, me, output_w, specs=[vmem, smem, vmem])

        (parts,) = call(partial_kernel, [shape((chips, FOLD, width // FOLD))], "partial")(
            own, shift(away, 1, count)
        )
        parts = chips_swap(parts, count)
        outs = [shape((2 if last else 1, width))]
        if not last:
            outs = outs + [shape((chips, FOLD, width // FOLD))]
        outs = call(functools.partial(finish_kernel, last), outs, "finish")(parts, hidden, scale)
        if last:
            return outs[0].reshape(STEPS, 1, width)
        hidden, carried = outs


def solution(mesh):
    in_specs = (
        P(("groups", "replica"), None),
        P(),
        P(None, "replica"),
        P(None, "replica"),
        P("replica", None),
        P("replica", None, None),
        P(None, None, "replica"),
        P(("groups", "replica")),
        P(),
        P(("groups", "replica")),
        P(("groups", "replica"), None, None, None),
    )
    out_specs = P(None, ("groups", "replica"), None)
    return jax.shard_map(shards, mesh=mesh, in_specs=in_specs, out_specs=out_specs, check_vma=False)
```

```python
import functools
import math

import jax
import jax.numpy as jnp
from jax import lax
from jax.experimental import pallas as pl
from jax.experimental.pallas import tpu as pltpu
from jax.sharding import PartitionSpec as P

H = 64
KVH = 8
HD = 128
STEPS = 2
GROUP = H // KVH
EPS = 1e-05
AXIS = "replica"
LANES = 128
LAST = (((1,), (1,)), ((), ()))
FIRST = (((0,), (0,)), ((), ()))

CORES = 2
FOLD = 8


def split_of(count):
    far = 1 << (count.bit_length() // 2)
    return far, count // far


def shift(block, distance, count):
    return lax.ppermute(block, AXIS, [(i, i ^ distance) for i in range(count)])


def across(block, strides, count):
    return [block] + [shift(block, d, count) for d in strides]


def swap(blocks):
    return lax.all_to_all(blocks, AXIS, split_axis=0, concat_axis=0, tiled=True)


def chips_swap(blocks, count):
    groups = [[i for i in range(count) if i % CORES == c] for c in range(CORES)]
    return lax.all_to_all(
        blocks, AXIS, split_axis=0, concat_axis=0, axis_index_groups=groups, tiled=True
    )


def call(body, outs, name, scratch=(), vmem=20 << 20, flops=1 << 20, moved=1 << 18):
    def run(*operands, specs=None):
        specs = specs or [pltpu.VMEM] * len(operands)
        return pl.pallas_call(
            body,
            out_shape=outs,
            in_specs=[pl.BlockSpec(memory_space=s) for s in specs],
            out_specs=[pl.BlockSpec(memory_space=pltpu.VMEM)] * len(outs),
            scratch_shapes=list(scratch),
            compiler_params=pltpu.CompilerParams(vmem_limit_bytes=vmem),
            cost_estimate=pl.CostEstimate(flops=flops, bytes_accessed=moved, transcendentals=0),
            name=name,
        )(*operands)

    return run


def shape(dims, dtype=jnp.bfloat16):
    return jax.ShapeDtypeStruct(dims, dtype)


def iota(dims, axis):
    return lax.broadcasted_iota(jnp.int32, dims, axis)


def dot(a, b, contract=(((1,), (0,)), ((), ()))):
    return lax.dot_general(a, b, contract, preferred_element_type=jnp.float32)


def normalized(hidden, scale):
    factor = lax.rsqrt(jnp.mean(hidden * hidden, axis=-1, keepdims=True) + EPS)
    return (hidden * factor * scale).astype(jnp.bfloat16)


def row_of(ref):
    lines = ref[...].astype(jnp.float32)
    return jnp.concatenate([lines[i : i + 1] for i in range(lines.shape[0])], axis=1)


def folded(out_ref, row):
    wide = row.shape[1] // FOLD
    for k in range(out_ref.shape[0]):
        for i in range(FOLD):
            out_ref[k, i : i + 1, :wide] = row[:, i * wide : (i + 1) * wide].astype(out_ref.dtype)


def first_kernel(hidden_ref, scale_ref, adapter_ref, length_ref, _, out_ref, length_out):
    length_out[...] = jnp.full(length_out.shape, length_ref[0], jnp.int32)
    width = hidden_ref.shape[1]
    hidden = hidden_ref[...].astype(jnp.float32)
    out_ref[:, :width] = normalized(hidden, row_of(scale_ref))
    digit = iota((1, LANES), 1)
    adapter = adapter_ref[0]
    length = length_ref[0]
    digits = jnp.where(digit == 0, adapter % 256, jnp.where(digit == 1, adapter // 256, 0))
    digits = jnp.where(digit == 2, length % 256, jnp.where(digit == 3, length // 256, digits))
    digits = digits.astype(jnp.float32)
    out_ref[:, width:] = digits.astype(jnp.bfloat16)


def stash_kernel(amount, token_ref, *refs):
    sources, refs = refs[:amount], refs[amount:]
    outs, out_token, sems = refs[:amount], refs[amount], refs[-1]
    copies = [
        pltpu.make_async_copy(sources[i], outs[i], sems.at[i]) for i in range(amount)
    ]
    for copy in copies:
        copy.start()
    out_token[...] = token_ref[...]
    for copy in copies:
        copy.wait()


def member_kernel(near, far, width, strides, *refs):
    amount = far if strides[0] > 1 else near
    pieces, (me_ref, storage_ref) = refs[:amount], refs[amount : amount + 2]
    member_ref, adapter_ref, lengths_ref, held = refs[-4:]
    kept = member_ref.shape[1]
    count = near * far
    me = me_ref[0]
    for l, piece in enumerate(pieces):
        digits = piece[:, width:].astype(jnp.float32)
        for k in range(digits.shape[0]):
            held[pl.ds(me ^ (l * strides[0] + k * strides[1]), 1), :] = digits[k : k + 1]
    adapter = (held[:, 0:1] + 256.0 * held[:, 1:2]).astype(jnp.int32)
    adapter_ref[...] = adapter
    lengths_ref[...] = (held[:, 2:3] + 256.0 * held[:, 3:4]).astype(jnp.int32)
    table = storage_ref.shape[1]
    chosen = jnp.where(iota((count, table), 1) == adapter, storage_ref[...], 0)
    storage = jnp.sum(chosen.astype(jnp.float32), axis=1, keepdims=True).astype(jnp.int32)
    member_ref[...] = (storage - me * kept == iota((count, kept), 1)).astype(jnp.int32)


def low_terms(held, member_ref, down_ref, fresh_w, rows_ref, *outs):
    rows = held[...].astype(jnp.bfloat16)
    rows_ref[...] = rows
    rank = down_ref.shape[1]
    low = jnp.zeros((rows.shape[0], rank), jnp.float32)
    for index in range(down_ref.shape[0]):
        part = dot(rows, down_ref[index], LAST)
        low = jnp.where(member_ref[:, index : index + 1] > 0, part, low)
    fresh = dot(rows, fresh_w[...]).astype(jnp.bfloat16)
    if len(outs) == 2:
        outs[0][...] = low.astype(jnp.bfloat16)
        outs[1][...] = fresh
    else:
        outs[0][:, :rank] = low.astype(jnp.bfloat16)
        outs[0][:, rank:LANES] = jnp.zeros((rows.shape[0], LANES - rank), jnp.bfloat16)
        outs[0][:, LANES:] = fresh


def low_first_kernel(amount, strides, *refs):
    pieces, (me_ref, member_ref, down_ref, fresh_w) = refs[:amount], refs[amount : amount + 4]
    outs, held = refs[amount + 4 : -1], refs[-1]
    width = held.shape[1]
    for l, piece in enumerate(pieces):
        block = piece[:, :width].astype(jnp.float32)
        for k in range(block.shape[0]):
            held[pl.ds(me_ref[0] ^ (l * strides[0] + k * strides[1]), 1), :] = block[k : k + 1]
    low_terms(held, member_ref, down_ref, fresh_w, *outs)


def low_later_kernel(own_ref, other_ref, me_ref, member_ref, down_ref, fresh_w, *refs):
    outs, held = refs[:-1], refs[-1]
    core = me_ref[0] % CORES
    for ref, flip in ((own_ref, 0), (other_ref, 1)):
        wide = ref.shape[2]
        for k in range(ref.shape[0]):
            block = ref[k].astype(jnp.float32)
            row = pl.ds(k * CORES + (core ^ flip), 1)
            for i in range(FOLD):
                held[row, i * wide : (i + 1) * wide] = block[i : i + 1]
    low_terms(held, member_ref, down_ref, fresh_w, *outs)


def join_kernel(amount, *refs):
    rows = [ref[...].astype(jnp.float32) for ref in refs[:amount]]
    refs[-1][...] = jnp.concatenate(rows, axis=0).astype(refs[-1].dtype)


def sum_kernel(amount, *refs):
    total = refs[0][...].astype(jnp.float32)
    for ref in refs[1:amount]:
        total = total + ref[...].astype(jnp.float32)
    refs[-1][...] = total.astype(refs[-1].dtype)


def project_kernel(rows_ref, query_w, query_ref):
    query_ref[...] = dot(rows_ref[...], query_w[...])


def up_terms(lows, query_ref, adapter_ref, up_ref):
    count, columns = query_ref.shape
    rank = lows[0].shape[1]
    low = functools.reduce(lambda a, b: a + b, lows).astype(jnp.bfloat16)
    query = query_ref[...]
    table = up_ref.shape[0]
    some = min(table, 32)
    wide = some * rank
    repeat = (iota((rank, wide), 1) % rank == iota((rank, wide), 0)).astype(jnp.bfloat16)
    wide_low = dot(low, repeat)
    place = iota((count, wide), 1) // rank
    for start in range(0, table, some):
        spread = jnp.where(place + start == adapter_ref[...], wide_low, 0.0).astype(jnp.bfloat16)
        query = query + dot(spread, up_ref[start : start + some].reshape(wide, columns))
    return query


def up_kernel(parts, *refs):
    lows, (query_ref, fresh_ref, adapter_ref, up_ref, out_ref, held) = refs[:parts], refs[parts:]
    count, columns = query_ref.shape
    query = up_terms([ref[...].astype(jnp.float32) for ref in lows], query_ref, adapter_ref, up_ref)
    line = out_ref.shape[2]
    lines = columns // line
    held[...] = jnp.zeros(held.shape, jnp.float32)
    for c in range(lines):
        held[:, c, :] = query[:, c * line : (c + 1) * line]
    fresh = fresh_ref[...].astype(jnp.float32)
    if fresh.shape[1] < line:
        fresh = jnp.concatenate(
            [fresh, jnp.zeros((count, line - fresh.shape[1]), jnp.float32)], axis=1
        )
    held[:, lines, :] = fresh
    for k in range(count):
        out_ref[k] = held[k].astype(jnp.bfloat16)


def pieces_of(lines, select, whole, size):
    if size >= whole:
        total = dot(select(len(lines), 0), lines[0])
        for c in range(1, len(lines)):
            total = total + dot(select(len(lines), c), lines[c])
        return total
    return jnp.concatenate([dot(select(0, p), lines[0]) for p in range(whole // size)], axis=1)


def attend_kernel(columns, fresh_columns, first, *refs):
    lines_ref, length_ref, cache_ref = refs[:3]
    refs = refs[3:]
    if not first:
        past, refs = refs[:2], refs[2:]
    out_ref, refs = refs[0], refs[1:]
    if first:
        keep, refs = refs[:2], refs[2:]
    held, scores = refs
    count, _, line = lines_ref.shape
    cache = cache_ref.shape[2]
    for k in range(count):
        held[k] = lines_ref[k].astype(jnp.float32)
    each = columns // line
    lines = [held[:, c, :].astype(jnp.bfloat16) for c in range(each + 1)]
    origin = iota((H, count), 1)
    head = iota((H, count), 0)

    def query_pick(each, c):
        if each:
            return (head == origin * each + c).astype(jnp.bfloat16)
        return (head * (HD // columns) + c == origin).astype(jnp.bfloat16)

    def fresh_pick(offset):
        def pick(each, c):
            want = head // GROUP + offset
            if each:
                return (want == origin * each + c).astype(jnp.bfloat16)
            return (want * (HD // fresh_columns) + c == origin).astype(jnp.bfloat16)

        return pick

    query = pieces_of(lines[:each], query_pick, HD, columns)
    fresh = [lines[each][:, :fresh_columns]]
    new = [
        (
            pieces_of(fresh, fresh_pick(0), HD, fresh_columns),
            pieces_of(fresh, fresh_pick(KVH), HD, fresh_columns),
        )
    ]
    if first:
        keep[0][...], keep[1][...] = new[0]
    else:
        new.insert(0, (past[0][...], past[1][...]))
    scale = 1.0 / math.sqrt(HD)
    for j in range(KVH):
        rows = slice(j * GROUP, (j + 1) * GROUP)
        scores[rows, :] = dot(
            query[rows].astype(jnp.bfloat16), cache_ref[0, 0, :, j * HD : (j + 1) * HD], LAST
        )
    in_cache = iota((H, cache), 1) < length_ref[0:1, 0:1]
    old = jnp.where(in_cache, scores[...] * scale, -jnp.inf)
    news = [jnp.sum(query * keys, axis=1, keepdims=True) * scale for keys, _ in new]
    peak = jnp.max(old, axis=1, keepdims=True)
    for score in news:
        peak = jnp.maximum(peak, score)
    old = jnp.exp(old - peak)
    news = [jnp.exp(score - peak) for score in news]
    total = jnp.sum(old, axis=1, keepdims=True)
    for score in news:
        total = total + score
    old = old / total
    extra = jnp.zeros((H, HD), jnp.float32)
    for score, (_, values) in zip(news, new):
        extra = extra + (score / total).astype(jnp.bfloat16).astype(jnp.float32) * values
    mixed = jnp.concatenate(
        [
            dot(
                old[j * GROUP : (j + 1) * GROUP].astype(jnp.bfloat16),
                cache_ref[0, 1, :, j * HD : (j + 1) * HD],
            )
            for j in range(KVH)
        ],
        axis=0,
    )
    mixed = mixed + extra
    if columns >= HD:
        for k in range(count):
            out_ref[k] = mixed[k * each : (k + 1) * each].astype(jnp.bfloat16)
    else:
        parts = HD // columns
        out = jnp.zeros((count, columns), jnp.float32)
        for p in range(parts):
            pick = (iota((count, H), 1) * parts + p == iota((count, H), 0)).astype(jnp.bfloat16)
            out = out + dot(pick, mixed[:, p * columns : (p + 1) * columns].astype(jnp.bfloat16))
        for k in range(count):
            out_ref[k] = out[k : k + 1].astype(jnp.bfloat16)


def output_terms(rows, core, weight_ref, own_ref, away_ref):
    count = rows.shape[0]
    chips = count // CORES
    slot = iota((count, count), 0)
    origin = (slot % chips) * CORES + (core ^ (slot // chips))
    order = (iota((count, count), 1) == origin).astype(jnp.bfloat16)
    rows = dot(order, rows).astype(jnp.bfloat16)
    width = weight_ref.shape[1]
    wide = width // 8
    for c in range(8):
        part = slice(c * wide, (c + 1) * wide)
        out = dot(rows, weight_ref[:, part])
        own_ref[:, part] = out[:chips]
        away_ref[:, part] = out[chips:].astype(jnp.bfloat16)


def output_kernel(lines_ref, me_ref, weight_ref, own_ref, away_ref, held):
    count, each, line = lines_ref.shape
    for k in range(count):
        held[k, :each, :] = lines_ref[k].astype(jnp.float32)
    rows = [held[:, c, :].astype(jnp.bfloat16) for c in range(each)]
    output_terms(jnp.concatenate(rows, axis=1), me_ref[0] % CORES, weight_ref, own_ref, away_ref)


def cut_kernel(sides, pair, me_ref, cache_hbm, *refs):
    outs, sems = refs[:-1], refs[-1]
    chip = me_ref[0] // CORES
    group = len(outs) * pair // sides
    copies = []
    for d in range(group):
        for s in range(sides):
            lanes = pl.ds(pl.multiple_of((chip ^ d ^ (s * group)) * HD, HD), HD)
            out = outs[d * (sides // pair) + s // pair].at[s % pair]
            copies.append(
                pltpu.make_async_copy(cache_hbm.at[0, :, :, lanes], out, sems.at[d * sides + s])
            )
    for copy in copies:
        copy.start()
    for copy in copies:
        copy.wait()


def gate_kernel(*_):
    pass


def pack_kernel(near, *refs):
    out_ref = refs[-1]
    total = refs[0][:, :LANES].astype(jnp.float32)
    for ref in refs[1:near]:
        total = total + ref[:, :LANES].astype(jnp.float32)
    out_ref[:, :LANES] = total.astype(jnp.bfloat16)
    for l in range(near):
        out_ref[:, (l + 1) * LANES : (l + 2) * LANES] = refs[l][:, LANES:]


def ask_kernel(sides, rank, *refs):
    lows = [ref[:, :rank].astype(jnp.float32) for ref in refs[:sides]]
    query_ref, adapter_ref, up_ref, me_ref = refs[sides : sides + 4]
    outs, held = refs[sides + 4 : -1], refs[-1]
    query = up_terms(lows, query_ref, adapter_ref, up_ref)
    some = outs[0].shape[0]
    for s in range(sides):
        held[s, :some] = query[s * some : (s + 1) * some]
    for s in range(sides):
        outs[s][...] = held[(me_ref[0] // some) ^ s, :some].astype(jnp.bfloat16)


def group_kernel(sides, near, steps, *refs):
    asked, refs = refs[:sides], refs[sides:]
    lows, refs = refs[:sides], refs[sides:]
    lengths_ref, me_ref, refs = refs[0], refs[1], refs[2:]
    if steps > 1:
        past_ref, refs = refs[0], refs[1:]
    new_ref, held, all_ref, mixed_ref = refs[-4:]
    outs, blocks = refs[-4 - sides : -4], refs[: -4 - sides]
    some, columns = asked[0].shape
    each = columns // HD
    lines = held.shape[2]
    me = me_ref[0]
    chip, core = me // CORES, me % CORES
    mine = me // some
    group = some // CORES
    held[...] = jnp.zeros(held.shape, jnp.float32)
    for s, ref in enumerate(asked):
        query = ref[...].astype(jnp.float32)
        for c in range(each):
            held[s, :, c, :] = query[:, c * HD : (c + 1) * HD]
    for k in range(sides):
        for l in range(near):
            all_ref[k * near + l] = lows[k][:, (l + 1) * LANES : (l + 2) * LANES].astype(jnp.float32)
    for s in range(sides):
        for v in range(2):
            holder = me ^ ((chip ^ (s * group)) + v * KVH)
            for row in range(some):
                new_ref[steps - 1, s, v, row : row + 1, :] = all_ref[
                    holder, pl.ds(mine * some + row, 1), :
                ]
    for t in range(steps - 1):
        new_ref[t] = past_ref[t]
    scale = 1.0 / math.sqrt(HD)
    pair = blocks[0].shape[0]
    where = []
    for l in range(CORES):
        for d in range(group):
            row = ((chip ^ d) % group) * CORES + (core ^ l)
            for s in range(sides):
                number = (l * group + d) * (sides // pair) + s // pair
                where.append((row, s, blocks[number].at[s % pair]))
    old, fresh = [], [[] for _ in range(steps)]
    for row, s, block in where:
        length = lengths_ref[pl.ds(mine * some + row, 1), :]
        query = held[s, row]
        score = dot(query.astype(jnp.bfloat16), block[0], LAST) * scale
        old.append(jnp.where(iota(score.shape, 1) < length, score, -jnp.inf))
        for t in range(steps):
            keys = new_ref[t, s, 0, pl.ds(row, 1), :]
            fresh[t].append(jnp.sum(query * keys, axis=1, keepdims=True) * scale)
    old = jnp.concatenate(old, axis=0)
    fresh = [jnp.concatenate(scores, axis=0) for scores in fresh]
    peak = jnp.max(old, axis=1, keepdims=True)
    for scores in fresh:
        peak = jnp.maximum(peak, scores)
    old = jnp.exp(old - peak)
    fresh = [jnp.exp(scores - peak) for scores in fresh]
    total = jnp.sum(old, axis=1, keepdims=True)
    for scores in fresh:
        total = total + scores
    old = (old / total).astype(jnp.bfloat16).astype(jnp.float32)
    fresh = [(scores / total).astype(jnp.bfloat16).astype(jnp.float32) for scores in fresh]
    for b, (row, s, block) in enumerate(where):
        part = slice(b * lines, (b + 1) * lines)
        mixed = dot(old[part].astype(jnp.bfloat16), block[1])
        for t in range(steps):
            mixed = mixed + fresh[t][part] * new_ref[t, s, 1, pl.ds(row, 1), :]
        mixed_ref[s, row] = mixed
    for s in range(sides):
        for c in range(each):
            outs[s][:, c * HD : (c + 1) * HD] = mixed_ref[s, :, c, :].astype(jnp.bfloat16)


def joined_kernel(sides, *refs):
    pieces, (me_ref, weight_ref, own_ref, away_ref, held) = refs[:sides], refs[sides:]
    some = pieces[0].shape[0]
    for s in range(sides):
        piece = pieces[s][...].astype(jnp.float32)
        for row in range(some):
            held[pl.ds(((me_ref[0] // some) ^ s) * some + row, 1), :] = piece[row : row + 1]
    output_terms(held[...].astype(jnp.bfloat16), me_ref[0] % CORES, weight_ref, own_ref, away_ref)


def partial_kernel(own_ref, other_ref, out_ref):
    total = own_ref[...] + other_ref[...].astype(jnp.float32)
    wide = out_ref.shape[2]
    for k in range(out_ref.shape[0]):
        for i in range(FOLD):
            out_ref[k, i : i + 1, :] = total[k : k + 1, i * wide : (i + 1) * wide].astype(
                out_ref.dtype
            )


def finish_kernel(last, parts_ref, hidden_ref, scale_ref, out_ref, *spread):
    total = parts_ref[0].astype(jnp.float32)
    for k in range(1, parts_ref.shape[0]):
        total = total + parts_ref[k].astype(jnp.float32)
    total = jnp.concatenate([total[i : i + 1] for i in range(FOLD)], axis=1)
    total = total.astype(jnp.bfloat16).astype(jnp.float32)
    before = hidden_ref[...].astype(jnp.float32)
    hidden = (before + total).astype(jnp.bfloat16).astype(jnp.float32)
    if last:
        out_ref[...] = jnp.concatenate([before, hidden], axis=0).astype(jnp.bfloat16)
    else:
        out_ref[...] = hidden.astype(jnp.bfloat16)
        folded(spread[0], normalized(hidden, row_of(scale_ref)).astype(jnp.float32))


def shards(
    hidden_state_input,
    attention_norm_scale,
    query_weight,
    key_value_weight,
    output_weight,
    adapter_down_weight,
    adapter_up_weight,
    row_adapter_index,
    adapter_storage_index,
    cache_length_per_row,
    key_value_cache,
):
    count = lax.axis_size(AXIS)
    chips = count // CORES
    far, near = split_of(count)
    far_steps = [k * near for k in range(1, far)]
    near_steps = list(range(1, near))
    kept, width, rank = adapter_down_weight.shape
    columns = query_weight.shape[1]
    fresh_columns = key_value_weight.shape[1]
    line = min(HD, columns)
    smem, vmem = pltpu.SMEM, pltpu.VMEM
    me = lax.axis_index(AXIS).astype(jnp.int32).reshape(1)
    down = adapter_down_weight.transpose(0, 2, 1)
    scale = attention_norm_scale.reshape(-1, LANES)
    storage = adapter_storage_index[None]

    def stash(token, arrays):
        outs = call(
            functools.partial(stash_kernel, len(arrays)),
            [pltpu.VMEM(a.shape, a.dtype) for a in arrays] + [shape((8, LANES), jnp.int32)],
            "stash",
            [pltpu.SemaphoreType.DMA((len(arrays),))],
            moved=sum(2 * a.size for a in arrays),
        )(
            token,
            *(pltpu.with_memory_space_constraint(a, pltpu.HBM) for a in arrays),
            specs=[vmem] + [pltpu.HBM] * len(arrays),
        )
        return outs[:-1], outs[-1]

    def gate(array, *behind):
        return pl.pallas_call(
            gate_kernel,
            out_shape=shape(array.shape, array.dtype),
            in_specs=[pl.BlockSpec(memory_space=pl.ANY)] * (1 + len(behind)),
            out_specs=pl.BlockSpec(memory_space=pl.ANY),
            input_output_aliases={0: 0},
            compiler_params=pltpu.CompilerParams(vmem_limit_bytes=1 << 20),
            name="gate",
        )(array, *behind)

    def by_rows(step, lows, query, fresh):
        first = step == 0
        (lines,) = call(
            functools.partial(up_kernel, far),
            [shape((count, 8, line))],
            "up",
            [pltpu.VMEM((count, 8, line), jnp.float32)],
        )(*lows, query, fresh, adapter, up_w)

        lines = swap(lines)
        outs = [shape((count, columns // line, line))]
        if first:
            outs = outs + [shape((H, HD), jnp.float32)] * 2
        outs = call(
            functools.partial(attend_kernel, columns, fresh_columns, first),
            outs,
            "attend",
            [
                pltpu.VMEM((count, 8, line), jnp.float32),
                pltpu.VMEM((H, key_value_cache.shape[2]), jnp.float32),
            ],
            moved=2 << 20,
        )(
            lines,
            length,
            held_cache[0],
            *past,
            specs=[vmem] * (3 + len(past)),
        )
        if first:
            past.extend(outs[1:])

        lines = swap(outs[0])
        own, away = call(
            output_kernel,
            [shape((chips, width), jnp.float32), shape((chips, width))],
            "output",
            [pltpu.VMEM((count, 8, line), jnp.float32)],
            flops=2 * count * width * columns,
            moved=2 * width * columns,
        )(lines, me, output_w, specs=[vmem, smem, vmem])
        return own, away

    def by_groups(step, lows, query):
        rows_group = shape((near, columns))
        asked = call(
            functools.partial(ask_kernel, far, rank),
            [rows_group] * far,
            "ask",
            [pltpu.VMEM((far, 8, columns), jnp.float32)],
        )(*lows, query, adapter, up_w, me, specs=[vmem] * (far + 3) + [smem])
        asked = [asked[0]] + [shift(a, d, count) for a, d in zip(asked[1:], far_steps)]
        if not blocks:
            still = gate(parts[-1], asked[1])
            blocks.extend([*parts[:-1], still, *sibs, shift(still, 1, count)])
        new = (step + 1, far, 2, near, HD)
        outs = call(
            functools.partial(group_kernel, far, near, step + 1),
            [rows_group] * far + [shape(new, jnp.float32)],
            "attend",
            [
                pltpu.VMEM((far, near, 8, HD), jnp.float32),
                pltpu.VMEM((count, count, LANES), jnp.float32),
                pltpu.VMEM((far, near, 8, HD), jnp.float32),
            ],
            moved=4 << 20,
        )(
            *asked,
            *lows,
            lengths,
            me,
            *past,
            *blocks,
            specs=[vmem] * (2 * far + 1) + [smem] + [vmem] * (len(past) + len(blocks)),
        )
        past[:] = [outs[-1]]
        pieces = [outs[0]] + [shift(a, d, count) for a, d in zip(outs[1:far], far_steps)]
        return call(
            functools.partial(joined_kernel, far),
            [shape((chips, width), jnp.float32), shape((chips, width))],
            "output",
            [pltpu.VMEM((count, columns), jnp.float32)],
            flops=2 * count * width * columns,
            moved=2 * width * columns,
        )(*pieces, me, output_w, specs=[vmem] * far + [smem, vmem])

    by_heads = (
        columns * CORES == GROUP * HD and count == CORES * KVH and fresh_columns == LANES
    )
    past, held_cache, blocks = [], [], []
    hidden = hidden_state_input
    carried, length = call(
        first_kernel, [shape((1, width + LANES)), shape((8, LANES), jnp.int32)], "first"
    )(
        hidden,
        scale,
        row_adapter_index,
        cache_length_per_row,
        me,
        specs=[vmem, vmem, smem, smem, smem],
    )
    for step in range(STEPS):
        first, last = step == 0, step == STEPS - 1
        low_outs = [shape((count, width))]
        if by_heads:
            low_outs = low_outs + [shape((count, LANES + fresh_columns))]
        else:
            low_outs = low_outs + [shape((count, rank)), shape((count, fresh_columns))]
        scratch = [pltpu.VMEM((count, width), jnp.float32)]
        behind = []
        if first:
            steps = (near_steps, far_steps) if by_heads else (far_steps, near_steps)
            strides = (near, 1) if by_heads else (1, near)
            amount = len(steps[1]) + 1
            early = [query_weight, key_value_weight, down]
            later = [output_weight, adapter_up_weight]
            if by_heads:
                group = near // CORES
                pair = far // 2
                cut = call(
                    functools.partial(cut_kernel, far, pair),
                    [pltpu.VMEM((pair, 2, key_value_cache.shape[2], HD), jnp.bfloat16)]
                    * (group * 2),
                    "cut",
                    [pltpu.SemaphoreType.DMA((group * far,))],
                )(
                    me,
                    pltpu.with_memory_space_constraint(key_value_cache, pltpu.HBM),
                    specs=[smem, pltpu.HBM],
                )
            else:
                later = later + [key_value_cache]
                (query_w, fresh_w, down_w), token = stash(length, early)
            pieces = across(carried, steps[0], count)
            ordered = [] if by_heads else [token]
            (carried,) = call(
                functools.partial(join_kernel, len(pieces)),
                [shape((len(pieces), width + LANES))],
                "join",
            )(*pieces, *ordered)
            if by_heads:
                (query_w, fresh_w, down_w), token = stash(length, early)
                there = shift(gate(cut[2], carried), CORES, count)
                parts = [gate(cut[0], carried)]
                beside = shift(parts[0], 1, count)
                behind = [there, beside]
            (output_w, up_w, *cached), token = stash(token, later)
            held_cache.extend(cached)
            pieces = across(carried, steps[1], count)
            member, adapter, lengths = call(
                functools.partial(member_kernel, near, far, width, strides),
                [shape((count, kept), jnp.int32)] + [shape((count, 1), jnp.int32)] * 2,
                "member",
                [pltpu.VMEM((count, LANES), jnp.float32)],
            )(
                *pieces,
                me,
                storage,
                token,
                *behind,
                specs=[vmem] * amount + [smem, vmem, vmem] + [pl.ANY] * len(behind),
            )
            rows, low, *fresh = call(
                functools.partial(low_first_kernel, amount, strides), low_outs, "low", scratch
            )(*pieces, me, member, down_w, fresh_w, specs=[vmem] * amount + [smem] + [vmem] * 3)
            behind = []
            if by_heads:
                still = gate(there, rows)
                parts = parts + [gate(cut[1], rows), still]
                sibs = [beside] + [shift(p, 1, count) for p in parts[1:]]
                behind = sibs[1:]
        else:
            own = chips_swap(carried, count)
            rows, low, *fresh = call(low_later_kernel, low_outs, "low", scratch)(
                own,
                shift(own, 1, count),
                me,
                member,
                down_w,
                fresh_w,
                specs=[vmem, vmem, smem, vmem, vmem, vmem],
            )
        if by_heads:
            body, dims = pack_kernel, (count, (near + 1) * LANES)
        else:
            body, dims = sum_kernel, (count, rank)
        (low,) = call(functools.partial(body, near), [shape(dims)], "sum")(
            *across(low, near_steps, count),
            *behind,
            specs=[vmem] * near + [pl.ANY] * len(behind),
        )
        if first and by_heads:
            parts = parts + [shift(gate(cut[3], low), CORES, count)]
        lows = across(low, far_steps, count)
        (query,) = call(
            project_kernel,
            [shape((count, columns), jnp.float32)],
            "project",
            flops=2 * count * width * columns,
            moved=2 * width * columns,
        )(rows, query_w)
        if by_heads:
            own, away = by_groups(step, lows, query)
        else:
            own, away = by_rows(step, lows, query, fresh[0])

        (parts,) = call(partial_kernel, [shape((chips, FOLD, width // FOLD))], "partial")(
            own, shift(away, 1, count)
        )
        parts = chips_swap(parts, count)
        outs = [shape((2 if last else 1, width))]
        if not last:
            outs = outs + [shape((chips, FOLD, width // FOLD))]
        outs = call(functools.partial(finish_kernel, last), outs, "finish")(parts, hidden, scale)
        if last:
            return outs[0].reshape(STEPS, 1, width)
        hidden, carried = outs


def solution(mesh):
    in_specs = (
        P(("groups", "replica"), None),
        P(),
        P(None, "replica"),
        P(None, "replica"),
        P("replica", None),
        P("replica", None, None),
        P(None, None, "replica"),
        P(("groups", "replica")),
        P(),
        P(("groups", "replica")),
        P(("groups", "replica"), None, None, None),
    )
    out_specs = P(None, ("groups", "replica"), None)
    return jax.shard_map(shards, mesh=mesh, in_specs=in_specs, out_specs=out_specs, check_vma=False)
```

```python
import functools
import math

import jax
import jax.numpy as jnp
from jax import lax
from jax.experimental import pallas as pl
from jax.experimental.pallas import tpu as pltpu
from jax.sharding import PartitionSpec as P

H = 64
KVH = 8
HD = 128
STEPS = 2
GROUP = H // KVH
EPS = 1e-05
AXIS = "replica"
LANES = 128
LAST = (((1,), (1,)), ((), ()))
FIRST = (((0,), (0,)), ((), ()))

CORES = 2
FOLD = 8


def split_of(count):
    far = 1 << (count.bit_length() // 2)
    return far, count // far


def shift(block, distance, count):
    return lax.ppermute(block, AXIS, [(i, i ^ distance) for i in range(count)])


def across(block, strides, count):
    return [block] + [shift(block, d, count) for d in strides]


def swap(blocks):
    return lax.all_to_all(blocks, AXIS, split_axis=0, concat_axis=0, tiled=True)


def chips_swap(blocks, count):
    groups = [[i for i in range(count) if i % CORES == c] for c in range(CORES)]
    return lax.all_to_all(
        blocks, AXIS, split_axis=0, concat_axis=0, axis_index_groups=groups, tiled=True
    )


def call(body, outs, name, scratch=(), vmem=20 << 20, flops=1 << 20, moved=1 << 18):
    def run(*operands, specs=None):
        specs = specs or [pltpu.VMEM] * len(operands)
        return pl.pallas_call(
            body,
            out_shape=outs,
            in_specs=[pl.BlockSpec(memory_space=s) for s in specs],
            out_specs=[pl.BlockSpec(memory_space=pltpu.VMEM)] * len(outs),
            scratch_shapes=list(scratch),
            compiler_params=pltpu.CompilerParams(vmem_limit_bytes=vmem),
            cost_estimate=pl.CostEstimate(flops=flops, bytes_accessed=moved, transcendentals=0),
            name=name,
        )(*operands)

    return run


def shape(dims, dtype=jnp.bfloat16):
    return jax.ShapeDtypeStruct(dims, dtype)


def iota(dims, axis):
    return lax.broadcasted_iota(jnp.int32, dims, axis)


def dot(a, b, contract=(((1,), (0,)), ((), ()))):
    return lax.dot_general(a, b, contract, preferred_element_type=jnp.float32)


def normalized(hidden, scale):
    factor = lax.rsqrt(jnp.mean(hidden * hidden, axis=-1, keepdims=True) + EPS)
    return (hidden * factor * scale).astype(jnp.bfloat16)


def row_of(ref):
    lines = ref[...].astype(jnp.float32)
    return jnp.concatenate([lines[i : i + 1] for i in range(lines.shape[0])], axis=1)


def first_kernel(hidden_ref, adapter_ref, length_ref, _, out_ref, length_out):
    length_out[...] = jnp.full(length_out.shape, length_ref[0], jnp.int32)
    width = hidden_ref.shape[1]
    out_ref[:, :width] = hidden_ref[...]
    digit = iota((1, LANES), 1)
    adapter = adapter_ref[0]
    high, low = adapter // 256, adapter % 256
    digits = jnp.where(digit == 0, low, jnp.where(digit == 1, high, 0)).astype(jnp.float32)
    out_ref[:, width:] = digits.astype(jnp.bfloat16)


def stash_kernel(amount, token_ref, *refs):
    sources, refs = refs[:amount], refs[amount:]
    outs, out_token, sems = refs[:amount], refs[amount], refs[-1]
    copies = [
        pltpu.make_async_copy(sources[i], outs[i], sems.at[i]) for i in range(amount)
    ]
    for copy in copies:
        copy.start()
    out_token[...] = token_ref[...]
    for copy in copies:
        copy.wait()


def member_kernel(near, far, width, *refs):
    pieces, refs = refs[:near], refs[near:]
    me_ref, storage_ref, _, member_ref, adapter_ref, held = refs
    kept = member_ref.shape[1]
    count = near * far
    me = me_ref[0]
    for l in range(near):
        digits = pieces[l][:, width:].astype(jnp.float32)
        for k in range(far):
            held[pl.ds(me ^ (k * near + l), 1), :] = digits[k : k + 1]
    adapter = (held[:, 0:1] + 256.0 * held[:, 1:2]).astype(jnp.int32)
    adapter_ref[...] = adapter
    table = storage_ref.shape[1]
    chosen = jnp.where(iota((count, table), 1) == adapter, storage_ref[...], 0)
    storage = jnp.sum(chosen.astype(jnp.float32), axis=1, keepdims=True).astype(jnp.int32)
    member_ref[...] = (storage - me * kept == iota((count, kept), 1)).astype(jnp.int32)


def low_terms(held, member_ref, down_ref, rows_ref, low_ref):
    rows = held[...].astype(jnp.bfloat16)
    rows_ref[...] = rows
    low = jnp.zeros(low_ref.shape, jnp.float32)
    for index in range(down_ref.shape[0]):
        part = dot(rows, down_ref[index], LAST)
        low = jnp.where(member_ref[:, index : index + 1] > 0, part, low)
    low_ref[...] = low.astype(jnp.bfloat16)


def low_first_kernel(near, far, *refs):
    pieces, refs = refs[:near], refs[near:]
    me_ref, member_ref, down_ref, rows_ref, low_ref, held = refs
    width = held.shape[1]
    for l in range(near):
        block = pieces[l][:, :width].astype(jnp.float32)
        for k in range(far):
            held[pl.ds(me_ref[0] ^ (k * near + l), 1), :] = block[k : k + 1]
    low_terms(held, member_ref, down_ref, rows_ref, low_ref)


def low_later_kernel(near, far, own_ref, other_ref, me_ref, member_ref, down_ref, rows_ref, low_ref, held):
    half = own_ref.shape[0]
    for start, ref in ((0, own_ref), (half, other_ref)):
        block = ref[...].astype(jnp.float32)
        for k in range(half):
            row = me_ref[0] ^ distance(start + k, near, far)
            held[pl.ds(row, 1), :] = block[k : k + 1]
    low_terms(held, member_ref, down_ref, rows_ref, low_ref)


def join_kernel(amount, *refs):
    scale_ref, _, hidden_ref, out_ref = refs[amount:]
    width = hidden_ref.shape[1]
    rows = [ref[...].astype(jnp.float32) for ref in refs[:amount]]
    rows = jnp.concatenate(rows, axis=0)
    hidden = rows[:, :width]
    hidden_ref[...] = hidden.astype(jnp.bfloat16)
    out_ref[:, :width] = normalized(hidden, row_of(scale_ref))
    out_ref[:, width:] = rows[:, width:].astype(jnp.bfloat16)


def stack_kernel(*refs):
    rows = [ref[...].astype(jnp.float32) for ref in refs[:-1]]
    refs[-1][...] = jnp.concatenate(rows, axis=0).astype(refs[-1].dtype)


def distance(slot, near, far):
    size, total = near * far, (slot % far) * near
    bit = 1
    while bit < near:
        size //= 2
        total = total + ((slot // size) % 2) * bit
        bit *= 2
    return total


def fold_kernel(own_ref, other_ref, keep_ref, away_ref):
    total = own_ref[...] + other_ref[...].astype(jnp.float32)
    half = keep_ref.shape[0]
    keep_ref[...] = total[:half]
    away_ref[...] = total[half:].astype(jnp.bfloat16)


def folded_kernel(own_ref, other_ref, out_ref):
    out_ref[...] = (own_ref[...] + other_ref[...].astype(jnp.float32)).astype(jnp.bfloat16)


def next_kernel(far, *refs):
    pieces, (hidden_ref, scale_ref, own_ref, out_ref) = refs[:far], refs[far:]
    sums = []
    for k in range(far):
        piece = pieces[k][...].astype(jnp.float32)
        sums.append(jnp.concatenate([piece[j ^ k : (j ^ k) + 1] for j in range(far)], axis=0))
    while len(sums) > 1:
        sums = [sums[i] + sums[i + 1] for i in range(0, len(sums), 2)]
    total = sums[0].astype(jnp.bfloat16).astype(jnp.float32)
    hidden = (hidden_ref[...].astype(jnp.float32) + total).astype(jnp.bfloat16)
    own_ref[...] = hidden.astype(jnp.float32)[:1].astype(jnp.bfloat16)
    out_ref[...] = normalized(hidden.astype(jnp.float32), row_of(scale_ref))


def sum_kernel(*refs):
    total = refs[0][...].astype(jnp.float32)
    for ref in refs[1:-1]:
        total = total + ref[...].astype(jnp.float32)
    refs[-1][...] = total.astype(refs[-1].dtype)


def project_kernel(rows_ref, query_w, fresh_w, query_ref, fresh_ref):
    query_ref[...] = dot(rows_ref[...], query_w[...])
    fresh_ref[...] = dot(rows_ref[...], fresh_w[...])


def up_kernel(parts, *refs):
    lows, (query_ref, fresh_ref, adapter_ref, up_ref, out_ref, held) = refs[:parts], refs[parts:]
    count, columns = query_ref.shape
    rank = lows[0].shape[1]
    low = lows[0][...].astype(jnp.float32)
    for ref in lows[1:]:
        low = low + ref[...].astype(jnp.float32)
    low = low.astype(jnp.bfloat16)
    query = query_ref[...]
    table = up_ref.shape[0]
    some = min(table, 32)
    wide = some * rank
    repeat = (iota((rank, wide), 1) % rank == iota((rank, wide), 0)).astype(jnp.bfloat16)
    wide_low = dot(low, repeat)
    place = iota((count, wide), 1) // rank
    for start in range(0, table, some):
        spread = jnp.where(place + start == adapter_ref[...], wide_low, 0.0).astype(jnp.bfloat16)
        query = query + dot(spread, up_ref[start : start + some].reshape(wide, columns))
    line = out_ref.shape[2]
    lines = columns // line
    held[...] = jnp.zeros(held.shape, jnp.float32)
    for c in range(lines):
        held[:, c, :] = query[:, c * line : (c + 1) * line]
    fresh = fresh_ref[...]
    if fresh.shape[1] < line:
        fresh = jnp.concatenate(
            [fresh, jnp.zeros((count, line - fresh.shape[1]), jnp.float32)], axis=1
        )
    held[:, lines, :] = fresh
    for k in range(count):
        out_ref[k] = held[k].astype(jnp.bfloat16)


def pieces_of(lines, select, whole, size):
    if size >= whole:
        total = dot(select(len(lines), 0), lines[0])
        for c in range(1, len(lines)):
            total = total + dot(select(len(lines), c), lines[c])
        return total
    return jnp.concatenate([dot(select(0, p), lines[0]) for p in range(whole // size)], axis=1)


def attend_kernel(columns, fresh_columns, first, *refs):
    lines_ref, length_ref, cache_ref = refs[:3]
    refs = refs[3:]
    if not first:
        past, refs = refs[:2], refs[2:]
    out_ref, refs = refs[0], refs[1:]
    if first:
        keep, refs = refs[:2], refs[2:]
    held, scores = refs
    count, _, line = lines_ref.shape
    cache = cache_ref.shape[2]
    for k in range(count):
        held[k] = lines_ref[k].astype(jnp.float32)
    each = columns // line
    lines = [held[:, c, :].astype(jnp.bfloat16) for c in range(each + 1)]
    origin = iota((H, count), 1)
    head = iota((H, count), 0)

    def query_pick(each, c):
        if each:
            return (head == origin * each + c).astype(jnp.bfloat16)
        return (head * (HD // columns) + c == origin).astype(jnp.bfloat16)

    def fresh_pick(offset):
        def pick(each, c):
            want = head // GROUP + offset
            if each:
                return (want == origin * each + c).astype(jnp.bfloat16)
            return (want * (HD // fresh_columns) + c == origin).astype(jnp.bfloat16)

        return pick

    query = pieces_of(lines[:each], query_pick, HD, columns)
    fresh = [lines[each][:, :fresh_columns]]
    new = [
        (
            pieces_of(fresh, fresh_pick(0), HD, fresh_columns),
            pieces_of(fresh, fresh_pick(KVH), HD, fresh_columns),
        )
    ]
    if first:
        keep[0][...], keep[1][...] = new[0]
    else:
        new.insert(0, (past[0][...], past[1][...]))
    scale = 1.0 / math.sqrt(HD)
    for j in range(KVH):
        rows = slice(j * GROUP, (j + 1) * GROUP)
        scores[rows, :] = dot(
            query[rows].astype(jnp.bfloat16), cache_ref[0, 0, :, j * HD : (j + 1) * HD], LAST
        )
    in_cache = iota((H, cache), 1) < length_ref[0:1, 0:1]
    old = jnp.where(in_cache, scores[...] * scale, -jnp.inf)
    news = [jnp.sum(query * keys, axis=1, keepdims=True) * scale for keys, _ in new]
    peak = jnp.max(old, axis=1, keepdims=True)
    for score in news:
        peak = jnp.maximum(peak, score)
    old = jnp.exp(old - peak)
    news = [jnp.exp(score - peak) for score in news]
    total = jnp.sum(old, axis=1, keepdims=True)
    for score in news:
        total = total + score
    old = old / total
    extra = jnp.zeros((H, HD), jnp.float32)
    for score, (_, values) in zip(news, new):
        extra = extra + (score / total).astype(jnp.bfloat16).astype(jnp.float32) * values
    mixed = jnp.concatenate(
        [
            dot(
                old[j * GROUP : (j + 1) * GROUP].astype(jnp.bfloat16),
                cache_ref[0, 1, :, j * HD : (j + 1) * HD],
            )
            for j in range(KVH)
        ],
        axis=0,
    )
    mixed = mixed + extra
    if columns >= HD:
        for k in range(count):
            out_ref[k] = mixed[k * each : (k + 1) * each].astype(jnp.bfloat16)
    else:
        parts = HD // columns
        out = jnp.zeros((count, columns), jnp.float32)
        for p in range(parts):
            pick = (iota((count, H), 1) * parts + p == iota((count, H), 0)).astype(jnp.bfloat16)
            out = out + dot(pick, mixed[:, p * columns : (p + 1) * columns].astype(jnp.bfloat16))
        for k in range(count):
            out_ref[k] = out[k : k + 1].astype(jnp.bfloat16)


def output_kernel(split, lines_ref, me_ref, weight_ref, own_ref, away_ref, held):
    count, each, line = lines_ref.shape
    chips = count // CORES
    for k in range(count):
        held[k, :each, :] = lines_ref[k].astype(jnp.float32)
    slot = iota((count, count), 0)
    if split:
        origin = me_ref[0] ^ distance(slot, *split)
    else:
        origin = (slot % chips) * CORES + ((me_ref[0] % CORES) ^ (slot // chips))
    order = (iota((count, count), 1) == origin).astype(jnp.bfloat16)
    rows = jnp.concatenate(
        [dot(order, held[:, c, :].astype(jnp.bfloat16)).astype(jnp.bfloat16) for c in range(each)],
        axis=1,
    )
    width = weight_ref.shape[1]
    wide = width // 8
    for c in range(8):
        part = slice(c * wide, (c + 1) * wide)
        out = dot(rows, weight_ref[:, part])
        own_ref[:, part] = out[:chips]
        away_ref[:, part] = out[chips:].astype(jnp.bfloat16)


def partial_kernel(own_ref, other_ref, out_ref):
    total = own_ref[...] + other_ref[...].astype(jnp.float32)
    wide = out_ref.shape[2]
    for k in range(out_ref.shape[0]):
        for i in range(FOLD):
            out_ref[k, i : i + 1, :] = total[k : k + 1, i * wide : (i + 1) * wide].astype(
                out_ref.dtype
            )


def finish_kernel(parts_ref, hidden_ref, out_ref):
    total = parts_ref[0].astype(jnp.float32)
    for k in range(1, parts_ref.shape[0]):
        total = total + parts_ref[k].astype(jnp.float32)
    total = jnp.concatenate([total[i : i + 1] for i in range(FOLD)], axis=1)
    total = total.astype(jnp.bfloat16).astype(jnp.float32)
    before = hidden_ref[...].astype(jnp.float32)
    out_ref[...] = jnp.concatenate([before, before + total], axis=0).astype(jnp.bfloat16)


def shards(
    hidden_state_input,
    attention_norm_scale,
    query_weight,
    key_value_weight,
    output_weight,
    adapter_down_weight,
    adapter_up_weight,
    row_adapter_index,
    adapter_storage_index,
    cache_length_per_row,
    key_value_cache,
):
    count = lax.axis_size(AXIS)
    chips = count // CORES
    far, near = split_of(count)
    far_steps = [k * near for k in range(1, far)]
    near_steps = list(range(1, near))
    kept, width, rank = adapter_down_weight.shape
    columns = query_weight.shape[1]
    fresh_columns = key_value_weight.shape[1]
    line = min(HD, columns)
    smem, vmem = pltpu.SMEM, pltpu.VMEM
    me = lax.axis_index(AXIS).astype(jnp.int32).reshape(1)
    down = adapter_down_weight.transpose(0, 2, 1)
    scale = attention_norm_scale.reshape(-1, LANES)
    storage = adapter_storage_index[None]

    def stash(token, arrays):
        outs = call(
            functools.partial(stash_kernel, len(arrays)),
            [pltpu.VMEM(a.shape, a.dtype) for a in arrays] + [shape((8, LANES), jnp.int32)],
            "stash",
            [pltpu.SemaphoreType.DMA((len(arrays),))],
            moved=sum(2 * a.size for a in arrays),
        )(
            token,
            *(pltpu.with_memory_space_constraint(a, pltpu.HBM) for a in arrays),
            specs=[vmem] + [pltpu.HBM] * len(arrays),
        )
        return outs[:-1], outs[-1]

    hidden = hidden_state_input
    carried, length = call(
        first_kernel, [shape((1, width + LANES)), shape((8, LANES), jnp.int32)], "first"
    )(
        hidden,
        row_adapter_index,
        cache_length_per_row,
        me,
        specs=[vmem, smem, smem, smem],
    )
    past = ()
    for step in range(STEPS):
        first, last = step == 0, step == STEPS - 1
        outs = [shape((count, width)), shape((count, rank))]
        scratch = [pltpu.VMEM((count, width), jnp.float32)]
        if first:
            early = [query_weight, key_value_weight, down]
            (query_w, fresh_w, down_w), token = stash(length, early)
            pieces = across(carried, far_steps, count)
            column, carried = call(
                functools.partial(join_kernel, far),
                [shape((far, width)), shape((far, width + LANES))],
                "join",
            )(*pieces, scale, token)
            later = [output_weight, key_value_cache, adapter_up_weight]
            (output_w, cache, up_w), token = stash(token, later)
            pieces = across(carried, near_steps, count)
            member, adapter = call(
                functools.partial(member_kernel, near, far, width),
                [shape((count, kept), jnp.int32), shape((count, 1), jnp.int32)],
                "member",
                [pltpu.VMEM((count, LANES), jnp.float32)],
            )(*pieces, me, storage, token, specs=[vmem] * near + [smem, vmem, vmem])
            rows, low = call(
                functools.partial(low_first_kernel, near, far), outs, "low", scratch
            )(*pieces, me, member, down_w, specs=[vmem] * near + [smem, vmem, vmem])
        else:
            rows, low = call(functools.partial(low_later_kernel, near, far), outs, "low", scratch)(
                carried,
                shift(carried, 1, count),
                me,
                member,
                down_w,
                specs=[vmem, vmem, smem, vmem, vmem],
            )
        (low,) = call(sum_kernel, [shape((count, rank))], "sum")(*across(low, near_steps, count))
        lows = across(low, far_steps, count)
        query, fresh = call(
            project_kernel,
            [shape((count, columns), jnp.float32), shape((count, fresh_columns), jnp.float32)],
            "project",
            flops=2 * count * width * (columns + fresh_columns),
            moved=2 * width * (columns + fresh_columns),
        )(rows, query_w, fresh_w)
        (lines,) = call(
            functools.partial(up_kernel, far),
            [shape((count, 8, line))],
            "up",
            [pltpu.VMEM((count, 8, line), jnp.float32)],
        )(*lows, query, fresh, adapter, up_w)

        lines = swap(lines)
        outs = [shape((count, columns // line, line))]
        if first:
            outs = outs + [shape((H, HD), jnp.float32)] * 2
        outs = call(
            functools.partial(attend_kernel, columns, fresh_columns, first),
            outs,
            "attend",
            [
                pltpu.VMEM((count, 8, line), jnp.float32),
                pltpu.VMEM((H, key_value_cache.shape[2]), jnp.float32),
            ],
            moved=2 << 20,
        )(
            lines,
            length,
            cache,
            *past,
            specs=[vmem] * (3 + len(past)),
        )
        if first:
            past = tuple(outs[1:])

        lines = swap(outs[0])
        own, away = call(
            functools.partial(output_kernel, None if last else (near, far)),
            [shape((chips, width), jnp.float32), shape((chips, width))],
            "output",
            [pltpu.VMEM((count, 8, line), jnp.float32)],
            flops=2 * count * width * columns,
            moved=2 * width * columns,
        )(lines, me, output_w, specs=[vmem, smem, vmem])

        if last:
            (parts,) = call(partial_kernel, [shape((chips, FOLD, width // FOLD))], "partial")(
                own, shift(away, 1, count)
            )
            parts = chips_swap(parts, count)
            (out,) = call(finish_kernel, [shape((STEPS, width))], "finish")(parts, hidden)
            return out.reshape(STEPS, 1, width)
        bit = 1
        while bit < near // 2:
            half = own.shape[0] // 2
            own, away = call(
                fold_kernel, [shape((half, width), jnp.float32), shape((half, width))], "fold"
            )(own, shift(away, bit, count))
            bit *= 2
        (own,) = call(folded_kernel, [shape((far, width))], "fold")(own, shift(away, bit, count))
        hidden, carried = call(
            functools.partial(next_kernel, far), [shape((1, width)), shape((far, width))], "next"
        )(*across(own, far_steps, count), column, scale)
        while bit > 1:
            (carried,) = call(stack_kernel, [shape((2 * carried.shape[0], width))], "stack")(
                carried, shift(carried, bit, count)
            )
            bit //= 2


def solution(mesh):
    in_specs = (
        P(("groups", "replica"), None),
        P(),
        P(None, "replica"),
        P(None, "replica"),
        P("replica", None),
        P("replica", None, None),
        P(None, None, "replica"),
        P(("groups", "replica")),
        P(),
        P(("groups", "replica")),
        P(("groups", "replica"), None, None, None),
    )
    out_specs = P(None, ("groups", "replica"), None)
    return jax.shard_map(shards, mesh=mesh, in_specs=in_specs, out_specs=out_specs, check_vma=False)
```

```python
import functools
import math

import jax
import jax.numpy as jnp
from jax import lax
from jax.experimental import pallas as pl
from jax.experimental.pallas import tpu as pltpu
from jax.sharding import PartitionSpec as P

H = 64
KVH = 8
HD = 128
STEPS = 2
GROUP = H // KVH
EPS = 1e-05
AXIS = "replica"
LANES = 128
LAST = (((1,), (1,)), ((), ()))
FIRST = (((0,), (0,)), ((), ()))

CORES = 2
FOLD = 8


def split_of(count):
    far = 1 << (count.bit_length() // 2)
    return far, count // far


def shift(block, distance, count):
    return lax.ppermute(block, AXIS, [(i, i ^ distance) for i in range(count)])


def across(block, strides, count):
    return [block] + [shift(block, d, count) for d in strides]


def swap(blocks):
    return lax.all_to_all(blocks, AXIS, split_axis=0, concat_axis=0, tiled=True)


def chips_swap(blocks, count):
    groups = [[i for i in range(count) if i % CORES == c] for c in range(CORES)]
    return lax.all_to_all(
        blocks, AXIS, split_axis=0, concat_axis=0, axis_index_groups=groups, tiled=True
    )


def call(body, outs, name, scratch=(), vmem=20 << 20, flops=1 << 20, moved=1 << 18):
    def run(*operands, specs=None):
        specs = specs or [pltpu.VMEM] * len(operands)
        return pl.pallas_call(
            body,
            out_shape=outs,
            in_specs=[pl.BlockSpec(memory_space=s) for s in specs],
            out_specs=[pl.BlockSpec(memory_space=pltpu.VMEM)] * len(outs),
            scratch_shapes=list(scratch),
            compiler_params=pltpu.CompilerParams(vmem_limit_bytes=vmem),
            cost_estimate=pl.CostEstimate(flops=flops, bytes_accessed=moved, transcendentals=0),
            name=name,
        )(*operands)

    return run


def shape(dims, dtype=jnp.bfloat16):
    return jax.ShapeDtypeStruct(dims, dtype)


def iota(dims, axis):
    return lax.broadcasted_iota(jnp.int32, dims, axis)


def dot(a, b, contract=(((1,), (0,)), ((), ()))):
    return lax.dot_general(a, b, contract, preferred_element_type=jnp.float32)


def normalized(hidden, scale):
    factor = lax.rsqrt(jnp.mean(hidden * hidden, axis=-1, keepdims=True) + EPS)
    return (hidden * factor * scale).astype(jnp.bfloat16)


def row_of(ref):
    lines = ref[...].astype(jnp.float32)
    return jnp.concatenate([lines[i : i + 1] for i in range(lines.shape[0])], axis=1)


def first_kernel(hidden_ref, adapter_ref, length_ref, _, out_ref, length_out):
    length_out[...] = jnp.full(length_out.shape, length_ref[0], jnp.int32)
    width = hidden_ref.shape[1]
    out_ref[:, :width] = hidden_ref[...]
    digit = iota((1, LANES), 1)
    adapter = adapter_ref[0]
    high, low = adapter // 256, adapter % 256
    digits = jnp.where(digit == 0, low, jnp.where(digit == 1, high, 0)).astype(jnp.float32)
    out_ref[:, width:] = digits.astype(jnp.bfloat16)


def stash_kernel(amount, token_ref, *refs):
    sources, refs = refs[:amount], refs[amount:]
    outs, out_token, sems = refs[-2 - amount : -2], refs[-2], refs[-1]
    copies = [
        pltpu.make_async_copy(sources[i], outs[i], sems.at[i]) for i in range(amount)
    ]
    for copy in copies:
        copy.start()
    out_token[...] = token_ref[...]
    for copy in copies:
        copy.wait()


def member_kernel(near, far, width, *refs):
    pieces, refs = refs[:near], refs[near:]
    me_ref, storage_ref, _, member_ref, adapter_ref, held = refs
    kept = member_ref.shape[1]
    count = near * far
    me = me_ref[0]
    for l in range(near):
        digits = pieces[l][:, width:].astype(jnp.float32)
        for k in range(far):
            held[pl.ds(me ^ (k * near + l), 1), :] = digits[k : k + 1]
    adapter = (held[:, 0:1] + 256.0 * held[:, 1:2]).astype(jnp.int32)
    adapter_ref[...] = adapter
    table = storage_ref.shape[1]
    chosen = jnp.where(iota((count, table), 1) == adapter, storage_ref[...], 0)
    storage = jnp.sum(chosen.astype(jnp.float32), axis=1, keepdims=True).astype(jnp.int32)
    member_ref[...] = (storage - me * kept == iota((count, kept), 1)).astype(jnp.int32)


def low_terms(held, member_ref, down_ref, rows_ref, low_ref):
    rows = held[...].astype(jnp.bfloat16)
    rows_ref[...] = rows
    low = jnp.zeros(low_ref.shape, jnp.float32)
    for index in range(down_ref.shape[0]):
        part = dot(rows, down_ref[index], LAST)
        low = jnp.where(member_ref[:, index : index + 1] > 0, part, low)
    low_ref[...] = low.astype(jnp.bfloat16)


def low_kernel(near, far, *refs):
    pieces, refs = refs[:near], refs[near:]
    me_ref, member_ref, down_ref, rows_ref, low_ref, held = refs
    width = held.shape[1]
    for l in range(near):
        block = pieces[l][:, :width].astype(jnp.float32)
        for k in range(far):
            held[pl.ds(me_ref[0] ^ (k * near + l), 1), :] = block[k : k + 1]
    low_terms(held, member_ref, down_ref, rows_ref, low_ref)


def join_kernel(amount, *refs):
    scale_ref, _, hidden_ref, out_ref = refs[amount:]
    width = hidden_ref.shape[1]
    rows = [ref[...].astype(jnp.float32) for ref in refs[:amount]]
    rows = jnp.concatenate(rows, axis=0)
    hidden = rows[:, :width]
    hidden_ref[...] = hidden.astype(jnp.bfloat16)
    out_ref[:, :width] = normalized(hidden, row_of(scale_ref))
    out_ref[:, width:] = rows[:, width:].astype(jnp.bfloat16)


def distance(slot, near, far):
    size, total = near * far, (slot % far) * near
    bit = 1
    while bit < near:
        size //= 2
        total = total + ((slot // size) % 2) * bit
        bit *= 2
    return total


def fold_kernel(own_ref, other_ref, keep_ref, away_ref):
    total = own_ref[...] + other_ref[...].astype(jnp.float32)
    half = keep_ref.shape[0]
    keep_ref[...] = total[:half]
    away_ref[...] = total[half:].astype(jnp.bfloat16)


def folded_kernel(own_ref, other_ref, out_ref):
    out_ref[...] = (own_ref[...] + other_ref[...].astype(jnp.float32)).astype(jnp.bfloat16)


def next_kernel(far, *refs):
    pieces, (hidden_ref, scale_ref, own_ref, out_ref) = refs[:far], refs[far:]
    sums = []
    for k in range(far):
        piece = pieces[k][...].astype(jnp.float32)
        sums.append(jnp.concatenate([piece[j ^ k : (j ^ k) + 1] for j in range(far)], axis=0))
    while len(sums) > 1:
        sums = [sums[i] + sums[i + 1] for i in range(0, len(sums), 2)]
    total = sums[0].astype(jnp.bfloat16).astype(jnp.float32)
    hidden = (hidden_ref[...].astype(jnp.float32) + total).astype(jnp.bfloat16)
    own_ref[...] = hidden.astype(jnp.float32)[:1].astype(jnp.bfloat16)
    out_ref[...] = normalized(hidden.astype(jnp.float32), row_of(scale_ref))


def sum_kernel(amount, *refs):
    total = refs[0][...].astype(jnp.float32)
    for ref in refs[1:amount]:
        total = total + ref[...].astype(jnp.float32)
    refs[-1][...] = total.astype(refs[-1].dtype)


def project_kernel(rows_ref, query_w, fresh_w, query_ref, fresh_ref):
    query_ref[...] = dot(rows_ref[...], query_w[...])
    fresh_ref[...] = dot(rows_ref[...], fresh_w[...])


def up_kernel(parts, *refs):
    lows, (query_ref, fresh_ref, adapter_ref, up_ref, out_ref, held) = refs[:parts], refs[parts:]
    count, columns = query_ref.shape
    rank = lows[0].shape[1]
    low = lows[0][...].astype(jnp.float32)
    for ref in lows[1:]:
        low = low + ref[...].astype(jnp.float32)
    low = low.astype(jnp.bfloat16)
    query = query_ref[...]
    table = up_ref.shape[0]
    some = min(table, 32)
    wide = some * rank
    repeat = (iota((rank, wide), 1) % rank == iota((rank, wide), 0)).astype(jnp.bfloat16)
    wide_low = dot(low, repeat)
    place = iota((count, wide), 1) // rank
    for start in range(0, table, some):
        spread = jnp.where(place + start == adapter_ref[...], wide_low, 0.0).astype(jnp.bfloat16)
        query = query + dot(spread, up_ref[start : start + some].reshape(wide, columns))
    line = out_ref.shape[2]
    lines = columns // line
    held[...] = jnp.zeros(held.shape, jnp.float32)
    for c in range(lines):
        held[:, c, :] = query[:, c * line : (c + 1) * line]
    fresh = fresh_ref[...]
    if fresh.shape[1] < line:
        fresh = jnp.concatenate(
            [fresh, jnp.zeros((count, line - fresh.shape[1]), jnp.float32)], axis=1
        )
    held[:, lines, :] = fresh
    for k in range(count):
        out_ref[k] = held[k].astype(jnp.bfloat16)


def pieces_of(lines, select, whole, size):
    if size >= whole:
        total = dot(select(len(lines), 0), lines[0])
        for c in range(1, len(lines)):
            total = total + dot(select(len(lines), c), lines[c])
        return total
    return jnp.concatenate([dot(select(0, p), lines[0]) for p in range(whole // size)], axis=1)


def attend_kernel(columns, fresh_columns, first, *refs):
    lines_ref, length_ref, cache_ref = refs[:3]
    refs = refs[3:]
    if not first:
        past, refs = refs[:2], refs[2:]
    out_ref, refs = refs[0], refs[1:]
    if first:
        keep, refs = refs[:2], refs[2:]
    held, scores = refs
    count, _, line = lines_ref.shape
    cache = cache_ref.shape[2]
    for k in range(count):
        held[k] = lines_ref[k].astype(jnp.float32)
    each = columns // line
    lines = [held[:, c, :].astype(jnp.bfloat16) for c in range(each + 1)]
    origin = iota((H, count), 1)
    head = iota((H, count), 0)

    def query_pick(each, c):
        if each:
            return (head == origin * each + c).astype(jnp.bfloat16)
        return (head * (HD // columns) + c == origin).astype(jnp.bfloat16)

    def fresh_pick(offset):
        def pick(each, c):
            want = head // GROUP + offset
            if each:
                return (want == origin * each + c).astype(jnp.bfloat16)
            return (want * (HD // fresh_columns) + c == origin).astype(jnp.bfloat16)

        return pick

    query = pieces_of(lines[:each], query_pick, HD, columns)
    fresh = [lines[each][:, :fresh_columns]]
    new = [
        (
            pieces_of(fresh, fresh_pick(0), HD, fresh_columns),
            pieces_of(fresh, fresh_pick(KVH), HD, fresh_columns),
        )
    ]
    if first:
        keep[0][...], keep[1][...] = new[0]
    else:
        new.insert(0, (past[0][...], past[1][...]))
    scale = 1.0 / math.sqrt(HD)
    for j in range(KVH):
        rows = slice(j * GROUP, (j + 1) * GROUP)
        scores[rows, :] = dot(
            query[rows].astype(jnp.bfloat16), cache_ref[0, 0, :, j * HD : (j + 1) * HD], LAST
        )
    in_cache = iota((H, cache), 1) < length_ref[0:1, 0:1]
    old = jnp.where(in_cache, scores[...] * scale, -jnp.inf)
    news = [jnp.sum(query * keys, axis=1, keepdims=True) * scale for keys, _ in new]
    peak = jnp.max(old, axis=1, keepdims=True)
    for score in news:
        peak = jnp.maximum(peak, score)
    old = jnp.exp(old - peak)
    news = [jnp.exp(score - peak) for score in news]
    total = jnp.sum(old, axis=1, keepdims=True)
    for score in news:
        total = total + score
    old = old / total
    extra = jnp.zeros((H, HD), jnp.float32)
    for score, (_, values) in zip(news, new):
        extra = extra + (score / total).astype(jnp.bfloat16).astype(jnp.float32) * values
    mixed = jnp.concatenate(
        [
            dot(
                old[j * GROUP : (j + 1) * GROUP].astype(jnp.bfloat16),
                cache_ref[0, 1, :, j * HD : (j + 1) * HD],
            )
            for j in range(KVH)
        ],
        axis=0,
    )
    mixed = mixed + extra
    if columns >= HD:
        for k in range(count):
            out_ref[k] = mixed[k * each : (k + 1) * each].astype(jnp.bfloat16)
    else:
        parts = HD // columns
        out = jnp.zeros((count, columns), jnp.float32)
        for p in range(parts):
            pick = (iota((count, H), 1) * parts + p == iota((count, H), 0)).astype(jnp.bfloat16)
            out = out + dot(pick, mixed[:, p * columns : (p + 1) * columns].astype(jnp.bfloat16))
        for k in range(count):
            out_ref[k] = out[k : k + 1].astype(jnp.bfloat16)


def output_kernel(split, lines_ref, me_ref, weight_ref, own_ref, away_ref, held):
    count, each, line = lines_ref.shape
    chips = count // CORES
    for k in range(count):
        held[k, :each, :] = lines_ref[k].astype(jnp.float32)
    slot = iota((count, count), 0)
    if split:
        origin = me_ref[0] ^ distance(slot, *split)
    else:
        origin = (slot % chips) * CORES + ((me_ref[0] % CORES) ^ (slot // chips))
    order = (iota((count, count), 1) == origin).astype(jnp.bfloat16)
    rows = jnp.concatenate(
        [dot(order, held[:, c, :].astype(jnp.bfloat16)).astype(jnp.bfloat16) for c in range(each)],
        axis=1,
    )
    width = weight_ref.shape[1]
    wide = width // 8
    for c in range(8):
        part = slice(c * wide, (c + 1) * wide)
        out = dot(rows, weight_ref[:, part])
        own_ref[:, part] = out[:chips]
        away_ref[:, part] = out[chips:].astype(jnp.bfloat16)


def partial_kernel(own_ref, other_ref, out_ref):
    total = own_ref[...] + other_ref[...].astype(jnp.float32)
    wide = out_ref.shape[2]
    for k in range(out_ref.shape[0]):
        for i in range(FOLD):
            out_ref[k, i : i + 1, :] = total[k : k + 1, i * wide : (i + 1) * wide].astype(
                out_ref.dtype
            )


def finish_kernel(parts_ref, hidden_ref, out_ref):
    total = parts_ref[0].astype(jnp.float32)
    for k in range(1, parts_ref.shape[0]):
        total = total + parts_ref[k].astype(jnp.float32)
    total = jnp.concatenate([total[i : i + 1] for i in range(FOLD)], axis=1)
    total = total.astype(jnp.bfloat16).astype(jnp.float32)
    before = hidden_ref[...].astype(jnp.float32)
    out_ref[...] = jnp.concatenate([before, before + total], axis=0).astype(jnp.bfloat16)


def shards(
    hidden_state_input,
    attention_norm_scale,
    query_weight,
    key_value_weight,
    output_weight,
    adapter_down_weight,
    adapter_up_weight,
    row_adapter_index,
    adapter_storage_index,
    cache_length_per_row,
    key_value_cache,
):
    count = lax.axis_size(AXIS)
    chips = count // CORES
    far, near = split_of(count)
    far_steps = [k * near for k in range(1, far)]
    near_steps = list(range(1, near))
    kept, width, rank = adapter_down_weight.shape
    columns = query_weight.shape[1]
    fresh_columns = key_value_weight.shape[1]
    line = min(HD, columns)
    smem, vmem = pltpu.SMEM, pltpu.VMEM
    me = lax.axis_index(AXIS).astype(jnp.int32).reshape(1)
    down = adapter_down_weight.transpose(0, 2, 1)
    scale = attention_norm_scale.reshape(-1, LANES)
    storage = adapter_storage_index[None]

    def stash(token, arrays, *behind):
        outs = call(
            functools.partial(stash_kernel, len(arrays)),
            [pltpu.VMEM(a.shape, a.dtype) for a in arrays] + [shape((8, LANES), jnp.int32)],
            "stash",
            [pltpu.SemaphoreType.DMA((len(arrays),))],
            moved=sum(2 * a.size for a in arrays),
        )(
            token,
            *(pltpu.with_memory_space_constraint(a, pltpu.HBM) for a in arrays),
            *behind,
            specs=[vmem] + [pltpu.HBM] * len(arrays) + [pl.ANY] * len(behind),
        )
        return outs[:-1], outs[-1]

    hidden = hidden_state_input
    carried, length = call(
        first_kernel, [shape((1, width + LANES)), shape((8, LANES), jnp.int32)], "first"
    )(
        hidden,
        row_adapter_index,
        cache_length_per_row,
        me,
        specs=[vmem, smem, smem, smem],
    )
    past = ()
    for step in range(STEPS):
        first, last = step == 0, step == STEPS - 1
        outs = [shape((count, width)), shape((count, rank))]
        scratch = [pltpu.VMEM((count, width), jnp.float32)]
        if first:
            (query_w, down_w), token = stash(length, [query_weight, down])
            pieces = across(carried, far_steps, count)
            column, carried = call(
                functools.partial(join_kernel, far),
                [shape((far, width)), shape((far, width + LANES))],
                "join",
            )(*pieces, scale, token)
            (output_w,), token = stash(token, [output_weight])
            pieces = across(carried, near_steps, count)
            member, adapter = call(
                functools.partial(member_kernel, near, far, width),
                [shape((count, kept), jnp.int32), shape((count, 1), jnp.int32)],
                "member",
                [pltpu.VMEM((count, LANES), jnp.float32)],
            )(*pieces, me, storage, token, specs=[vmem] * near + [smem, vmem, vmem])
        else:
            pieces = across(carried, near_steps, count)
        rows, low = call(functools.partial(low_kernel, near, far), outs, "low", scratch)(
            *pieces, me, member, down_w, specs=[vmem] * near + [smem, vmem, vmem]
        )
        behind = []
        if first:
            rest = [key_value_weight, adapter_up_weight, key_value_cache]
            (fresh_w, up_w, cache), token = stash(token, rest, low)
            behind = [token]
        (low,) = call(functools.partial(sum_kernel, near), [shape((count, rank))], "sum")(
            *across(low, near_steps, count), *behind
        )
        lows = across(low, far_steps, count)
        query, fresh = call(
            project_kernel,
            [shape((count, columns), jnp.float32), shape((count, fresh_columns), jnp.float32)],
            "project",
            flops=2 * count * width * (columns + fresh_columns),
            moved=2 * width * (columns + fresh_columns),
        )(rows, query_w, fresh_w)
        (lines,) = call(
            functools.partial(up_kernel, far),
            [shape((count, 8, line))],
            "up",
            [pltpu.VMEM((count, 8, line), jnp.float32)],
        )(*lows, query, fresh, adapter, up_w)

        lines = swap(lines)
        outs = [shape((count, columns // line, line))]
        if first:
            outs = outs + [shape((H, HD), jnp.float32)] * 2
        outs = call(
            functools.partial(attend_kernel, columns, fresh_columns, first),
            outs,
            "attend",
            [
                pltpu.VMEM((count, 8, line), jnp.float32),
                pltpu.VMEM((H, key_value_cache.shape[2]), jnp.float32),
            ],
            moved=2 << 20,
        )(
            lines,
            length,
            cache,
            *past,
            specs=[vmem] * (3 + len(past)),
        )
        if first:
            past = tuple(outs[1:])

        lines = swap(outs[0])
        own, away = call(
            functools.partial(output_kernel, None if last else (near, far)),
            [shape((chips, width), jnp.float32), shape((chips, width))],
            "output",
            [pltpu.VMEM((count, 8, line), jnp.float32)],
            flops=2 * count * width * columns,
            moved=2 * width * columns,
        )(lines, me, output_w, specs=[vmem, smem, vmem])

        if last:
            (parts,) = call(partial_kernel, [shape((chips, FOLD, width // FOLD))], "partial")(
                own, shift(away, 1, count)
            )
            parts = chips_swap(parts, count)
            (out,) = call(finish_kernel, [shape((STEPS, width))], "finish")(parts, hidden)
            return out.reshape(STEPS, 1, width)
        bit = 1
        while bit < near // 2:
            half = own.shape[0] // 2
            own, away = call(
                fold_kernel, [shape((half, width), jnp.float32), shape((half, width))], "fold"
            )(own, shift(away, bit, count))
            bit *= 2
        (own,) = call(folded_kernel, [shape((far, width))], "fold")(own, shift(away, bit, count))
        hidden, carried = call(
            functools.partial(next_kernel, far), [shape((1, width)), shape((far, width))], "next"
        )(*across(own, far_steps, count), column, scale)


def solution(mesh):
    in_specs = (
        P(("groups", "replica"), None),
        P(),
        P(None, "replica"),
        P(None, "replica"),
        P("replica", None),
        P("replica", None, None),
        P(None, None, "replica"),
        P(("groups", "replica")),
        P(),
        P(("groups", "replica")),
        P(("groups", "replica"), None, None, None),
    )
    out_specs = P(None, ("groups", "replica"), None)
    return jax.shard_map(shards, mesh=mesh, in_specs=in_specs, out_specs=out_specs, check_vma=False)
```

```python
import functools
import math

import jax
import jax.numpy as jnp
from jax import lax
from jax.experimental import pallas as pl
from jax.experimental.pallas import tpu as pltpu
from jax.sharding import PartitionSpec as P

H = 64
KVH = 8
HD = 128
STEPS = 2
GROUP = H // KVH
EPS = 1e-05
AXIS = "replica"
LANES = 128
LAST = (((1,), (1,)), ((), ()))
FIRST = (((0,), (0,)), ((), ()))

CORES = 2
FOLD = 8


def split_of(count):
    far = 1 << (count.bit_length() // 2)
    return far, count // far


def shift(block, distance, count):
    return lax.ppermute(block, AXIS, [(i, i ^ distance) for i in range(count)])


def across(block, strides, count):
    return [block] + [shift(block, d, count) for d in strides]


def swap(blocks):
    return lax.all_to_all(blocks, AXIS, split_axis=0, concat_axis=0, tiled=True)


def chips_swap(blocks, count):
    groups = [[i for i in range(count) if i % CORES == c] for c in range(CORES)]
    return lax.all_to_all(
        blocks, AXIS, split_axis=0, concat_axis=0, axis_index_groups=groups, tiled=True
    )


def call(body, outs, name, scratch=(), vmem=20 << 20, flops=1 << 20, moved=1 << 18):
    def run(*operands, specs=None):
        specs = specs or [pltpu.VMEM] * len(operands)
        return pl.pallas_call(
            body,
            out_shape=outs,
            in_specs=[pl.BlockSpec(memory_space=s) for s in specs],
            out_specs=[pl.BlockSpec(memory_space=pltpu.VMEM)] * len(outs),
            scratch_shapes=list(scratch),
            compiler_params=pltpu.CompilerParams(vmem_limit_bytes=vmem),
            cost_estimate=pl.CostEstimate(flops=flops, bytes_accessed=moved, transcendentals=0),
            name=name,
        )(*operands)

    return run


def shape(dims, dtype=jnp.bfloat16):
    return jax.ShapeDtypeStruct(dims, dtype)


def iota(dims, axis):
    return lax.broadcasted_iota(jnp.int32, dims, axis)


def dot(a, b, contract=(((1,), (0,)), ((), ()))):
    return lax.dot_general(a, b, contract, preferred_element_type=jnp.float32)


def normalized(hidden, scale):
    factor = lax.rsqrt(jnp.mean(hidden * hidden, axis=-1, keepdims=True) + EPS)
    return (hidden * factor * scale).astype(jnp.bfloat16)


def row_of(ref):
    lines = ref[...].astype(jnp.float32)
    return jnp.concatenate([lines[i : i + 1] for i in range(lines.shape[0])], axis=1)


def first_kernel(hidden_ref, adapter_ref, length_ref, _, out_ref, length_out):
    length_out[...] = jnp.full(length_out.shape, length_ref[0], jnp.int32)
    width = hidden_ref.shape[1]
    out_ref[:, :width] = hidden_ref[...]
    digit = iota((1, LANES), 1)
    adapter = adapter_ref[0]
    high, low = adapter // 256, adapter % 256
    digits = jnp.where(digit == 0, low, jnp.where(digit == 1, high, 0)).astype(jnp.float32)
    out_ref[:, width:] = digits.astype(jnp.bfloat16)


def stash_kernel(amount, token_ref, *refs):
    sources, refs = refs[:amount], refs[amount:]
    outs, out_token, sems = refs[-2 - amount : -2], refs[-2], refs[-1]
    copies = [
        pltpu.make_async_copy(sources[i], outs[i], sems.at[i]) for i in range(amount)
    ]
    for copy in copies:
        copy.start()
    out_token[...] = token_ref[...]
    for copy in copies:
        copy.wait()


def low_terms(held, member_ref, down_ref, rows_ref, low_ref):
    rows = held[...].astype(jnp.bfloat16)
    rows_ref[...] = rows
    low = jnp.zeros(low_ref.shape, jnp.float32)
    for index in range(down_ref.shape[0]):
        part = dot(rows, down_ref[index], LAST)
        low = jnp.where(member_ref[:, index : index + 1] > 0, part, low)
    low_ref[...] = low.astype(jnp.bfloat16)


def gathered(near, far, pieces, me, held):
    width = held.shape[1]
    for l in range(near):
        block = pieces[l][:, :width].astype(jnp.float32)
        for k in range(far):
            held[pl.ds(me ^ (k * near + l), 1), :] = block[k : k + 1]


def low_kernel(near, far, *refs):
    pieces, refs = refs[:near], refs[near:]
    me_ref, member_ref, down_ref, rows_ref, low_ref, held = refs
    gathered(near, far, pieces, me_ref[0], held)
    low_terms(held, member_ref, down_ref, rows_ref, low_ref)


def low_first_kernel(near, far, *refs):
    pieces, refs = refs[:near], refs[near:]
    me_ref, storage_ref, down_ref, _, rows_ref, low_ref, member_ref, adapter_ref = refs[:8]
    held, digits = refs[-2:]
    width = held.shape[1]
    me = me_ref[0]
    kept = member_ref.shape[1]
    count = near * far
    for l in range(near):
        block = pieces[l][:, width:].astype(jnp.float32)
        for k in range(far):
            digits[pl.ds(me ^ (k * near + l), 1), :] = block[k : k + 1]
    adapter = (digits[:, 0:1] + 256.0 * digits[:, 1:2]).astype(jnp.int32)
    adapter_ref[...] = adapter
    table = storage_ref.shape[1]
    chosen = jnp.where(iota((count, table), 1) == adapter, storage_ref[...], 0)
    storage = jnp.sum(chosen.astype(jnp.float32), axis=1, keepdims=True).astype(jnp.int32)
    member_ref[...] = (storage - me * kept == iota((count, kept), 1)).astype(jnp.int32)
    gathered(near, far, pieces, me, held)
    low_terms(held, member_ref, down_ref, rows_ref, low_ref)


def join_kernel(amount, *refs):
    scale_ref, _, hidden_ref, out_ref = refs[amount:]
    width = hidden_ref.shape[1]
    rows = [ref[...].astype(jnp.float32) for ref in refs[:amount]]
    rows = jnp.concatenate(rows, axis=0)
    hidden = rows[:, :width]
    hidden_ref[...] = hidden.astype(jnp.bfloat16)
    out_ref[:, :width] = normalized(hidden, row_of(scale_ref))
    out_ref[:, width:] = rows[:, width:].astype(jnp.bfloat16)


def fold_kernel(*refs):
    total = refs[0][...]
    for ref in refs[1:-1]:
        total = total + ref[...].astype(jnp.float32)
    refs[-1][...] = total.astype(jnp.bfloat16)


def next_kernel(far, *refs):
    pieces, (hidden_ref, scale_ref, own_ref, out_ref) = refs[:far], refs[far:]
    sums = []
    for k in range(far):
        piece = pieces[k][...].astype(jnp.float32)
        sums.append(jnp.concatenate([piece[j ^ k : (j ^ k) + 1] for j in range(far)], axis=0))
    while len(sums) > 1:
        sums = [sums[i] + sums[i + 1] for i in range(0, len(sums), 2)]
    total = sums[0].astype(jnp.bfloat16).astype(jnp.float32)
    hidden = (hidden_ref[...].astype(jnp.float32) + total).astype(jnp.bfloat16)
    own_ref[...] = hidden.astype(jnp.float32)[:1].astype(jnp.bfloat16)
    out_ref[...] = normalized(hidden.astype(jnp.float32), row_of(scale_ref))


def sum_kernel(amount, *refs):
    total = refs[0][...].astype(jnp.float32)
    for ref in refs[1:amount]:
        total = total + ref[...].astype(jnp.float32)
    refs[-1][...] = total.astype(refs[-1].dtype)


def project_kernel(rows_ref, query_w, fresh_w, query_ref, fresh_ref):
    query_ref[...] = dot(rows_ref[...], query_w[...])
    fresh_ref[...] = dot(rows_ref[...], fresh_w[...])


def up_kernel(parts, *refs):
    lows, (query_ref, fresh_ref, adapter_ref, up_ref, out_ref, held) = refs[:parts], refs[parts:]
    count, columns = query_ref.shape
    rank = lows[0].shape[1]
    low = lows[0][...].astype(jnp.float32)
    for ref in lows[1:]:
        low = low + ref[...].astype(jnp.float32)
    low = low.astype(jnp.bfloat16)
    query = query_ref[...]
    table = up_ref.shape[0]
    some = min(table, 32)
    wide = some * rank
    low = low.astype(jnp.float32)
    wide_low = jnp.concatenate([low] * max(1, LANES // rank), axis=1)
    wide_low = jnp.concatenate([wide_low] * (wide // wide_low.shape[1]), axis=1)
    place = iota((count, wide), 1) // rank
    for start in range(0, table, some):
        spread = jnp.where(place + start == adapter_ref[...], wide_low, 0.0).astype(jnp.bfloat16)
        query = query + dot(spread, up_ref[start : start + some].reshape(wide, columns))
    line = out_ref.shape[2]
    lines = columns // line
    held[...] = jnp.zeros(held.shape, jnp.float32)
    for c in range(lines):
        held[:, c, :] = query[:, c * line : (c + 1) * line]
    fresh = fresh_ref[...]
    if fresh.shape[1] < line:
        fresh = jnp.concatenate(
            [fresh, jnp.zeros((count, line - fresh.shape[1]), jnp.float32)], axis=1
        )
    held[:, lines, :] = fresh
    for k in range(count):
        out_ref[k] = held[k].astype(jnp.bfloat16)


def pieces_of(lines, select, whole, size):
    if size >= whole:
        total = dot(select(len(lines), 0), lines[0])
        for c in range(1, len(lines)):
            total = total + dot(select(len(lines), c), lines[c])
        return total
    return jnp.concatenate([dot(select(0, p), lines[0]) for p in range(whole // size)], axis=1)


def attend_kernel(columns, fresh_columns, first, *refs):
    lines_ref, length_ref, cache_ref = refs[:3]
    refs = refs[3:]
    if not first:
        past, refs = refs[:2], refs[2:]
    out_ref, refs = refs[0], refs[1:]
    if first:
        keep, refs = refs[:2], refs[2:]
    held, scores = refs
    count, _, line = lines_ref.shape
    cache = cache_ref.shape[2]
    for k in range(count):
        held[k] = lines_ref[k].astype(jnp.float32)
    each = columns // line
    lines = [held[:, c, :].astype(jnp.bfloat16) for c in range(each + 1)]
    origin = iota((H, count), 1)
    head = iota((H, count), 0)

    def query_pick(each, c):
        if each:
            return (head == origin * each + c).astype(jnp.bfloat16)
        return (head * (HD // columns) + c == origin).astype(jnp.bfloat16)

    def fresh_pick(offset):
        def pick(each, c):
            want = head // GROUP + offset
            if each:
                return (want == origin * each + c).astype(jnp.bfloat16)
            return (want * (HD // fresh_columns) + c == origin).astype(jnp.bfloat16)

        return pick

    query = pieces_of(lines[:each], query_pick, HD, columns)
    fresh = [lines[each][:, :fresh_columns]]
    new = [
        (
            pieces_of(fresh, fresh_pick(0), HD, fresh_columns),
            pieces_of(fresh, fresh_pick(KVH), HD, fresh_columns),
        )
    ]
    if first:
        keep[0][...], keep[1][...] = new[0]
    else:
        new.insert(0, (past[0][...], past[1][...]))
    scale = 1.0 / math.sqrt(HD)
    for j in range(KVH):
        rows = slice(j * GROUP, (j + 1) * GROUP)
        scores[rows, :] = dot(
            query[rows].astype(jnp.bfloat16), cache_ref[0, 0, :, j * HD : (j + 1) * HD], LAST
        )
    in_cache = iota((H, cache), 1) < length_ref[0:1, 0:1]
    old = jnp.where(in_cache, scores[...] * scale, -jnp.inf)
    news = [jnp.sum(query * keys, axis=1, keepdims=True) * scale for keys, _ in new]
    peak = jnp.max(old, axis=1, keepdims=True)
    for score in news:
        peak = jnp.maximum(peak, score)
    old = jnp.exp(old - peak)
    news = [jnp.exp(score - peak) for score in news]
    total = jnp.sum(old, axis=1, keepdims=True)
    for score in news:
        total = total + score
    old = old / total
    extra = jnp.zeros((H, HD), jnp.float32)
    for score, (_, values) in zip(news, new):
        extra = extra + (score / total).astype(jnp.bfloat16).astype(jnp.float32) * values
    mixed = jnp.concatenate(
        [
            dot(
                old[j * GROUP : (j + 1) * GROUP].astype(jnp.bfloat16),
                cache_ref[0, 1, :, j * HD : (j + 1) * HD],
            )
            for j in range(KVH)
        ],
        axis=0,
    )
    mixed = mixed + extra
    if columns >= HD:
        for k in range(count):
            out_ref[k] = mixed[k * each : (k + 1) * each].astype(jnp.bfloat16)
    else:
        parts = HD // columns
        out = jnp.zeros((count, columns), jnp.float32)
        for p in range(parts):
            pick = (iota((count, H), 1) * parts + p == iota((count, H), 0)).astype(jnp.bfloat16)
            out = out + dot(pick, mixed[:, p * columns : (p + 1) * columns].astype(jnp.bfloat16))
        for k in range(count):
            out_ref[k] = out[k : k + 1].astype(jnp.bfloat16)


def output_kernel(split, lines_ref, me_ref, weight_ref, own_ref, *refs):
    aways, held = refs[:-1], refs[-1]
    count, each, line = lines_ref.shape
    chips = count // CORES
    for k in range(count):
        held[k, :each, :] = lines_ref[k].astype(jnp.float32)
    slot = iota((count, count), 0)
    if split:
        near, far = split
        origin = me_ref[0] ^ ((slot % far) * near + slot // far)
    else:
        origin = (slot % chips) * CORES + ((me_ref[0] % CORES) ^ (slot // chips))
    order = (iota((count, count), 1) == origin).astype(jnp.bfloat16)
    rows = jnp.concatenate(
        [dot(order, held[:, c, :].astype(jnp.bfloat16)).astype(jnp.bfloat16) for c in range(each)],
        axis=1,
    )
    width = weight_ref.shape[1]
    wide = width // 8
    for c in range(8):
        part = slice(c * wide, (c + 1) * wide)
        out = dot(rows, weight_ref[:, part])
        some = own_ref.shape[0]
        own_ref[:, part] = out[:some]
        for l, ref in enumerate(aways):
            ref[:, part] = out[(l + 1) * some : (l + 2) * some].astype(jnp.bfloat16)


def partial_kernel(own_ref, other_ref, out_ref):
    total = own_ref[...] + other_ref[...].astype(jnp.float32)
    wide = out_ref.shape[2]
    for k in range(out_ref.shape[0]):
        for i in range(FOLD):
            out_ref[k, i : i + 1, :] = total[k : k + 1, i * wide : (i + 1) * wide].astype(
                out_ref.dtype
            )


def finish_kernel(parts_ref, hidden_ref, out_ref):
    total = parts_ref[0].astype(jnp.float32)
    for k in range(1, parts_ref.shape[0]):
        total = total + parts_ref[k].astype(jnp.float32)
    total = jnp.concatenate([total[i : i + 1] for i in range(FOLD)], axis=1)
    total = total.astype(jnp.bfloat16).astype(jnp.float32)
    before = hidden_ref[...].astype(jnp.float32)
    out_ref[...] = jnp.concatenate([before, before + total], axis=0).astype(jnp.bfloat16)


def shards(
    hidden_state_input,
    attention_norm_scale,
    query_weight,
    key_value_weight,
    output_weight,
    adapter_down_weight,
    adapter_up_weight,
    row_adapter_index,
    adapter_storage_index,
    cache_length_per_row,
    key_value_cache,
):
    count = lax.axis_size(AXIS)
    chips = count // CORES
    far, near = split_of(count)
    far_steps = [k * near for k in range(1, far)]
    near_steps = list(range(1, near))
    kept, width, rank = adapter_down_weight.shape
    columns = query_weight.shape[1]
    fresh_columns = key_value_weight.shape[1]
    line = min(HD, columns)
    smem, vmem = pltpu.SMEM, pltpu.VMEM
    me = lax.axis_index(AXIS).astype(jnp.int32).reshape(1)
    down = adapter_down_weight.transpose(0, 2, 1)
    scale = attention_norm_scale.reshape(-1, LANES)
    storage = adapter_storage_index[None]

    def stash(token, arrays, *behind):
        outs = call(
            functools.partial(stash_kernel, len(arrays)),
            [pltpu.VMEM(a.shape, a.dtype) for a in arrays] + [shape((8, LANES), jnp.int32)],
            "stash",
            [pltpu.SemaphoreType.DMA((len(arrays),))],
            moved=sum(2 * a.size for a in arrays),
        )(
            token,
            *(pltpu.with_memory_space_constraint(a, pltpu.HBM) for a in arrays),
            *behind,
            specs=[vmem] + [pltpu.HBM] * len(arrays) + [pl.ANY] * len(behind),
        )
        return outs[:-1], outs[-1]

    hidden = hidden_state_input
    carried, length = call(
        first_kernel, [shape((1, width + LANES)), shape((8, LANES), jnp.int32)], "first"
    )(
        hidden,
        row_adapter_index,
        cache_length_per_row,
        me,
        specs=[vmem, smem, smem, smem],
    )
    past = ()
    for step in range(STEPS):
        first, last = step == 0, step == STEPS - 1
        outs = [shape((count, width)), shape((count, rank))]
        scratch = [pltpu.VMEM((count, width), jnp.float32)]
        if first:
            (query_w, down_w), token = stash(length, [query_weight, down])
            pieces = across(carried, far_steps, count)
            column, carried = call(
                functools.partial(join_kernel, far),
                [shape((far, width)), shape((far, width + LANES))],
                "join",
            )(*pieces, scale, token)
            (output_w,), token = stash(token, [output_weight])
            pieces = across(carried, near_steps, count)
            outs = outs + [shape((count, kept), jnp.int32), shape((count, 1), jnp.int32)]
            rows, low, member, adapter = call(
                functools.partial(low_first_kernel, near, far),
                outs,
                "low",
                scratch + [pltpu.VMEM((count, LANES), jnp.float32)],
            )(
                *pieces,
                me,
                storage,
                down_w,
                token,
                specs=[vmem] * near + [smem] + [vmem] * 3,
            )
        else:
            pieces = across(carried, near_steps, count)
            rows, low = call(functools.partial(low_kernel, near, far), outs, "low", scratch)(
                *pieces, me, member, down_w, specs=[vmem] * near + [smem, vmem, vmem]
            )
        behind = []
        if first:
            rest = [key_value_weight, adapter_up_weight, key_value_cache]
            (fresh_w, up_w, cache), token = stash(token, rest, low)
            behind = [token]
        (low,) = call(functools.partial(sum_kernel, near), [shape((count, rank))], "sum")(
            *across(low, near_steps, count), *behind
        )
        lows = across(low, far_steps, count)
        query, fresh = call(
            project_kernel,
            [shape((count, columns), jnp.float32), shape((count, fresh_columns), jnp.float32)],
            "project",
            flops=2 * count * width * (columns + fresh_columns),
            moved=2 * width * (columns + fresh_columns),
        )(rows, query_w, fresh_w)
        (lines,) = call(
            functools.partial(up_kernel, far),
            [shape((count, 8, line))],
            "up",
            [pltpu.VMEM((count, 8, line), jnp.float32)],
        )(*lows, query, fresh, adapter, up_w)

        lines = swap(lines)
        outs = [shape((count, columns // line, line))]
        if first:
            outs = outs + [shape((H, HD), jnp.float32)] * 2
        outs = call(
            functools.partial(attend_kernel, columns, fresh_columns, first),
            outs,
            "attend",
            [
                pltpu.VMEM((count, 8, line), jnp.float32),
                pltpu.VMEM((H, key_value_cache.shape[2]), jnp.float32),
            ],
            moved=2 << 20,
        )(
            lines,
            length,
            cache,
            *past,
            specs=[vmem] * (3 + len(past)),
        )
        if first:
            past = tuple(outs[1:])

        lines = swap(outs[0])
        some = chips if last else far
        own, *aways = call(
            functools.partial(output_kernel, None if last else (near, far)),
            [shape((some, width), jnp.float32)] + [shape((some, width))] * (count // some - 1),
            "output",
            [pltpu.VMEM((count, 8, line), jnp.float32)],
            flops=2 * count * width * columns,
            moved=2 * width * columns,
        )(lines, me, output_w, specs=[vmem, smem, vmem])

        if last:
            (parts,) = call(partial_kernel, [shape((chips, FOLD, width // FOLD))], "partial")(
                own, shift(aways[0], 1, count)
            )
            parts = chips_swap(parts, count)
            (out,) = call(finish_kernel, [shape((STEPS, width))], "finish")(parts, hidden)
            return out.reshape(STEPS, 1, width)
        aways = [shift(a, d, count) for a, d in zip(aways, near_steps)]
        (own,) = call(fold_kernel, [shape((far, width))], "fold")(own, *aways)
        hidden, carried = call(
            functools.partial(next_kernel, far), [shape((1, width)), shape((far, width))], "next"
        )(*across(own, far_steps, count), column, scale)


def solution(mesh):
    in_specs = (
        P(("groups", "replica"), None),
        P(),
        P(None, "replica"),
        P(None, "replica"),
        P("replica", None),
        P("replica", None, None),
        P(None, None, "replica"),
        P(("groups", "replica")),
        P(),
        P(("groups", "replica")),
        P(("groups", "replica"), None, None, None),
    )
    out_specs = P(None, ("groups", "replica"), None)
    return jax.shard_map(shards, mesh=mesh, in_specs=in_specs, out_specs=out_specs, check_vma=False)
```

```python
import functools
import math

import jax
import jax.numpy as jnp
from jax import lax
from jax.experimental import pallas as pl
from jax.experimental.pallas import tpu as pltpu
from jax.sharding import PartitionSpec as P

H = 64
KVH = 8
HD = 128
STEPS = 2
GROUP = H // KVH
EPS = 1e-05
AXIS = "replica"
LANES = 128
LAST = (((1,), (1,)), ((), ()))
FIRST = (((0,), (0,)), ((), ()))

CORES = 2
FOLD = 8


def split_of(count):
    far = 1 << (count.bit_length() // 2)
    return far, count // far


def shift(block, distance, count):
    return lax.ppermute(block, AXIS, [(i, i ^ distance) for i in range(count)])


def across(block, strides, count):
    return [block] + [shift(block, d, count) for d in strides]


def swap(blocks):
    return lax.all_to_all(blocks, AXIS, split_axis=0, concat_axis=0, tiled=True)


def chips_swap(blocks, count):
    groups = [[i for i in range(count) if i % CORES == c] for c in range(CORES)]
    return lax.all_to_all(
        blocks, AXIS, split_axis=0, concat_axis=0, axis_index_groups=groups, tiled=True
    )


def call(body, outs, name, scratch=(), vmem=20 << 20, flops=1 << 20, moved=1 << 18):
    def run(*operands, specs=None):
        specs = specs or [pltpu.VMEM] * len(operands)
        return pl.pallas_call(
            body,
            out_shape=outs,
            in_specs=[pl.BlockSpec(memory_space=s) for s in specs],
            out_specs=[pl.BlockSpec(memory_space=pltpu.VMEM)] * len(outs),
            scratch_shapes=list(scratch),
            compiler_params=pltpu.CompilerParams(vmem_limit_bytes=vmem),
            cost_estimate=pl.CostEstimate(flops=flops, bytes_accessed=moved, transcendentals=0),
            name=name,
        )(*operands)

    return run


def shape(dims, dtype=jnp.bfloat16):
    return jax.ShapeDtypeStruct(dims, dtype)


def iota(dims, axis):
    return lax.broadcasted_iota(jnp.int32, dims, axis)


def dot(a, b, contract=(((1,), (0,)), ((), ()))):
    return lax.dot_general(a, b, contract, preferred_element_type=jnp.float32)


def normalized(hidden, scale):
    factor = lax.rsqrt(jnp.mean(hidden * hidden, axis=-1, keepdims=True) + EPS)
    return (hidden * factor * scale).astype(jnp.bfloat16)


def row_of(ref):
    lines = ref[...].astype(jnp.float32)
    return jnp.concatenate([lines[i : i + 1] for i in range(lines.shape[0])], axis=1)


def first_kernel(hidden_ref, adapter_ref, length_ref, _, out_ref, length_out):
    length_out[...] = jnp.full(length_out.shape, length_ref[0], jnp.int32)
    width = hidden_ref.shape[1]
    out_ref[:, :width] = hidden_ref[...]
    digit = iota((1, LANES), 1)
    adapter = adapter_ref[0]
    high, low = adapter // 256, adapter % 256
    digits = jnp.where(digit == 0, low, jnp.where(digit == 1, high, 0)).astype(jnp.float32)
    out_ref[:, width:] = digits.astype(jnp.bfloat16)


def stash_kernel(amount, token_ref, *refs):
    sources, refs = refs[:amount], refs[amount:]
    outs, out_token, sems = refs[-2 - amount : -2], refs[-2], refs[-1]
    copies = [
        pltpu.make_async_copy(sources[i], outs[i], sems.at[i]) for i in range(amount)
    ]
    for copy in copies:
        copy.start()
    out_token[...] = token_ref[...]
    for copy in copies:
        copy.wait()


def low_terms(held, member_ref, down_ref, rows_ref, low_ref):
    rows = held[...].astype(jnp.bfloat16)
    rows_ref[...] = rows
    low = jnp.zeros(low_ref.shape, jnp.float32)
    for index in range(down_ref.shape[0]):
        part = dot(rows, down_ref[index], LAST)
        low = jnp.where(member_ref[:, index : index + 1] > 0, part, low)
    low_ref[...] = low.astype(jnp.bfloat16)


def gathered(near, far, pieces, me, held):
    width = held.shape[1]
    for l in range(near):
        block = pieces[l][:, :width].astype(jnp.float32)
        for k in range(far):
            held[pl.ds(me ^ (k * near + l), 1), :] = block[k : k + 1]


def low_kernel(near, far, *refs):
    pieces, refs = refs[:near], refs[near:]
    me_ref, member_ref, down_ref, rows_ref, low_ref, held = refs
    gathered(near, far, pieces, me_ref[0], held)
    low_terms(held, member_ref, down_ref, rows_ref, low_ref)


def low_first_kernel(near, far, *refs):
    pieces, refs = refs[:near], refs[near:]
    me_ref, storage_ref, down_ref, _, rows_ref, low_ref, member_ref, adapter_ref = refs[:8]
    held, digits = refs[-2:]
    width = held.shape[1]
    me = me_ref[0]
    kept = member_ref.shape[1]
    count = near * far
    for l in range(near):
        block = pieces[l][:, width:].astype(jnp.float32)
        for k in range(far):
            digits[pl.ds(me ^ (k * near + l), 1), :] = block[k : k + 1]
    adapter = (digits[:, 0:1] + 256.0 * digits[:, 1:2]).astype(jnp.int32)
    adapter_ref[...] = adapter
    table = storage_ref.shape[1]
    chosen = jnp.where(iota((count, table), 1) == adapter, storage_ref[...], 0)
    storage = jnp.sum(chosen.astype(jnp.float32), axis=1, keepdims=True).astype(jnp.int32)
    member_ref[...] = (storage - me * kept == iota((count, kept), 1)).astype(jnp.int32)
    gathered(near, far, pieces, me, held)
    low_terms(held, member_ref, down_ref, rows_ref, low_ref)


def join_kernel(amount, *refs):
    scale_ref, _, hidden_ref, out_ref = refs[amount:]
    width = hidden_ref.shape[1]
    rows = [ref[...].astype(jnp.float32) for ref in refs[:amount]]
    rows = jnp.concatenate(rows, axis=0)
    hidden = rows[:, :width]
    hidden_ref[...] = hidden.astype(jnp.bfloat16)
    out_ref[:, :width] = normalized(hidden, row_of(scale_ref))
    out_ref[:, width:] = rows[:, width:].astype(jnp.bfloat16)


def distance(slot, near, far):
    size, total = near * far, (slot % far) * near
    bit = 1
    while bit < near:
        size //= 2
        total = total + ((slot // size) % 2) * bit
        bit *= 2
    return total


def fold_kernel(own_ref, other_ref, keep_ref, away_ref):
    total = own_ref[...] + other_ref[...].astype(jnp.float32)
    half = keep_ref.shape[0]
    keep_ref[...] = total[:half]
    away_ref[...] = total[half:].astype(jnp.bfloat16)


def folded_kernel(own_ref, other_ref, out_ref):
    out_ref[...] = (own_ref[...] + other_ref[...].astype(jnp.float32)).astype(jnp.bfloat16)


def next_kernel(far, *refs):
    pieces, (hidden_ref, scale_ref, own_ref, out_ref) = refs[:far], refs[far:]
    sums = []
    for k in range(far):
        piece = pieces[k][...].astype(jnp.float32)
        sums.append(jnp.concatenate([piece[j ^ k : (j ^ k) + 1] for j in range(far)], axis=0))
    while len(sums) > 1:
        sums = [sums[i] + sums[i + 1] for i in range(0, len(sums), 2)]
    total = sums[0].astype(jnp.bfloat16).astype(jnp.float32)
    hidden = (hidden_ref[...].astype(jnp.float32) + total).astype(jnp.bfloat16)
    own_ref[...] = hidden.astype(jnp.float32)[:1].astype(jnp.bfloat16)
    out_ref[...] = normalized(hidden.astype(jnp.float32), row_of(scale_ref))


def sum_kernel(amount, *refs):
    total = refs[0][...].astype(jnp.float32)
    for ref in refs[1:amount]:
        total = total + ref[...].astype(jnp.float32)
    refs[-1][...] = total.astype(refs[-1].dtype)


def project_kernel(rows_ref, query_w, fresh_w, query_ref, fresh_ref):
    query_ref[...] = dot(rows_ref[...], query_w[...])
    fresh_ref[...] = dot(rows_ref[...], fresh_w[...])


def up_kernel(parts, *refs):
    lows, (query_ref, fresh_ref, adapter_ref, up_ref, out_ref, held) = refs[:parts], refs[parts:]
    count, columns = query_ref.shape
    rank = lows[0].shape[1]
    low = lows[0][...].astype(jnp.float32)
    for ref in lows[1:]:
        low = low + ref[...].astype(jnp.float32)
    low = low.astype(jnp.bfloat16)
    query = query_ref[...]
    table = up_ref.shape[0]
    some = min(table, 32)
    wide = some * rank
    low = low.astype(jnp.float32)
    wide_low = jnp.concatenate([low] * max(1, LANES // rank), axis=1)
    wide_low = jnp.concatenate([wide_low] * (wide // wide_low.shape[1]), axis=1)
    place = iota((count, wide), 1) // rank
    for start in range(0, table, some):
        spread = jnp.where(place + start == adapter_ref[...], wide_low, 0.0).astype(jnp.bfloat16)
        query = query + dot(spread, up_ref[start : start + some].reshape(wide, columns))
    line = out_ref.shape[2]
    lines = columns // line
    held[...] = jnp.zeros(held.shape, jnp.float32)
    for c in range(lines):
        held[:, c, :] = query[:, c * line : (c + 1) * line]
    fresh = fresh_ref[...]
    if fresh.shape[1] < line:
        fresh = jnp.concatenate(
            [fresh, jnp.zeros((count, line - fresh.shape[1]), jnp.float32)], axis=1
        )
    held[:, lines, :] = fresh
    for k in range(count):
        out_ref[k] = held[k].astype(jnp.bfloat16)


def pieces_of(lines, select, whole, size):
    if size >= whole:
        total = dot(select(len(lines), 0), lines[0])
        for c in range(1, len(lines)):
            total = total + dot(select(len(lines), c), lines[c])
        return total
    return jnp.concatenate([dot(select(0, p), lines[0]) for p in range(whole // size)], axis=1)


def attend_kernel(columns, fresh_columns, first, *refs):
    lines_ref, length_ref, cache_ref = refs[:3]
    refs = refs[3:]
    if not first:
        past, refs = refs[:2], refs[2:]
    out_ref, refs = refs[0], refs[1:]
    if first:
        keep, refs = refs[:2], refs[2:]
    held, scores = refs
    count, _, line = lines_ref.shape
    cache = cache_ref.shape[2]
    for k in range(count):
        held[k] = lines_ref[k].astype(jnp.float32)
    each = columns // line
    lines = [held[:, c, :].astype(jnp.bfloat16) for c in range(each + 1)]
    origin = iota((H, count), 1)
    head = iota((H, count), 0)

    def query_pick(each, c):
        if each:
            return (head == origin * each + c).astype(jnp.bfloat16)
        return (head * (HD // columns) + c == origin).astype(jnp.bfloat16)

    def fresh_pick(offset):
        def pick(each, c):
            want = head // GROUP + offset
            if each:
                return (want == origin * each + c).astype(jnp.bfloat16)
            return (want * (HD // fresh_columns) + c == origin).astype(jnp.bfloat16)

        return pick

    query = pieces_of(lines[:each], query_pick, HD, columns)
    fresh = [lines[each][:, :fresh_columns]]
    new = [
        (
            pieces_of(fresh, fresh_pick(0), HD, fresh_columns),
            pieces_of(fresh, fresh_pick(KVH), HD, fresh_columns),
        )
    ]
    if first:
        keep[0][...], keep[1][...] = new[0]
    else:
        new.insert(0, (past[0][...], past[1][...]))
    scale = 1.0 / math.sqrt(HD)
    for j in range(KVH):
        rows = slice(j * GROUP, (j + 1) * GROUP)
        scores[rows, :] = dot(
            query[rows].astype(jnp.bfloat16), cache_ref[0, 0, :, j * HD : (j + 1) * HD], LAST
        )
    in_cache = iota((H, cache), 1) < length_ref[0:1, 0:1]
    old = jnp.where(in_cache, scores[...] * scale, -jnp.inf)
    news = [jnp.sum(query * keys, axis=1, keepdims=True) * scale for keys, _ in new]
    peak = jnp.max(old, axis=1, keepdims=True)
    for score in news:
        peak = jnp.maximum(peak, score)
    old = jnp.exp(old - peak)
    news = [jnp.exp(score - peak) for score in news]
    total = jnp.sum(old, axis=1, keepdims=True)
    for score in news:
        total = total + score
    old = old / total
    extra = jnp.zeros((H, HD), jnp.float32)
    for score, (_, values) in zip(news, new):
        extra = extra + (score / total).astype(jnp.bfloat16).astype(jnp.float32) * values
    mixed = jnp.concatenate(
        [
            dot(
                old[j * GROUP : (j + 1) * GROUP].astype(jnp.bfloat16),
                cache_ref[0, 1, :, j * HD : (j + 1) * HD],
            )
            for j in range(KVH)
        ],
        axis=0,
    )
    mixed = mixed + extra
    if columns >= HD:
        for k in range(count):
            out_ref[k] = mixed[k * each : (k + 1) * each].astype(jnp.bfloat16)
    else:
        parts = HD // columns
        out = jnp.zeros((count, columns), jnp.float32)
        for p in range(parts):
            pick = (iota((count, H), 1) * parts + p == iota((count, H), 0)).astype(jnp.bfloat16)
            out = out + dot(pick, mixed[:, p * columns : (p + 1) * columns].astype(jnp.bfloat16))
        for k in range(count):
            out_ref[k] = out[k : k + 1].astype(jnp.bfloat16)


def output_kernel(split, lines_ref, me_ref, weight_ref, own_ref, away_ref, held):
    count, each, line = lines_ref.shape
    chips = count // CORES
    for k in range(count):
        held[k, :each, :] = lines_ref[k].astype(jnp.float32)
    slot = iota((count, count), 0)
    if split:
        origin = me_ref[0] ^ distance(slot, *split)
    else:
        origin = (slot % chips) * CORES + ((me_ref[0] % CORES) ^ (slot // chips))
    order = (iota((count, count), 1) == origin).astype(jnp.bfloat16)
    rows = jnp.concatenate(
        [dot(order, held[:, c, :].astype(jnp.bfloat16)).astype(jnp.bfloat16) for c in range(each)],
        axis=1,
    )
    width = weight_ref.shape[1]
    wide = width // 8
    for c in range(8):
        part = slice(c * wide, (c + 1) * wide)
        out = dot(rows, weight_ref[:, part])
        own_ref[:, part] = out[:chips]
        away_ref[:, part] = out[chips:].astype(jnp.bfloat16)


def partial_kernel(own_ref, other_ref, out_ref):
    total = own_ref[...] + other_ref[...].astype(jnp.float32)
    wide = out_ref.shape[2]
    for k in range(out_ref.shape[0]):
        for i in range(FOLD):
            out_ref[k, i : i + 1, :] = total[k : k + 1, i * wide : (i + 1) * wide].astype(
                out_ref.dtype
            )


def finish_kernel(parts_ref, hidden_ref, out_ref):
    total = parts_ref[0].astype(jnp.float32)
    for k in range(1, parts_ref.shape[0]):
        total = total + parts_ref[k].astype(jnp.float32)
    total = jnp.concatenate([total[i : i + 1] for i in range(FOLD)], axis=1)
    total = total.astype(jnp.bfloat16).astype(jnp.float32)
    before = hidden_ref[...].astype(jnp.float32)
    out_ref[...] = jnp.concatenate([before, before + total], axis=0).astype(jnp.bfloat16)


def shards(
    hidden_state_input,
    attention_norm_scale,
    query_weight,
    key_value_weight,
    output_weight,
    adapter_down_weight,
    adapter_up_weight,
    row_adapter_index,
    adapter_storage_index,
    cache_length_per_row,
    key_value_cache,
):
    count = lax.axis_size(AXIS)
    chips = count // CORES
    far, near = split_of(count)
    far_steps = [k * near for k in range(1, far)]
    near_steps = list(range(1, near))
    kept, width, rank = adapter_down_weight.shape
    columns = query_weight.shape[1]
    fresh_columns = key_value_weight.shape[1]
    line = min(HD, columns)
    smem, vmem = pltpu.SMEM, pltpu.VMEM
    me = lax.axis_index(AXIS).astype(jnp.int32).reshape(1)
    down = adapter_down_weight.transpose(0, 2, 1)
    scale = attention_norm_scale.reshape(-1, LANES)
    storage = adapter_storage_index[None]

    def stash(token, arrays, *behind):
        outs = call(
            functools.partial(stash_kernel, len(arrays)),
            [pltpu.VMEM(a.shape, a.dtype) for a in arrays] + [shape((8, LANES), jnp.int32)],
            "stash",
            [pltpu.SemaphoreType.DMA((len(arrays),))],
            moved=sum(2 * a.size for a in arrays),
        )(
            token,
            *(pltpu.with_memory_space_constraint(a, pltpu.HBM) for a in arrays),
            *behind,
            specs=[vmem] + [pltpu.HBM] * len(arrays) + [pl.ANY] * len(behind),
        )
        return outs[:-1], outs[-1]

    hidden = hidden_state_input
    carried, length = call(
        first_kernel, [shape((1, width + LANES)), shape((8, LANES), jnp.int32)], "first"
    )(
        hidden,
        row_adapter_index,
        cache_length_per_row,
        me,
        specs=[vmem, smem, smem, smem],
    )
    past = ()
    for step in range(STEPS):
        first, last = step == 0, step == STEPS - 1
        outs = [shape((count, width)), shape((count, rank))]
        scratch = [pltpu.VMEM((count, width), jnp.float32)]
        if first:
            (query_w, down_w), token = stash(length, [query_weight, down])
            pieces = across(carried, far_steps, count)
            column, carried = call(
                functools.partial(join_kernel, far),
                [shape((far, width)), shape((far, width + LANES))],
                "join",
            )(*pieces, scale, token)
            (output_w,), token = stash(token, [output_weight])
            pieces = across(carried, near_steps, count)
            outs = outs + [shape((count, kept), jnp.int32), shape((count, 1), jnp.int32)]
            rows, low, member, adapter = call(
                functools.partial(low_first_kernel, near, far),
                outs,
                "low",
                scratch + [pltpu.VMEM((count, LANES), jnp.float32)],
            )(
                *pieces,
                me,
                storage,
                down_w,
                token,
                specs=[vmem] * near + [smem] + [vmem] * 3,
            )
        else:
            pieces = across(carried, near_steps, count)
            rows, low = call(functools.partial(low_kernel, near, far), outs, "low", scratch)(
                *pieces, me, member, down_w, specs=[vmem] * near + [smem, vmem, vmem]
            )
        behind = []
        if first:
            rest = [key_value_weight, adapter_up_weight, key_value_cache]
            (fresh_w, up_w, cache), token = stash(token, rest, low)
            behind = [token]
        (low,) = call(functools.partial(sum_kernel, near), [shape((count, rank))], "sum")(
            *across(low, near_steps, count), *behind
        )
        lows = across(low, far_steps, count)
        query, fresh = call(
            project_kernel,
            [shape((count, columns), jnp.float32), shape((count, fresh_columns), jnp.float32)],
            "project",
            flops=2 * count * width * (columns + fresh_columns),
            moved=2 * width * (columns + fresh_columns),
        )(rows, query_w, fresh_w)
        (lines,) = call(
            functools.partial(up_kernel, far),
            [shape((count, 8, line))],
            "up",
            [pltpu.VMEM((count, 8, line), jnp.float32)],
        )(*lows, query, fresh, adapter, up_w)

        lines = swap(lines)
        outs = [shape((count, columns // line, line))]
        if first:
            outs = outs + [shape((H, HD), jnp.float32)] * 2
        outs = call(
            functools.partial(attend_kernel, columns, fresh_columns, first),
            outs,
            "attend",
            [
                pltpu.VMEM((count, 8, line), jnp.float32),
                pltpu.VMEM((H, key_value_cache.shape[2]), jnp.float32),
            ],
            moved=2 << 20,
        )(
            lines,
            length,
            cache,
            *past,
            specs=[vmem] * (3 + len(past)),
        )
        if first:
            past = tuple(outs[1:])

        lines = swap(outs[0])
        own, away = call(
            functools.partial(output_kernel, None if last else (near, far)),
            [shape((chips, width), jnp.float32), shape((chips, width))],
            "output",
            [pltpu.VMEM((count, 8, line), jnp.float32)],
            flops=2 * count * width * columns,
            moved=2 * width * columns,
        )(lines, me, output_w, specs=[vmem, smem, vmem])

        if last:
            (parts,) = call(partial_kernel, [shape((chips, FOLD, width // FOLD))], "partial")(
                own, shift(away, 1, count)
            )
            parts = chips_swap(parts, count)
            (out,) = call(finish_kernel, [shape((STEPS, width))], "finish")(parts, hidden)
            return out.reshape(STEPS, 1, width)
        bit = 1
        while bit < near // 2:
            half = own.shape[0] // 2
            own, away = call(
                fold_kernel, [shape((half, width), jnp.float32), shape((half, width))], "fold"
            )(own, shift(away, bit, count))
            bit *= 2
        (own,) = call(folded_kernel, [shape((far, width))], "fold")(own, shift(away, bit, count))
        hidden, carried = call(
            functools.partial(next_kernel, far), [shape((1, width)), shape((far, width))], "next"
        )(*across(own, far_steps, count), column, scale)


def solution(mesh):
    in_specs = (
        P(("groups", "replica"), None),
        P(),
        P(None, "replica"),
        P(None, "replica"),
        P("replica", None),
        P("replica", None, None),
        P(None, None, "replica"),
        P(("groups", "replica")),
        P(),
        P(("groups", "replica")),
        P(("groups", "replica"), None, None, None),
    )
    out_specs = P(None, ("groups", "replica"), None)
    return jax.shard_map(shards, mesh=mesh, in_specs=in_specs, out_specs=out_specs, check_vma=False)
```

```python
import functools
import math

import jax
import jax.numpy as jnp
from jax import lax
from jax.experimental import pallas as pl
from jax.experimental.pallas import tpu as pltpu
from jax.sharding import PartitionSpec as P

H = 64
KVH = 8
HD = 128
STEPS = 2
GROUP = H // KVH
EPS = 1e-05
AXIS = "replica"
LANES = 128
LAST = (((1,), (1,)), ((), ()))
FIRST = (((0,), (0,)), ((), ()))

CORES = 2
FOLD = 8


def split_of(count):
    far = 1 << (count.bit_length() // 2)
    return far, count // far


def shift(block, distance, count):
    return lax.ppermute(block, AXIS, [(i, i ^ distance) for i in range(count)])


def across(block, strides, count):
    return [block] + [shift(block, d, count) for d in strides]


def swap(blocks):
    return lax.all_to_all(blocks, AXIS, split_axis=0, concat_axis=0, tiled=True)


def chips_swap(blocks, count):
    groups = [[i for i in range(count) if i % CORES == c] for c in range(CORES)]
    return lax.all_to_all(
        blocks, AXIS, split_axis=0, concat_axis=0, axis_index_groups=groups, tiled=True
    )


def call(body, outs, name, scratch=(), vmem=20 << 20, flops=1 << 20, moved=1 << 18):
    def run(*operands, specs=None):
        specs = specs or [pltpu.VMEM] * len(operands)
        return pl.pallas_call(
            body,
            out_shape=outs,
            in_specs=[pl.BlockSpec(memory_space=s) for s in specs],
            out_specs=[pl.BlockSpec(memory_space=pltpu.VMEM)] * len(outs),
            scratch_shapes=list(scratch),
            compiler_params=pltpu.CompilerParams(vmem_limit_bytes=vmem),
            cost_estimate=pl.CostEstimate(flops=flops, bytes_accessed=moved, transcendentals=0),
            name=name,
        )(*operands)

    return run


def shape(dims, dtype=jnp.bfloat16):
    return jax.ShapeDtypeStruct(dims, dtype)


def iota(dims, axis):
    return lax.broadcasted_iota(jnp.int32, dims, axis)


def dot(a, b, contract=(((1,), (0,)), ((), ()))):
    return lax.dot_general(a, b, contract, preferred_element_type=jnp.float32)


def normalized(hidden, scale):
    factor = lax.rsqrt(jnp.mean(hidden * hidden, axis=-1, keepdims=True) + EPS)
    return (hidden * factor * scale).astype(jnp.bfloat16)


def row_of(ref):
    lines = ref[...].astype(jnp.float32)
    return jnp.concatenate([lines[i : i + 1] for i in range(lines.shape[0])], axis=1)


def first_kernel(hidden_ref, adapter_ref, length_ref, _, out_ref, length_out):
    length_out[...] = jnp.full(length_out.shape, length_ref[0], jnp.int32)
    width = hidden_ref.shape[1]
    out_ref[:, :width] = hidden_ref[...]
    digit = iota((1, LANES), 1)
    adapter = adapter_ref[0]
    high, low = adapter // 256, adapter % 256
    digits = jnp.where(digit == 0, low, jnp.where(digit == 1, high, 0)).astype(jnp.float32)
    out_ref[:, width:] = digits.astype(jnp.bfloat16)


def stash_kernel(amount, token_ref, *refs):
    sources, refs = refs[:amount], refs[amount:]
    outs, out_token, sems = refs[-2 - amount : -2], refs[-2], refs[-1]
    copies = [
        pltpu.make_async_copy(sources[i], outs[i], sems.at[i]) for i in range(amount)
    ]
    for copy in copies:
        copy.start()
    out_token[...] = token_ref[...]
    for copy in copies:
        copy.wait()


def low_terms(held, member_ref, down_ref, rows_ref, low_ref):
    rows = held[...].astype(jnp.bfloat16)
    rows_ref[...] = rows
    low = jnp.zeros(low_ref.shape, jnp.float32)
    for index in range(down_ref.shape[0]):
        part = dot(rows, down_ref[index], LAST)
        low = jnp.where(member_ref[:, index : index + 1] > 0, part, low)
    low_ref[...] = low.astype(jnp.bfloat16)


def gathered(near, far, pieces, me, held):
    width = held.shape[1]
    for l in range(near):
        block = pieces[l][:, :width].astype(jnp.float32)
        for k in range(far):
            held[pl.ds(me ^ (k * near + l), 1), :] = block[k : k + 1]


def low_kernel(near, far, *refs):
    pieces, refs = refs[:near], refs[near:]
    me_ref, member_ref, down_ref, rows_ref, low_ref, held = refs
    gathered(near, far, pieces, me_ref[0], held)
    low_terms(held, member_ref, down_ref, rows_ref, low_ref)


def low_first_kernel(near, far, *refs):
    pieces, refs = refs[:near], refs[near:]
    me_ref, storage_ref, down_ref, _, rows_ref, low_ref, member_ref, adapter_ref = refs[:8]
    held, digits = refs[-2:]
    width = held.shape[1]
    me = me_ref[0]
    kept = member_ref.shape[1]
    count = near * far
    for l in range(near):
        block = pieces[l][:, width:].astype(jnp.float32)
        for k in range(far):
            digits[pl.ds(me ^ (k * near + l), 1), :] = block[k : k + 1]
    adapter = (digits[:, 0:1] + 256.0 * digits[:, 1:2]).astype(jnp.int32)
    adapter_ref[...] = adapter
    table = storage_ref.shape[1]
    chosen = jnp.where(iota((count, table), 1) == adapter, storage_ref[...], 0)
    storage = jnp.sum(chosen.astype(jnp.float32), axis=1, keepdims=True).astype(jnp.int32)
    member_ref[...] = (storage - me * kept == iota((count, kept), 1)).astype(jnp.int32)
    gathered(near, far, pieces, me, held)
    low_terms(held, member_ref, down_ref, rows_ref, low_ref)


def join_kernel(amount, *refs):
    scale_ref, _, hidden_ref, out_ref = refs[amount:]
    width = hidden_ref.shape[1]
    rows = [ref[...].astype(jnp.float32) for ref in refs[:amount]]
    rows = jnp.concatenate(rows, axis=0)
    hidden = rows[:, :width]
    hidden_ref[...] = hidden.astype(jnp.bfloat16)
    out_ref[:, :width] = normalized(hidden, row_of(scale_ref))
    out_ref[:, width:] = rows[:, width:].astype(jnp.bfloat16)


def distance(slot, near, far):
    size, total = near * far, (slot % far) * near
    bit = 1
    while bit < near:
        size //= 2
        total = total + ((slot // size) % 2) * bit
        bit *= 2
    return total


def fold_kernel(own_ref, other_ref, keep_ref, away_ref):
    total = own_ref[...] + other_ref[...].astype(jnp.float32)
    half = keep_ref.shape[0]
    keep_ref[...] = total[:half]
    away_ref[...] = total[half:].astype(jnp.bfloat16)


def folded_kernel(own_ref, other_ref, out_ref):
    out_ref[...] = (own_ref[...] + other_ref[...].astype(jnp.float32)).astype(jnp.bfloat16)


def next_kernel(far, *refs):
    pieces, (hidden_ref, scale_ref, own_ref, out_ref) = refs[:far], refs[far:]
    sums = []
    for k in range(far):
        piece = pieces[k][...].astype(jnp.float32)
        sums.append(jnp.concatenate([piece[j ^ k : (j ^ k) + 1] for j in range(far)], axis=0))
    while len(sums) > 1:
        sums = [sums[i] + sums[i + 1] for i in range(0, len(sums), 2)]
    total = sums[0].astype(jnp.bfloat16).astype(jnp.float32)
    hidden = (hidden_ref[...].astype(jnp.float32) + total).astype(jnp.bfloat16)
    own_ref[...] = hidden.astype(jnp.float32)[:1].astype(jnp.bfloat16)
    out_ref[...] = normalized(hidden.astype(jnp.float32), row_of(scale_ref))


def sum_kernel(amount, *refs):
    total = refs[0][...].astype(jnp.float32)
    for ref in refs[1:amount]:
        total = total + ref[...].astype(jnp.float32)
    refs[-1][...] = total.astype(refs[-1].dtype)


def project_kernel(rows_ref, query_w, fresh_w, query_ref, fresh_ref):
    query_ref[...] = dot(rows_ref[...], query_w[...])
    fresh_ref[...] = dot(rows_ref[...], fresh_w[...])


def up_kernel(parts, *refs):
    lows, (query_ref, fresh_ref, adapter_ref, up_ref, out_ref, held) = refs[:parts], refs[parts:]
    count, columns = query_ref.shape
    rank = lows[0].shape[1]
    low = lows[0][...].astype(jnp.float32)
    for ref in lows[1:]:
        low = low + ref[...].astype(jnp.float32)
    low = low.astype(jnp.bfloat16)
    query = query_ref[...]
    table = up_ref.shape[0]
    some = min(table, 32)
    wide = some * rank
    low = low.astype(jnp.float32)
    wide_low = jnp.concatenate([low] * max(1, LANES // rank), axis=1)
    wide_low = jnp.concatenate([wide_low] * (wide // wide_low.shape[1]), axis=1)
    place = iota((count, wide), 1) // rank
    for start in range(0, table, some):
        spread = jnp.where(place + start == adapter_ref[...], wide_low, 0.0).astype(jnp.bfloat16)
        query = query + dot(spread, up_ref[start : start + some].reshape(wide, columns))
    line = out_ref.shape[2]
    lines = columns // line
    held[...] = jnp.zeros(held.shape, jnp.float32)
    for c in range(lines):
        held[:, c, :] = query[:, c * line : (c + 1) * line]
    fresh = fresh_ref[...]
    if fresh.shape[1] < line:
        fresh = jnp.concatenate(
            [fresh, jnp.zeros((count, line - fresh.shape[1]), jnp.float32)], axis=1
        )
    held[:, lines, :] = fresh
    for k in range(count):
        out_ref[k] = held[k].astype(jnp.bfloat16)


def pieces_of(lines, select, whole, size):
    if size >= whole:
        total = dot(select(len(lines), 0), lines[0])
        for c in range(1, len(lines)):
            total = total + dot(select(len(lines), c), lines[c])
        return total
    return jnp.concatenate([dot(select(0, p), lines[0]) for p in range(whole // size)], axis=1)


def attend_kernel(columns, fresh_columns, first, *refs):
    lines_ref, length_ref, cache_ref = refs[:3]
    refs = refs[3:]
    if not first:
        past, refs = refs[:2], refs[2:]
    out_ref, refs = refs[0], refs[1:]
    if first:
        keep, refs = refs[:2], refs[2:]
    held, scores = refs
    count, _, line = lines_ref.shape
    cache = cache_ref.shape[2]
    for k in range(count):
        held[k] = lines_ref[k].astype(jnp.float32)
    each = columns // line
    lines = [held[:, c, :].astype(jnp.bfloat16) for c in range(each + 1)]
    origin = iota((H, count), 1)
    head = iota((H, count), 0)

    def query_pick(each, c):
        if each:
            return (head == origin * each + c).astype(jnp.bfloat16)
        return (head * (HD // columns) + c == origin).astype(jnp.bfloat16)

    def fresh_pick(offset):
        def pick(each, c):
            want = head // GROUP + offset
            if each:
                return (want == origin * each + c).astype(jnp.bfloat16)
            return (want * (HD // fresh_columns) + c == origin).astype(jnp.bfloat16)

        return pick

    query = pieces_of(lines[:each], query_pick, HD, columns)
    fresh = [lines[each][:, :fresh_columns]]
    new = [
        (
            pieces_of(fresh, fresh_pick(0), HD, fresh_columns),
            pieces_of(fresh, fresh_pick(KVH), HD, fresh_columns),
        )
    ]
    if first:
        keep[0][...], keep[1][...] = new[0]
    else:
        new.insert(0, (past[0][...], past[1][...]))
    scale = 1.0 / math.sqrt(HD)
    for j in range(KVH):
        rows = slice(j * GROUP, (j + 1) * GROUP)
        scores[rows, :] = dot(
            query[rows].astype(jnp.bfloat16), cache_ref[0, 0, :, j * HD : (j + 1) * HD], LAST
        )
    in_cache = iota((H, cache), 1) < length_ref[0:1, 0:1]
    old = jnp.where(in_cache, scores[...] * scale, -jnp.inf)
    news = [jnp.sum(query * keys, axis=1, keepdims=True) * scale for keys, _ in new]
    peak = jnp.max(old, axis=1, keepdims=True)
    for score in news:
        peak = jnp.maximum(peak, score)
    old = jnp.exp(old - peak)
    news = [jnp.exp(score - peak) for score in news]
    total = jnp.sum(old, axis=1, keepdims=True)
    for score in news:
        total = total + score
    old = old / total
    extra = jnp.zeros((H, HD), jnp.float32)
    for score, (_, values) in zip(news, new):
        extra = extra + (score / total).astype(jnp.bfloat16).astype(jnp.float32) * values
    mixed = jnp.concatenate(
        [
            dot(
                old[j * GROUP : (j + 1) * GROUP].astype(jnp.bfloat16),
                cache_ref[0, 1, :, j * HD : (j + 1) * HD],
            )
            for j in range(KVH)
        ],
        axis=0,
    )
    mixed = mixed + extra
    if columns >= HD:
        for k in range(count):
            out_ref[k] = mixed[k * each : (k + 1) * each].astype(jnp.bfloat16)
    else:
        parts = HD // columns
        out = jnp.zeros((count, columns), jnp.float32)
        for p in range(parts):
            pick = (iota((count, H), 1) * parts + p == iota((count, H), 0)).astype(jnp.bfloat16)
            out = out + dot(pick, mixed[:, p * columns : (p + 1) * columns].astype(jnp.bfloat16))
        for k in range(count):
            out_ref[k] = out[k : k + 1].astype(jnp.bfloat16)


def output_kernel(split, lines_ref, me_ref, weight_ref, own_ref, away_ref, held):
    count, each, line = lines_ref.shape
    chips = count // CORES
    for k in range(count):
        held[k, :each, :] = lines_ref[k].astype(jnp.float32)
    slot = iota((count, count), 0)
    if split:
        origin = me_ref[0] ^ distance(slot, *split)
    else:
        origin = (slot % chips) * CORES + ((me_ref[0] % CORES) ^ (slot // chips))
    order = (iota((count, count), 1) == origin).astype(jnp.bfloat16)
    rows = jnp.concatenate(
        [dot(order, held[:, c, :].astype(jnp.bfloat16)).astype(jnp.bfloat16) for c in range(each)],
        axis=1,
    )
    width = weight_ref.shape[1]
    wide = width // 8
    for c in range(8):
        part = slice(c * wide, (c + 1) * wide)
        out = dot(rows, weight_ref[:, part])
        own_ref[:, part] = out[:chips]
        away_ref[:, part] = out[chips:].astype(jnp.bfloat16)


def partial_kernel(own_ref, other_ref, out_ref):
    total = own_ref[...] + other_ref[...].astype(jnp.float32)
    wide = out_ref.shape[2]
    for k in range(out_ref.shape[0]):
        for i in range(FOLD):
            out_ref[k, i : i + 1, :] = total[k : k + 1, i * wide : (i + 1) * wide].astype(
                out_ref.dtype
            )


def finish_kernel(parts_ref, hidden_ref, out_ref):
    total = parts_ref[0].astype(jnp.float32)
    for k in range(1, parts_ref.shape[0]):
        total = total + parts_ref[k].astype(jnp.float32)
    total = jnp.concatenate([total[i : i + 1] for i in range(FOLD)], axis=1)
    total = total.astype(jnp.bfloat16).astype(jnp.float32)
    before = hidden_ref[...].astype(jnp.float32)
    out_ref[...] = jnp.concatenate([before, before + total], axis=0).astype(jnp.bfloat16)


def shards(
    hidden_state_input,
    attention_norm_scale,
    query_weight,
    key_value_weight,
    output_weight,
    adapter_down_weight,
    adapter_up_weight,
    row_adapter_index,
    adapter_storage_index,
    cache_length_per_row,
    key_value_cache,
):
    count = lax.axis_size(AXIS)
    chips = count // CORES
    far, near = split_of(count)
    far_steps = [k * near for k in range(1, far)]
    near_steps = list(range(1, near))
    kept, width, rank = adapter_down_weight.shape
    columns = query_weight.shape[1]
    fresh_columns = key_value_weight.shape[1]
    line = min(HD, columns)
    smem, vmem = pltpu.SMEM, pltpu.VMEM
    me = lax.axis_index(AXIS).astype(jnp.int32).reshape(1)
    down = adapter_down_weight.transpose(0, 2, 1)
    scale = attention_norm_scale.reshape(-1, LANES)
    storage = adapter_storage_index[None]

    def stash(token, arrays, *behind):
        outs = call(
            functools.partial(stash_kernel, len(arrays)),
            [pltpu.VMEM(a.shape, a.dtype) for a in arrays] + [shape((8, LANES), jnp.int32)],
            "stash",
            [pltpu.SemaphoreType.DMA((len(arrays),))],
            moved=sum(2 * a.size for a in arrays),
        )(
            token,
            *(pltpu.with_memory_space_constraint(a, pltpu.HBM) for a in arrays),
            *behind,
            specs=[vmem] + [pltpu.HBM] * len(arrays) + [pl.ANY] * len(behind),
        )
        return outs[:-1], outs[-1]

    hidden = hidden_state_input
    carried, length = call(
        first_kernel, [shape((1, width + LANES)), shape((8, LANES), jnp.int32)], "first"
    )(
        hidden,
        row_adapter_index,
        cache_length_per_row,
        me,
        specs=[vmem, smem, smem, smem],
    )
    past = ()
    for step in range(STEPS):
        first, last = step == 0, step == STEPS - 1
        outs = [shape((count, width)), shape((count, rank))]
        scratch = [pltpu.VMEM((count, width), jnp.float32)]
        if first:
            (query_w, down_w), token = stash(length, [query_weight, down])
            pieces = across(carried, far_steps, count)
            column, carried = call(
                functools.partial(join_kernel, far),
                [shape((far, width)), shape((far, width + LANES))],
                "join",
            )(*pieces, scale, token)
            (output_w,), token = stash(token, [output_weight])
            pieces = across(carried, near_steps, count)
            outs = outs + [shape((count, kept), jnp.int32), shape((count, 1), jnp.int32)]
            rows, low, member, adapter = call(
                functools.partial(low_first_kernel, near, far),
                outs,
                "low",
                scratch + [pltpu.VMEM((count, LANES), jnp.float32)],
            )(
                *pieces,
                me,
                storage,
                down_w,
                token,
                specs=[vmem] * near + [smem] + [vmem] * 3,
            )
        else:
            pieces = across(carried, near_steps, count)
            rows, low = call(functools.partial(low_kernel, near, far), outs, "low", scratch)(
                *pieces, me, member, down_w, specs=[vmem] * near + [smem, vmem, vmem]
            )
        behind = []
        if first:
            rest = [key_value_weight, adapter_up_weight, key_value_cache]
            (fresh_w, up_w, cache), token = stash(token, rest, low)
            behind = [token]
        (low,) = call(functools.partial(sum_kernel, far), [shape((count, rank))], "sum")(
            *across(low, far_steps, count), *behind
        )
        lows = across(low, near_steps, count)
        query, fresh = call(
            project_kernel,
            [shape((count, columns), jnp.float32), shape((count, fresh_columns), jnp.float32)],
            "project",
            flops=2 * count * width * (columns + fresh_columns),
            moved=2 * width * (columns + fresh_columns),
        )(rows, query_w, fresh_w)
        (lines,) = call(
            functools.partial(up_kernel, near),
            [shape((count, 8, line))],
            "up",
            [pltpu.VMEM((count, 8, line), jnp.float32)],
        )(*lows, query, fresh, adapter, up_w)

        lines = swap(lines)
        outs = [shape((count, columns // line, line))]
        if first:
            outs = outs + [shape((H, HD), jnp.float32)] * 2
        outs = call(
            functools.partial(attend_kernel, columns, fresh_columns, first),
            outs,
            "attend",
            [
                pltpu.VMEM((count, 8, line), jnp.float32),
                pltpu.VMEM((H, key_value_cache.shape[2]), jnp.float32),
            ],
            moved=2 << 20,
        )(
            lines,
            length,
            cache,
            *past,
            specs=[vmem] * (3 + len(past)),
        )
        if first:
            past = tuple(outs[1:])

        lines = swap(outs[0])
        own, away = call(
            functools.partial(output_kernel, None if last else (near, far)),
            [shape((chips, width), jnp.float32), shape((chips, width))],
            "output",
            [pltpu.VMEM((count, 8, line), jnp.float32)],
            flops=2 * count * width * columns,
            moved=2 * width * columns,
        )(lines, me, output_w, specs=[vmem, smem, vmem])

        if last:
            (parts,) = call(partial_kernel, [shape((chips, FOLD, width // FOLD))], "partial")(
                own, shift(away, 1, count)
            )
            parts = chips_swap(parts, count)
            (out,) = call(finish_kernel, [shape((STEPS, width))], "finish")(parts, hidden)
            return out.reshape(STEPS, 1, width)
        bit = 1
        while bit < near // 2:
            half = own.shape[0] // 2
            own, away = call(
                fold_kernel, [shape((half, width), jnp.float32), shape((half, width))], "fold"
            )(own, shift(away, bit, count))
            bit *= 2
        (own,) = call(folded_kernel, [shape((far, width))], "fold")(own, shift(away, bit, count))
        hidden, carried = call(
            functools.partial(next_kernel, far), [shape((1, width)), shape((far, width))], "next"
        )(*across(own, far_steps, count), column, scale)


def solution(mesh):
    in_specs = (
        P(("groups", "replica"), None),
        P(),
        P(None, "replica"),
        P(None, "replica"),
        P("replica", None),
        P("replica", None, None),
        P(None, None, "replica"),
        P(("groups", "replica")),
        P(),
        P(("groups", "replica")),
        P(("groups", "replica"), None, None, None),
    )
    out_specs = P(None, ("groups", "replica"), None)
    return jax.shard_map(shards, mesh=mesh, in_specs=in_specs, out_specs=out_specs, check_vma=False)
```

```python
import functools
import math

import jax
import jax.numpy as jnp
from jax import lax
from jax.experimental import pallas as pl
from jax.experimental.pallas import tpu as pltpu
from jax.sharding import PartitionSpec as P

H = 64
KVH = 8
HD = 128
STEPS = 2
GROUP = H // KVH
EPS = 1e-05
AXIS = "replica"
LANES = 128
LAST = (((1,), (1,)), ((), ()))
FIRST = (((0,), (0,)), ((), ()))

CORES = 2
FOLD = 8


def split_of(count):
    far = 1 << (count.bit_length() // 2)
    return far, count // far


def shift(block, distance, count):
    return lax.ppermute(block, AXIS, [(i, i ^ distance) for i in range(count)])


def across(block, strides, count):
    return [block] + [shift(block, d, count) for d in strides]


def swap(blocks):
    return lax.all_to_all(blocks, AXIS, split_axis=0, concat_axis=0, tiled=True)


def chips_swap(blocks, count):
    groups = [[i for i in range(count) if i % CORES == c] for c in range(CORES)]
    return lax.all_to_all(
        blocks, AXIS, split_axis=0, concat_axis=0, axis_index_groups=groups, tiled=True
    )


def call(body, outs, name, scratch=(), vmem=20 << 20, flops=1 << 20, moved=1 << 18):
    def run(*operands, specs=None):
        specs = specs or [pltpu.VMEM] * len(operands)
        return pl.pallas_call(
            body,
            out_shape=outs,
            in_specs=[pl.BlockSpec(memory_space=s) for s in specs],
            out_specs=[pl.BlockSpec(memory_space=pltpu.VMEM)] * len(outs),
            scratch_shapes=list(scratch),
            compiler_params=pltpu.CompilerParams(vmem_limit_bytes=vmem),
            cost_estimate=pl.CostEstimate(flops=flops, bytes_accessed=moved, transcendentals=0),
            name=name,
        )(*operands)

    return run


def shape(dims, dtype=jnp.bfloat16):
    return jax.ShapeDtypeStruct(dims, dtype)


def iota(dims, axis):
    return lax.broadcasted_iota(jnp.int32, dims, axis)


def dot(a, b, contract=(((1,), (0,)), ((), ()))):
    return lax.dot_general(a, b, contract, preferred_element_type=jnp.float32)


def normalized(hidden, scale):
    factor = lax.rsqrt(jnp.mean(hidden * hidden, axis=-1, keepdims=True) + EPS)
    return (hidden * factor * scale).astype(jnp.bfloat16)


def row_of(ref):
    lines = ref[...].astype(jnp.float32)
    return jnp.concatenate([lines[i : i + 1] for i in range(lines.shape[0])], axis=1)


def first_kernel(hidden_ref, adapter_ref, length_ref, _, out_ref, length_out):
    length_out[...] = jnp.full(length_out.shape, length_ref[0], jnp.int32)
    width = hidden_ref.shape[1]
    out_ref[:, :width] = hidden_ref[...]
    digit = iota((1, LANES), 1)
    adapter = adapter_ref[0]
    high, low = adapter // 256, adapter % 256
    digits = jnp.where(digit == 0, low, jnp.where(digit == 1, high, 0)).astype(jnp.float32)
    out_ref[:, width:] = digits.astype(jnp.bfloat16)


def stash_kernel(amount, token_ref, *refs):
    sources, refs = refs[:amount], refs[amount:]
    outs, out_token, sems = refs[-2 - amount : -2], refs[-2], refs[-1]
    copies = [
        pltpu.make_async_copy(sources[i], outs[i], sems.at[i]) for i in range(amount)
    ]
    for copy in copies:
        copy.start()
    out_token[...] = token_ref[...]
    for copy in copies:
        copy.wait()


def low_terms(held, member_ref, down_ref, rows_ref, low_ref):
    rows = held[...].astype(jnp.bfloat16)
    rows_ref[...] = rows
    low = jnp.zeros(low_ref.shape, jnp.float32)
    for index in range(down_ref.shape[0]):
        part = dot(rows, down_ref[index], LAST)
        low = jnp.where(member_ref[:, index : index + 1] > 0, part, low)
    low_ref[...] = low.astype(jnp.bfloat16)


def gathered(near, far, pieces, me, held):
    width = held.shape[1]
    for l in range(near):
        block = pieces[l][:, :width].astype(jnp.float32)
        for k in range(far):
            held[pl.ds(me ^ (k * near + l), 1), :] = block[k : k + 1]


def low_kernel(near, far, *refs):
    pieces, refs = refs[:near], refs[near:]
    me_ref, member_ref, down_ref, rows_ref, low_ref, held = refs
    gathered(near, far, pieces, me_ref[0], held)
    low_terms(held, member_ref, down_ref, rows_ref, low_ref)


def low_first_kernel(near, far, *refs):
    pieces, refs = refs[:near], refs[near:]
    me_ref, storage_ref, down_ref, _, rows_ref, low_ref, member_ref, adapter_ref = refs[:8]
    held, digits = refs[-2:]
    width = held.shape[1]
    me = me_ref[0]
    kept = member_ref.shape[1]
    count = near * far
    for l in range(near):
        block = pieces[l][:, width:].astype(jnp.float32)
        for k in range(far):
            digits[pl.ds(me ^ (k * near + l), 1), :] = block[k : k + 1]
    adapter = (digits[:, 0:1] + 256.0 * digits[:, 1:2]).astype(jnp.int32)
    adapter_ref[...] = adapter
    table = storage_ref.shape[1]
    chosen = jnp.where(iota((count, table), 1) == adapter, storage_ref[...], 0)
    storage = jnp.sum(chosen.astype(jnp.float32), axis=1, keepdims=True).astype(jnp.int32)
    member_ref[...] = (storage - me * kept == iota((count, kept), 1)).astype(jnp.int32)
    gathered(near, far, pieces, me, held)
    low_terms(held, member_ref, down_ref, rows_ref, low_ref)


def join_kernel(amount, *refs):
    scale_ref, _, hidden_ref, out_ref, row_ref = refs[amount:]
    row_ref[...] = row_of(scale_ref)
    width = hidden_ref.shape[1]
    rows = [ref[...].astype(jnp.float32) for ref in refs[:amount]]
    rows = jnp.concatenate(rows, axis=0)
    hidden = rows[:, :width]
    hidden_ref[...] = hidden.astype(jnp.bfloat16)
    out_ref[:, :width] = normalized(hidden, row_of(scale_ref))
    out_ref[:, width:] = rows[:, width:].astype(jnp.bfloat16)


def distance(slot, near, far):
    size, total = near * far, (slot % far) * near
    bit = 1
    while bit < near:
        size //= 2
        total = total + ((slot // size) % 2) * bit
        bit *= 2
    return total


def fold_kernel(own_ref, other_ref, keep_ref, away_ref):
    total = own_ref[...] + other_ref[...].astype(jnp.float32)
    half = keep_ref.shape[0]
    keep_ref[...] = total[:half]
    away_ref[...] = total[half:].astype(jnp.bfloat16)


def folded_kernel(own_ref, other_ref, out_ref):
    out_ref[...] = (own_ref[...] + other_ref[...].astype(jnp.float32)).astype(jnp.bfloat16)


def next_kernel(far, *refs):
    pieces, (hidden_ref, scale_ref, own_ref, out_ref) = refs[:far], refs[far:]
    sums = []
    for k in range(far):
        piece = pieces[k][...].astype(jnp.float32)
        sums.append(jnp.concatenate([piece[j ^ k : (j ^ k) + 1] for j in range(far)], axis=0))
    while len(sums) > 1:
        sums = [sums[i] + sums[i + 1] for i in range(0, len(sums), 2)]
    total = sums[0].astype(jnp.bfloat16).astype(jnp.float32)
    hidden = (hidden_ref[...].astype(jnp.float32) + total).astype(jnp.bfloat16)
    own_ref[...] = hidden.astype(jnp.float32)[:1].astype(jnp.bfloat16)
    out_ref[...] = normalized(hidden.astype(jnp.float32), scale_ref[...])


def sum_kernel(amount, *refs):
    total = refs[0][...].astype(jnp.float32)
    for ref in refs[1:amount]:
        total = total + ref[...].astype(jnp.float32)
    refs[-1][...] = total.astype(refs[-1].dtype)


def project_kernel(rows_ref, query_w, fresh_w, query_ref, fresh_ref):
    query_ref[...] = dot(rows_ref[...], query_w[...])
    fresh_ref[...] = dot(rows_ref[...], fresh_w[...])


def up_kernel(parts, *refs):
    lows, (query_ref, fresh_ref, adapter_ref, up_ref, out_ref, held) = refs[:parts], refs[parts:]
    count, columns = query_ref.shape
    rank = lows[0].shape[1]
    low = lows[0][...].astype(jnp.float32)
    for ref in lows[1:]:
        low = low + ref[...].astype(jnp.float32)
    low = low.astype(jnp.bfloat16)
    query = query_ref[...]
    table = up_ref.shape[0]
    some = min(table, 32)
    wide = some * rank
    low = low.astype(jnp.float32)
    wide_low = jnp.concatenate([low] * max(1, LANES // rank), axis=1)
    wide_low = jnp.concatenate([wide_low] * (wide // wide_low.shape[1]), axis=1)
    place = iota((count, wide), 1) // rank
    for start in range(0, table, some):
        spread = jnp.where(place + start == adapter_ref[...], wide_low, 0.0).astype(jnp.bfloat16)
        query = query + dot(spread, up_ref[start : start + some].reshape(wide, columns))
    line = out_ref.shape[2]
    lines = columns // line
    held[...] = jnp.zeros(held.shape, jnp.float32)
    for c in range(lines):
        held[:, c, :] = query[:, c * line : (c + 1) * line]
    fresh = fresh_ref[...]
    if fresh.shape[1] < line:
        fresh = jnp.concatenate(
            [fresh, jnp.zeros((count, line - fresh.shape[1]), jnp.float32)], axis=1
        )
    held[:, lines, :] = fresh
    for k in range(count):
        out_ref[k] = held[k].astype(jnp.bfloat16)


def pieces_of(lines, select, whole, size):
    if size >= whole:
        total = dot(select(len(lines), 0), lines[0])
        for c in range(1, len(lines)):
            total = total + dot(select(len(lines), c), lines[c])
        return total
    return jnp.concatenate([dot(select(0, p), lines[0]) for p in range(whole // size)], axis=1)


def attend_kernel(columns, fresh_columns, first, *refs):
    lines_ref, length_ref, cache_ref = refs[:3]
    refs = refs[3:]
    if not first:
        past, refs = refs[:2], refs[2:]
    out_ref, refs = refs[0], refs[1:]
    if first:
        keep, refs = refs[:2], refs[2:]
    held, scores = refs
    count, _, line = lines_ref.shape
    cache = cache_ref.shape[2]
    for k in range(count):
        held[k] = lines_ref[k].astype(jnp.float32)
    each = columns // line
    lines = [held[:, c, :].astype(jnp.bfloat16) for c in range(each + 1)]
    origin = iota((H, count), 1)
    head = iota((H, count), 0)

    def query_pick(each, c):
        if each:
            return (head == origin * each + c).astype(jnp.bfloat16)
        return (head * (HD // columns) + c == origin).astype(jnp.bfloat16)

    def fresh_pick(offset):
        def pick(each, c):
            want = head // GROUP + offset
            if each:
                return (want == origin * each + c).astype(jnp.bfloat16)
            return (want * (HD // fresh_columns) + c == origin).astype(jnp.bfloat16)

        return pick

    query = pieces_of(lines[:each], query_pick, HD, columns)
    fresh = [lines[each][:, :fresh_columns]]
    new = [
        (
            pieces_of(fresh, fresh_pick(0), HD, fresh_columns),
            pieces_of(fresh, fresh_pick(KVH), HD, fresh_columns),
        )
    ]
    if first:
        keep[0][...], keep[1][...] = new[0]
    else:
        new.insert(0, (past[0][...], past[1][...]))
    scale = 1.0 / math.sqrt(HD)
    for j in range(KVH):
        rows = slice(j * GROUP, (j + 1) * GROUP)
        scores[rows, :] = dot(
            query[rows].astype(jnp.bfloat16), cache_ref[0, 0, :, j * HD : (j + 1) * HD], LAST
        )
    in_cache = iota((H, cache), 1) < length_ref[0:1, 0:1]
    old = jnp.where(in_cache, scores[...] * scale, -jnp.inf)
    news = [jnp.sum(query * keys, axis=1, keepdims=True) * scale for keys, _ in new]
    peak = jnp.max(old, axis=1, keepdims=True)
    for score in news:
        peak = jnp.maximum(peak, score)
    old = jnp.exp(old - peak)
    news = [jnp.exp(score - peak) for score in news]
    total = jnp.sum(old, axis=1, keepdims=True)
    for score in news:
        total = total + score
    old = old / total
    extra = jnp.zeros((H, HD), jnp.float32)
    for score, (_, values) in zip(news, new):
        extra = extra + (score / total).astype(jnp.bfloat16).astype(jnp.float32) * values
    mixed = jnp.concatenate(
        [
            dot(
                old[j * GROUP : (j + 1) * GROUP].astype(jnp.bfloat16),
                cache_ref[0, 1, :, j * HD : (j + 1) * HD],
            )
            for j in range(KVH)
        ],
        axis=0,
    )
    mixed = mixed + extra
    if columns >= HD:
        for k in range(count):
            out_ref[k] = mixed[k * each : (k + 1) * each].astype(jnp.bfloat16)
    else:
        parts = HD // columns
        out = jnp.zeros((count, columns), jnp.float32)
        for p in range(parts):
            pick = (iota((count, H), 1) * parts + p == iota((count, H), 0)).astype(jnp.bfloat16)
            out = out + dot(pick, mixed[:, p * columns : (p + 1) * columns].astype(jnp.bfloat16))
        for k in range(count):
            out_ref[k] = out[k : k + 1].astype(jnp.bfloat16)


def output_kernel(split, lines_ref, me_ref, weight_ref, own_ref, away_ref, held):
    count, each, line = lines_ref.shape
    chips = count // CORES
    for k in range(count):
        held[k, :each, :] = lines_ref[k].astype(jnp.float32)
    slot = iota((count, count), 0)
    if split:
        origin = me_ref[0] ^ distance(slot, *split)
    else:
        origin = (slot % chips) * CORES + ((me_ref[0] % CORES) ^ (slot // chips))
    order = (iota((count, count), 1) == origin).astype(jnp.bfloat16)
    rows = jnp.concatenate(
        [dot(order, held[:, c, :].astype(jnp.bfloat16)).astype(jnp.bfloat16) for c in range(each)],
        axis=1,
    )
    width = weight_ref.shape[1]
    wide = width // 8
    for c in range(8):
        part = slice(c * wide, (c + 1) * wide)
        out = dot(rows, weight_ref[:, part])
        own_ref[:, part] = out[:chips]
        away_ref[:, part] = out[chips:].astype(jnp.bfloat16)


def partial_kernel(own_ref, other_ref, out_ref):
    total = own_ref[...] + other_ref[...].astype(jnp.float32)
    wide = out_ref.shape[2]
    for k in range(out_ref.shape[0]):
        for i in range(FOLD):
            out_ref[k, i : i + 1, :] = total[k : k + 1, i * wide : (i + 1) * wide].astype(
                out_ref.dtype
            )


def finish_kernel(parts_ref, hidden_ref, out_ref):
    total = parts_ref[0].astype(jnp.float32)
    for k in range(1, parts_ref.shape[0]):
        total = total + parts_ref[k].astype(jnp.float32)
    total = jnp.concatenate([total[i : i + 1] for i in range(FOLD)], axis=1)
    total = total.astype(jnp.bfloat16).astype(jnp.float32)
    before = hidden_ref[...].astype(jnp.float32)
    out_ref[...] = jnp.concatenate([before, before + total], axis=0).astype(jnp.bfloat16)


def shards(
    hidden_state_input,
    attention_norm_scale,
    query_weight,
    key_value_weight,
    output_weight,
    adapter_down_weight,
    adapter_up_weight,
    row_adapter_index,
    adapter_storage_index,
    cache_length_per_row,
    key_value_cache,
):
    count = lax.axis_size(AXIS)
    chips = count // CORES
    far, near = split_of(count)
    far_steps = [k * near for k in range(1, far)]
    near_steps = list(range(1, near))
    kept, width, rank = adapter_down_weight.shape
    columns = query_weight.shape[1]
    fresh_columns = key_value_weight.shape[1]
    line = min(HD, columns)
    smem, vmem = pltpu.SMEM, pltpu.VMEM
    me = lax.axis_index(AXIS).astype(jnp.int32).reshape(1)
    down = adapter_down_weight.transpose(0, 2, 1)
    scale = attention_norm_scale.reshape(-1, LANES)
    storage = adapter_storage_index[None]

    def stash(token, arrays, *behind):
        outs = call(
            functools.partial(stash_kernel, len(arrays)),
            [pltpu.VMEM(a.shape, a.dtype) for a in arrays] + [shape((8, LANES), jnp.int32)],
            "stash",
            [pltpu.SemaphoreType.DMA((len(arrays),))],
            moved=sum(2 * a.size for a in arrays),
        )(
            token,
            *(pltpu.with_memory_space_constraint(a, pltpu.HBM) for a in arrays),
            *behind,
            specs=[vmem] + [pltpu.HBM] * len(arrays) + [pl.ANY] * len(behind),
        )
        return outs[:-1], outs[-1]

    hidden = hidden_state_input
    carried, length = call(
        first_kernel, [shape((1, width + LANES)), shape((8, LANES), jnp.int32)], "first"
    )(
        hidden,
        row_adapter_index,
        cache_length_per_row,
        me,
        specs=[vmem, smem, smem, smem],
    )
    past = ()
    for step in range(STEPS):
        first, last = step == 0, step == STEPS - 1
        outs = [shape((count, width)), shape((count, rank))]
        scratch = [pltpu.VMEM((count, width), jnp.float32)]
        if first:
            (query_w, down_w), token = stash(length, [query_weight, down])
            pieces = across(carried, far_steps, count)
            column, carried, scale_row = call(
                functools.partial(join_kernel, far),
                [
                    shape((far, width)),
                    shape((far, width + LANES)),
                    shape((1, width), jnp.float32),
                ],
                "join",
            )(*pieces, scale, token)
            (output_w,), token = stash(token, [output_weight])
            pieces = across(carried, near_steps, count)
            outs = outs + [shape((count, kept), jnp.int32), shape((count, 1), jnp.int32)]
            rows, low, member, adapter = call(
                functools.partial(low_first_kernel, near, far),
                outs,
                "low",
                scratch + [pltpu.VMEM((count, LANES), jnp.float32)],
            )(
                *pieces,
                me,
                storage,
                down_w,
                token,
                specs=[vmem] * near + [smem] + [vmem] * 3,
            )
        else:
            pieces = across(carried, near_steps, count)
            rows, low = call(functools.partial(low_kernel, near, far), outs, "low", scratch)(
                *pieces, me, member, down_w, specs=[vmem] * near + [smem, vmem, vmem]
            )
        behind = []
        if first:
            rest = [key_value_weight, adapter_up_weight, key_value_cache]
            (fresh_w, up_w, cache), token = stash(token, rest, low)
            behind = [token]
        (low,) = call(functools.partial(sum_kernel, far), [shape((count, rank))], "sum")(
            *across(low, far_steps, count), *behind
        )
        lows = across(low, near_steps, count)
        query, fresh = call(
            project_kernel,
            [shape((count, columns), jnp.float32), shape((count, fresh_columns), jnp.float32)],
            "project",
            flops=2 * count * width * (columns + fresh_columns),
            moved=2 * width * (columns + fresh_columns),
        )(rows, query_w, fresh_w)
        (lines,) = call(
            functools.partial(up_kernel, near),
            [shape((count, 8, line))],
            "up",
            [pltpu.VMEM((count, 8, line), jnp.float32)],
        )(*lows, query, fresh, adapter, up_w)

        lines = swap(lines)
        outs = [shape((count, columns // line, line))]
        if first:
            outs = outs + [shape((H, HD), jnp.float32)] * 2
        outs = call(
            functools.partial(attend_kernel, columns, fresh_columns, first),
            outs,
            "attend",
            [
                pltpu.VMEM((count, 8, line), jnp.float32),
                pltpu.VMEM((H, key_value_cache.shape[2]), jnp.float32),
            ],
            moved=2 << 20,
        )(
            lines,
            length,
            cache,
            *past,
            specs=[vmem] * (3 + len(past)),
        )
        if first:
            past = tuple(outs[1:])

        lines = swap(outs[0])
        own, away = call(
            functools.partial(output_kernel, None if last else (near, far)),
            [shape((chips, width), jnp.float32), shape((chips, width))],
            "output",
            [pltpu.VMEM((count, 8, line), jnp.float32)],
            flops=2 * count * width * columns,
            moved=2 * width * columns,
        )(lines, me, output_w, specs=[vmem, smem, vmem])

        if last:
            (parts,) = call(partial_kernel, [shape((chips, FOLD, width // FOLD))], "partial")(
                own, shift(away, 1, count)
            )
            parts = chips_swap(parts, count)
            (out,) = call(finish_kernel, [shape((STEPS, width))], "finish")(parts, hidden)
            return out.reshape(STEPS, 1, width)
        bit = 1
        while bit < near // 2:
            half = own.shape[0] // 2
            own, away = call(
                fold_kernel, [shape((half, width), jnp.float32), shape((half, width))], "fold"
            )(own, shift(away, bit, count))
            bit *= 2
        (own,) = call(folded_kernel, [shape((far, width))], "fold")(own, shift(away, bit, count))
        hidden, carried = call(
            functools.partial(next_kernel, far), [shape((1, width)), shape((far, width))], "next"
        )(*across(own, far_steps, count), column, scale_row)


def solution(mesh):
    in_specs = (
        P(("groups", "replica"), None),
        P(),
        P(None, "replica"),
        P(None, "replica"),
        P("replica", None),
        P("replica", None, None),
        P(None, None, "replica"),
        P(("groups", "replica")),
        P(),
        P(("groups", "replica")),
        P(("groups", "replica"), None, None, None),
    )
    out_specs = P(None, ("groups", "replica"), None)
    return jax.shard_map(shards, mesh=mesh, in_specs=in_specs, out_specs=out_specs, check_vma=False)
```
